32 devices in a mesh: dp: 8 (over z, y), pair: 4 (over x, core).
Axes of the slice: x: 2, y: 2, z: 4, core: 2. Of those that a mesh axis runs over, the one named last changes fastest.
Arguments:
- actions: bfloat16 [4, 1536, 16, 256], P(None, ('dp', 'pair')), may hold values from -6 to 6
- observations: bfloat16 [4, 384, 1024], P(None, 'dp', 'pair'), may hold values from -6 to 6
- tsteps: int32 [4, 1536], P(None, ('dp', 'pair')), may hold values from 0 to 99
- lengths: int32 [4, 1536], P(None, ('dp', 'pair')), may hold values from 4 to 16
- cot_skip: bfloat16 [4, 1536, 16, 512], P(None, ('dp', 'pair')), may hold values from -6 to 6
- cot_down: bfloat16 [4, 1536, 8, 512], P(None, ('dp', 'pair')), may hold values from -6 to 6
- owners: int32 [62], replicated, may hold values from 0 to 7, as said below
- master: float32 [128, 128, 512], P('dp'), may hold values from -0.1875 to 0.1875
- moment_one: float32 [128, 128, 512], P('dp'), may hold values from -224 to 224
- moment_two: float32 [128, 128, 512], P('dp'), may hold values from 98.304 to 393.216
- small_master: float32 [10, 512], replicated, as said below
- small_one: float32 [10, 512], replicated, may hold values from -224 to 224
- small_two: float32 [10, 512], replicated, may hold values from 98.304 to 393.216
Outputs:
- skip_out: bfloat16 [4, 1536, 16, 512], P(None, ('dp', 'pair'))
- down_out: bfloat16 [4, 1536, 8, 512], P(None, ('dp', 'pair'))
- actions_grad: float32 [4, 1536, 16, 256], P(None, ('dp', 'pair'))
- observations_grad: float32 [4, 384, 1024], P(None, 'dp', 'pair')
- new_moment_one: float32 [128, 128, 512], P('dp')
- new_moment_two: float32 [128, 128, 512], P('dp')
- new_master: float32 [128, 128, 512], P('dp')
- new_small_one: float32 [10, 512], replicated
- new_small_two: float32 [10, 512], replicated
- new_small: float32 [10, 512], replicated
The draws below stay inside these ranges and needn't reach their ends.
Inputs may be any that keep to these rules, and one draw needn't show every extreme that they name: `owners`: no index owns more than 16 blocks, and one owns exactly 16. `lengths`: frames at or past a window's length are padding. `small_master`: rows 1 and 6 are gains, the others biases.
All inputs are finite; a program needn't handle non-finite values.
Results may differ from the reference program's by a relative error of at most 0.0086.
Values may be sent and summed in bfloat16 or wider, within the bound.
No kernel may reach another device: no remote copies, remote signals or barrier semaphores. Data moves between devices by JAX's collectives and lax.ppermute only.
A program may use at most 192 MiB of HBM per device.

```python
import math
import jax
import jax.numpy as jnp
from jax import lax

CI = 256
C = 512
OBS = 1024
TE = 128
GROUPS = 8
KW = 5
H = 16
KD = 3
NSMALL = 10
NSTEPS = 100
STEP = 10
MICRO = 4
BLK = 128
SAMP = 48
COND = 1152
SAMPLES = 1536
OBSN = 384
ROWS = 7936
NBLK = 62
MOST = 16
SLOTS = 128
N_DP = 8
N_PAIR = 4


def draw_owners(key, part):
    key = jax.random.fold_in(key, 7)
    key_order, key_shuffle = jax.random.split(key, 2)
    order = jax.random.permutation(key_order, SLOTS).astype(jnp.int32)
    chosen_owner = order[0] // MOST
    others = order[jnp.argsort((order // MOST == chosen_owner).astype(jnp.int32), stable=True)]
    picked = jnp.concatenate([chosen_owner * MOST + jnp.arange(MOST, dtype=jnp.int32), others[:NBLK - MOST]])
    picked = jax.random.permutation(key_shuffle, picked)
    return (picked // MOST).astype(jnp.int32)


def draw_small_master(key, part):
    key = jax.random.fold_in(key, 11)
    base = jax.random.normal(key, (NSMALL, C), jnp.float32) * 0.3
    row_ids = jnp.arange(NSMALL)[:, None]
    gain_rows = (row_ids == 1) | (row_ids == 6)
    return jnp.where(gain_rows, 1.0 + base, base)


def set_ends(values, rng, low, top_value):
    shape = values.shape
    spot = [jax.random.randint(jax.random.fold_in(rng, axis), (), 0, shape[axis]) for axis in range(len(shape))]
    values = values.at[tuple(spot)].set(low)
    longest = shape.index(max(shape))
    spot[longest] = (spot[longest] + 1) % shape[longest]
    return values.at[tuple(spot)].set(top_value)


def block_scale(key, dims, cuts, least, high):
    factor_of = 1.0
    for axis_at, blocks in cuts:
        draws = jax.random.uniform(jax.random.fold_in(jax.random.fold_in(key, 6), axis_at), (blocks,), jnp.float32, least / len(cuts), high / len(cuts))
        factor_of = factor_of * jnp.repeat(jnp.exp(draws), dims[axis_at] // blocks).reshape((-1,) + (1,) * (len(dims) - 1 - axis_at))
    return factor_of


def gaussian(stream_key, extent, scale, bound, cuts=(), held_as=jnp.bfloat16):
    result = scale * jax.random.normal(stream_key, extent, jnp.float32)
    if cuts:
        result = result * block_scale(stream_key, extent, cuts, -0.22, 0.18)
    return jnp.clip(result, -bound, bound).astype(held_as)


def setup_inputs(seed: int = 0) -> dict:
    seeds = jax.random.split(jax.random.key(seed), 14)
    return {
        "actions": gaussian(seeds[0], (MICRO, SAMPLES, H, CI), 1.0, 6.0, ((1, 32),)),
        "observations": gaussian(seeds[1], (MICRO, OBSN, OBS), 1.0, 6.0, ((1, 8), (2, 4))),
        "tsteps": set_ends(jax.random.randint(seeds[2], (MICRO, SAMPLES), 0, NSTEPS), jax.random.fold_in(seeds[2], 1), 0, NSTEPS - 1).astype(jnp.int32),
        "lengths": set_ends(jax.random.randint(seeds[3], (MICRO, SAMPLES), 4, H + 1), jax.random.fold_in(seeds[3], 1), 4, H).astype(jnp.int32),
        "cot_skip": gaussian(seeds[4], (MICRO, SAMPLES, H, C), 1.0, 6.0, ((1, 32),)),
        "cot_down": gaussian(seeds[5], (MICRO, SAMPLES, H // 2, C), 1.0, 6.0, ((1, 32),)),
        "owners": draw_owners(jax.random.fold_in(seeds[13], 71), 0),
        "master": gaussian(seeds[7], (SLOTS, BLK, C), 0.03, 0.1875, ((0, 8),), jnp.float32),
        "moment_one": gaussian(seeds[8], (SLOTS, BLK, C), (0.11 * (MICRO * SAMPLES * H) ** 0.5), 224.0, ((0, 8),), jnp.float32),
        "moment_two": jnp.clip(jnp.exp(math.log(393.216) - 1.3862944 * jax.random.uniform(seeds[9], (SLOTS, BLK, C), jnp.float32) ** block_scale(seeds[9], (SLOTS, BLK, C), ((0, 8),), -0.2, 0.2)), 98.304, 393.216),
        "small_master": draw_small_master(jax.random.fold_in(seeds[13], 71), 0),
        "small_one": gaussian(seeds[11], (NSMALL, C), (0.11 * (MICRO * SAMPLES * H) ** 0.5), 224.0, (), jnp.float32),
        "small_two": jnp.clip(jnp.exp(jax.random.uniform(seeds[12], (NSMALL, C), jnp.float32, math.log(98.304), math.log(393.216))), 98.304, 393.216),
    }


@jax.custom_vjp
def low(v):
    return lax.optimization_barrier(v.astype(jnp.bfloat16)).astype(jnp.float32)

@jax.custom_vjp
def low_back(v):
    return v

def low_keep(v):
    return (low(v), None)

def low_pass(kept, grad):
    return (grad,)

def back_keep(v):
    return (v, None)

def back_low(kept, grad):
    return (low(grad),)
low.defvjp(low_keep, low_pass)
low_back.defvjp(back_keep, back_low)
BETA_ONE = 0.9
BETA_TWO = 0.999
EPS_ADAM = 1e-08
DECAY = 0.01
RATE_MATRIX = 0.1
RATE_SMALL = 1.0
HIGHEST = lax.Precision.HIGHEST

def mish(value):
    return value * jnp.tanh(jax.nn.softplus(value))

def time_embed(step_ids, width):
    half = width // 2
    freq = jnp.exp(-math.log(10000.0) * jnp.arange(half, dtype=jnp.float32) / (half - 1))
    angle = step_ids.astype(jnp.float32)[:, None] * freq[None, :]
    return jnp.concatenate([jnp.sin(angle), jnp.cos(angle)], axis=1)

def group_norm(value, frame_mask, gain, bias):
    count_s, frames, chans = value.shape
    grouped = value.reshape(count_s, frames, GROUPS, chans // GROUPS)
    weight = frame_mask[:, :, None, None]
    count = lax.optimization_barrier(jnp.sum(frame_mask, axis=1))[:, None] * (chans // GROUPS)
    mean = lax.optimization_barrier(jnp.sum(grouped * weight, axis=(1, 3))) / count
    centered = grouped - mean[:, None, :, None]
    var = lax.optimization_barrier(jnp.sum(centered * centered * weight, axis=(1, 3))) / count
    normed = centered * lax.rsqrt(var + 1e-05)[:, None, :, None]
    return normed.reshape(count_s, frames, chans) * gain + bias

def unfold(value, taps, stride):
    pad_width = (taps - 1) // 2
    padded = jnp.pad(value, ((0, 0), (pad_width, pad_width), (0, 0)))
    count = value.shape[1] // stride
    pieces = [padded[:, tap_index:tap_index + stride * (count - 1) + 1:stride] for tap_index in range(taps)]
    return jnp.concatenate(pieces, axis=2)

def convolve(value, weight, taps, stride):
    cols = unfold(value, taps, stride)
    flat = cols.reshape(-1, cols.shape[2])
    return jnp.dot(flat, weight, precision=HIGHEST).reshape(cols.shape[0], cols.shape[1], weight.shape[1])

def slot_of(owners, slot_count):
    same = owners[:, None] == owners[None, :]
    order = jnp.arange(owners.shape[0], dtype=jnp.int32)
    earlier = order[:, None] > order[None, :]
    rank = lax.optimization_barrier(jnp.sum((same & earlier).astype(jnp.int32), axis=1)).astype(jnp.int32)
    return (owners * slot_count + rank).astype(jnp.int32)

def adamw(weight, first_m, second_m, grad, rate):
    first_new = BETA_ONE * first_m + (1.0 - BETA_ONE) * grad
    second_new = BETA_TWO * second_m + (1.0 - BETA_TWO) * grad * grad
    fix_one = 1.0 - BETA_ONE ** STEP
    fix_two = 1.0 - BETA_TWO ** STEP
    update = first_new / fix_one / (jnp.sqrt(second_new / fix_two) + EPS_ADAM) + DECAY * weight
    return (first_new, second_new, weight - rate * update)

def block_forward(x_in, obs_in, step_ids, lens, weights, small):
    frame_mask = (jnp.arange(H)[None, :] < lens[:, None]).astype(jnp.float32)
    masked = x_in * frame_mask[:, :, None]
    offset = 0
    w_first = weights[offset:offset + KW * CI]
    offset = offset + KW * CI
    w_second = weights[offset:offset + KW * C]
    offset = offset + KW * C
    w_res = weights[offset:offset + CI]
    offset = offset + CI
    w_down = weights[offset:offset + KD * C]
    offset = offset + KD * C
    w_film = jnp.concatenate([weights[offset:offset + COND], weights[offset + COND:offset + 2 * COND]], axis=1)
    condition = jnp.concatenate([time_embed(step_ids, TE), obs_in], axis=1)
    cond_low = low(mish(condition))
    b_film = jnp.concatenate([small[3], small[4]])
    modulation = low_back(jnp.dot(cond_low, w_film, precision=HIGHEST) + b_film)
    scale = modulation[:, :C]
    shift = modulation[:, C:]
    first = low_back(convolve(masked, w_first, KW, 1) + small[0])
    hidden = (scale[:, None, :] * mish(group_norm(first, frame_mask, small[1], small[2])) + shift[:, None, :]) * frame_mask[:, :, None]
    hidden = low(hidden)
    second = low_back(convolve(hidden, w_second, KW, 1) + small[5])
    branch = jnp.dot(masked.reshape(-1, CI), w_res, precision=HIGHEST).reshape(masked.shape[0], H, C) + small[8]
    skip = low_back(mish(group_norm(second, frame_mask, small[6], small[7])) + branch)
    skip = low(skip)
    down = convolve(skip, w_down, KD, 2) + small[9]
    return (skip, down)

def reference(actions, observations, tsteps, lengths, cot_skip, cot_down, owners, master, moment_one, moment_two, small_master, small_one, small_two):
    slot_index = slot_of(owners, MOST)
    weights = master.astype(jnp.bfloat16).astype(jnp.float32)[slot_index].reshape(ROWS, C)
    groups_all = MICRO * N_DP * N_PAIR
    x_arr = actions.reshape(groups_all, SAMP, H, CI)
    obs_arr = jnp.broadcast_to(observations.reshape(MICRO, N_DP, 1, SAMP, OBS), (MICRO, N_DP, N_PAIR, SAMP, OBS)).reshape(groups_all, SAMP, OBS)
    step_arr = tsteps.reshape(groups_all, SAMP)
    len_arr = lengths.reshape(groups_all, SAMP)
    cot_one = cot_skip.reshape(groups_all, SAMP, H, C)
    cot_two = cot_down.reshape(groups_all, SAMP, H // 2, C)

    def one_group(carry, item):
        x_g, obs_g, step_g, len_g, cot_a, cot_b = item

        def forward(x_in, obs_in, weight_in, small_in):
            return block_forward(x_in, obs_in, step_g, len_g, weight_in, small_in)
        outs, back = jax.vjp(forward, x_g.astype(jnp.float32), obs_g.astype(jnp.float32), weights, small_master)
        d_x, d_obs, d_weights, d_small = back((cot_a.astype(jnp.float32), cot_b.astype(jnp.float32)))
        carry = (carry[0] + d_weights, carry[1] + d_small)
        return (carry, (outs[0].astype(jnp.bfloat16), outs[1].astype(jnp.bfloat16), d_x, d_obs))
    init = (jnp.zeros((ROWS, C), jnp.float32), jnp.zeros((NSMALL, C), jnp.float32))
    sums, stacked = lax.scan(one_group, init, (x_arr, obs_arr, step_arr, len_arr, cot_one, cot_two))
    grad_weights, grad_small = sums
    skip_out = stacked[0].reshape(MICRO, SAMPLES, H, C)
    down_out = stacked[1].reshape(MICRO, SAMPLES, H // 2, C)
    actions_grad = stacked[2].reshape(MICRO, SAMPLES, H, CI)
    observations_grad = lax.optimization_barrier(jnp.sum(stacked[3].reshape(MICRO, N_DP, N_PAIR, SAMP, OBS), axis=2)).reshape(MICRO, N_DP * SAMP, OBS)
    grad_slots = jnp.zeros((SLOTS, BLK, C), jnp.float32).at[slot_index].set(grad_weights.reshape(NBLK, BLK, C))
    new_one, new_two, new_master = adamw(master, moment_one, moment_two, grad_slots, RATE_MATRIX)
    small_first, small_second, new_small = adamw(small_master, small_one, small_two, grad_small, RATE_SMALL)
    return (skip_out, down_out, actions_grad, observations_grad, new_one, new_two, new_master, small_first, small_second, new_small)
```

```python
import functools
import math

import jax
import jax.numpy as jnp
from jax import lax
from jax.experimental import pallas as pl
from jax.experimental.pallas import tpu as pltpu
from jax.sharding import PartitionSpec as P

CI = 256
C = 512
TE = 128
KW = 5
H = 16
HD = 8
KD = 3
NSMALL = 10
STEP = 10
BLK = 128
COND = 1152
NBLK = 62
GC = 64

FIRST_AT, FIRST_N = 0, 10
SECOND_AT, SECOND_N = 10, 20
RES_AT, RES_N = 30, 2
DOWN_AT, DOWN_N = 32, 12
SCALE_AT, SHIFT_AT, FILM_N = 44, 53, 9

BETA_ONE = 0.9
BETA_TWO = 0.999
EPS_ADAM = 1e-08
DECAY = 0.01
RATE_MATRIX = 0.1
RATE_SMALL = 1.0

F32 = jnp.float32
BF = jnp.bfloat16
NT = (((1,), (1,)), ((), ()))
TN = (((0,), (0,)), ((), ()))
VMEM_LIMIT = 56 * 2**20


def mish(value):
    return value * jnp.tanh(jax.nn.softplus(value))


def time_embed(step_ids, width):
    half = width // 2
    freq = jnp.exp(-math.log(10000.0) * jnp.arange(half, dtype=F32) / (half - 1))
    angle = step_ids.astype(F32)[:, None] * freq[None, :]
    return jnp.concatenate([jnp.sin(angle), jnp.cos(angle)], axis=1)


def slot_of(owners, slot_count):
    same = owners[:, None] == owners[None, :]
    order = jnp.arange(owners.shape[0], dtype=jnp.int32)
    earlier = order[:, None] > order[None, :]
    rank = jnp.sum((same & earlier).astype(jnp.int32), axis=1)
    return owners * slot_count + rank


def adamw(weight, first_m, second_m, grad, rate):
    first_new = BETA_ONE * first_m + (1.0 - BETA_ONE) * grad
    second_new = BETA_TWO * second_m + (1.0 - BETA_TWO) * grad * grad
    fix_one = 1.0 - BETA_ONE**STEP
    fix_two = 1.0 - BETA_TWO**STEP
    update = first_new / fix_one / (jnp.sqrt(second_new / fix_two) + EPS_ADAM) + DECAY * weight
    return (first_new, second_new, weight - rate * update)


def recip(value):
    r = pl.reciprocal(value, approx=True)
    return r * (2.0 - value * r)


def mish_parts(v):
    w = jnp.exp(jnp.minimum(v, 30.0))
    n = w * (w + 2.0)
    r = recip(n + 2.0)
    return w, n * r, r


def mish_only(v):
    _, t, _ = mish_parts(v)
    return v * t


def mish_both(v):
    w, t, r = mish_parts(v)
    return v * t, t + (4.0 * v) * (((w * (1.0 + w)) * r) * r)


def group_sum(value):
    low_half = lax.broadcasted_iota(jnp.int32, value.shape, 1) < GC
    zero = jnp.zeros_like(value)
    left = jnp.sum(jnp.where(low_half, value, zero), axis=1, keepdims=True)
    right = jnp.sum(jnp.where(low_half, zero, value), axis=1, keepdims=True)
    return jnp.where(low_half, left, right)


def lanes(q):
    return slice(q * 128, (q + 1) * 128)


def fetch(w_hbm, at, count, dst, sem, k):
    return [
        pltpu.make_async_copy(w_hbm.at[p, at : at + count], dst.at[:, p], sem.at[k, p])
        for p in range(4)
    ]


def begin(copies):
    for copy in copies:
        copy.start()


def finish(copies):
    for copy in copies:
        copy.wait()


def matrix(ref, at, count):
    return ref[at : at + count].reshape(count * BLK, C)


def first_kernel(w_hbm, x_ref, cond_ref, lens_ref, inv_ref, small_ref, normed_ref, rstd_ref, hid_ref, mod_ref,
                 w_one, w_film, xp, fst, sem):
    step = pl.program_id(0)
    frames, width, _ = x_ref.shape
    rows = frames * width

    @pl.when(step == 0)
    def _():
        film = fetch(w_hbm, SCALE_AT, 2 * FILM_N, w_film, sem, 0)
        one = fetch(w_hbm, FIRST_AT, FIRST_N, w_one, sem, 1)
        begin(film)
        begin(one)
        xp[0:2] = jnp.zeros((2, width, CI), BF)
        xp[frames + 2 :] = jnp.zeros((2, width, CI), BF)
        finish(film)
        for k in range(2):
            mod_ref[k] = (
                jnp.dot(cond_ref[...], matrix(w_film, k * FILM_N, FILM_N), preferred_element_type=F32)
                + small_ref[3 + k : 4 + k]
            )
        finish(one)

    xp[2 : frames + 2] = x_ref[...]
    acc = jnp.dot(xp[0:frames].reshape(rows, CI), matrix(w_one, 0, 2), preferred_element_type=F32)
    for a in range(1, KW):
        acc = acc + jnp.dot(
            xp[a : a + frames].reshape(rows, CI), matrix(w_one, 2 * a, 2), preferred_element_type=F32
        )
    fst[...] = (acc + small_ref[0:1]).reshape(frames, width, C)

    here = pl.ds(pl.multiple_of(step * width, width), width)
    lens = lens_ref[...]
    inv = inv_ref[...]
    for q in range(C // 128):
        ls = lanes(q)
        total = jnp.zeros((width, 128), F32)
        for t in range(frames):
            total = total + jnp.where(lens > t, fst[t, :, ls], 0.0)
        mean = group_sum(total) * inv
        total = jnp.zeros((width, 128), F32)
        for t in range(frames):
            centered = fst[t, :, ls] - mean
            total = total + jnp.where(lens > t, centered * centered, 0.0)
        rstd = lax.rsqrt(group_sum(total) * inv + 1e-05)
        rstd_ref[:, ls] = rstd
        gain, bias = small_ref[1:2, ls], small_ref[2:3, ls]
        scale, shift = mod_ref[0, here, ls], mod_ref[1, here, ls]
        for t in range(frames):
            normed = (fst[t, :, ls] - mean) * rstd
            normed_ref[t, :, ls] = normed
            value = scale * mish_only(normed * gain + bias) + shift
            hid_ref[t, :, ls] = jnp.where(lens > t, value, 0.0).astype(BF)


def second_kernel(w_hbm, hid_ref, x_ref, cs_ref, cd_ref, lens_ref, inv_ref, small_ref, skip_ref, dskip_ref, g2_ref,
                  gw_ref, gs_ref, w_two, w_res, w_down, hp, cdp, sec, br, dev, dod, se, so, acc, sem):
    step = pl.program_id(0)
    last = pl.num_programs(0) - 1
    frames, width, _ = x_ref.shape
    half = frames // 2
    rows = frames * width

    @pl.when(step == 0)
    def _():
        down = fetch(w_hbm, DOWN_AT, DOWN_N, w_down, sem, 0)
        res = fetch(w_hbm, RES_AT, RES_N, w_res, sem, 1)
        two = fetch(w_hbm, SECOND_AT, SECOND_N, w_two, sem, 2)
        begin(down)
        begin(res)
        begin(two)
        hp[0:2] = jnp.zeros((2, width, C), BF)
        hp[frames + 2 :] = jnp.zeros((2, width, C), BF)
        cdp[half:] = jnp.zeros((1, width, C), BF)
        so[0:1] = jnp.zeros((1, width, C), BF)
        acc[...] = jnp.zeros_like(acc)
        gs_ref[...] = jnp.zeros_like(gs_ref)
        finish(down)
        finish(res)
        finish(two)

    hp[2 : frames + 2] = hid_ref[...]
    cdp[0:half] = cd_ref[...]
    cot = cdp[0:half].reshape(half * width, C)
    cot_next = cdp[1 : half + 1].reshape(half * width, C)
    dev[...] = lax.dot_general(cot, matrix(w_down, 4, 4), NT, preferred_element_type=F32).reshape(half, width, C)
    dod[...] = (
        lax.dot_general(cot, matrix(w_down, 8, 4), NT, preferred_element_type=F32)
        + lax.dot_general(cot_next, matrix(w_down, 0, 4), NT, preferred_element_type=F32)
    ).reshape(half, width, C)
    br[...] = (
        jnp.dot(x_ref[...].reshape(rows, CI), matrix(w_res, 0, 2), preferred_element_type=F32) + small_ref[8:9]
    ).reshape(frames, width, C)
    total = jnp.dot(hp[0:frames].reshape(rows, C), matrix(w_two, 0, 4), preferred_element_type=F32)
    for a in range(1, KW):
        total = total + jnp.dot(
            hp[a : a + frames].reshape(rows, C), matrix(w_two, 4 * a, 4), preferred_element_type=F32
        )
    sec[...] = (total + small_ref[5:6]).reshape(frames, width, C)

    lens = lens_ref[...]
    inv = inv_ref[...]
    zero = jnp.zeros((width, 128), F32)
    for q in range(C // 128):
        ls = lanes(q)
        total = zero
        for t in range(frames):
            total = total + jnp.where(lens > t, sec[t, :, ls], 0.0)
        mean = group_sum(total) * inv
        total = zero
        for t in range(frames):
            centered = sec[t, :, ls] - mean
            total = total + jnp.where(lens > t, centered * centered, 0.0)
        rstd = lax.rsqrt(group_sum(total) * inv + 1e-05)
        gain, bias = small_ref[6:7, ls], small_ref[7:8, ls]
        sum_dy, sum_dyn, sum_ds = zero, zero, zero
        for t in range(frames):
            normed = (sec[t, :, ls] - mean) * rstd
            sec[t, :, ls] = normed
            act, slope = mish_both(normed * gain + bias)
            skip = (act + br[t, :, ls]).astype(BF)
            skip_ref[t, :, ls] = skip
            if t % 2:
                so[t // 2 + 1, :, ls] = skip
                back = dod[t // 2, :, ls]
            else:
                se[t // 2, :, ls] = skip
                back = dev[t // 2, :, ls]
            ds = (cs_ref[t, :, ls].astype(F32) + back).astype(BF)
            dskip_ref[t, :, ls] = ds
            ds = ds.astype(F32)
            sum_ds = sum_ds + ds
            dy = ds * slope
            br[t, :, ls] = dy
            sum_dy = sum_dy + dy
            sum_dyn = sum_dyn + dy * normed
        mean_a = group_sum(sum_dy * gain) * inv
        mean_an = group_sum(sum_dyn * gain) * inv
        sum_g, sum_cd = zero, zero
        for t in range(frames):
            normed = sec[t, :, ls]
            grad = rstd * (br[t, :, ls] * gain - jnp.where(lens > t, mean_a + normed * mean_an, 0.0))
            grad = grad.astype(BF)
            g2_ref[t, :, ls] = grad
            sum_g = sum_g + grad.astype(F32)
        for t in range(half):
            sum_cd = sum_cd + cd_ref[t, :, ls].astype(F32)
        for k, part in enumerate((sum_g, sum_dyn, sum_dy, sum_ds, sum_cd)):
            gs_ref[k : k + 1, ls] += jnp.sum(part, axis=0, keepdims=True)

    grad_two = g2_ref[...].reshape(rows, C)
    for a in range(KW):
        acc[a * C : (a + 1) * C] += lax.dot_general(
            hp[a : a + frames].reshape(rows, C), grad_two, TN, preferred_element_type=F32
        )
    at = KW * C
    acc[at : at + CI] += lax.dot_general(
        x_ref[...].reshape(rows, CI), dskip_ref[...].reshape(rows, C), TN, preferred_element_type=F32
    )
    at = at + CI
    for a, source in enumerate((so.at[0:half], se, so.at[1 : half + 1])):
        acc[at + a * C : at + (a + 1) * C] += lax.dot_general(
            source[...].reshape(half * width, C), cot, TN, preferred_element_type=F32
        )

    @pl.when(step == last)
    def _():
        for b in range(acc.shape[0] // BLK):
            for p in range(4):
                at = b * BLK + p * 32
                gw_ref[p, b] = acc[at : at + 32].astype(BF)


def third_kernel(w_hbm, g2_ref, x_ref, cond_ref, normed_ref, rstd_ref, mod_ref, lens_ref, inv_ref, small_ref,
                 g1_ref, dmod_ref, gw_ref, gs_ref, w_two, gp, xp, dh, acc, sem):
    step = pl.program_id(0)
    last = pl.num_programs(0) - 1
    frames, width, _ = x_ref.shape
    rows = frames * width

    @pl.when(step == 0)
    def _():
        two = fetch(w_hbm, SECOND_AT, SECOND_N, w_two, sem, 0)
        begin(two)
        gp[0:2] = jnp.zeros((2, width, C), BF)
        gp[frames + 2 :] = jnp.zeros((2, width, C), BF)
        xp[0:2] = jnp.zeros((2, width, CI), BF)
        xp[frames + 2 :] = jnp.zeros((2, width, CI), BF)
        acc[...] = jnp.zeros_like(acc)
        gs_ref[...] = jnp.zeros_like(gs_ref)
        finish(two)

    gp[2 : frames + 2] = g2_ref[...]
    xp[2 : frames + 2] = x_ref[...]
    total = lax.dot_general(gp[4 : 4 + frames].reshape(rows, C), matrix(w_two, 0, 4), NT, preferred_element_type=F32)
    for a in range(1, KW):
        total = total + lax.dot_general(
            gp[4 - a : 4 - a + frames].reshape(rows, C), matrix(w_two, 4 * a, 4), NT, preferred_element_type=F32
        )
    dh[...] = total.reshape(frames, width, C)

    here = pl.ds(pl.multiple_of(step * width, width), width)
    lens = lens_ref[...]
    inv = inv_ref[...]
    zero = jnp.zeros((width, 128), F32)
    for q in range(C // 128):
        ls = lanes(q)
        gain, bias = small_ref[1:2, ls], small_ref[2:3, ls]
        scale = mod_ref[0, here, ls]
        sum_dy, sum_dyn, d_scale, d_shift = zero, zero, zero, zero
        for t in range(frames):
            normed = normed_ref[t, :, ls]
            act, slope = mish_both(normed * gain + bias)
            grad = jnp.where(lens > t, dh[t, :, ls], 0.0)
            d_scale = d_scale + grad * act
            d_shift = d_shift + grad
            dy = (grad * scale) * slope
            dh[t, :, ls] = dy
            sum_dy = sum_dy + dy
            sum_dyn = sum_dyn + dy * normed
        mean_a = group_sum(sum_dy * gain) * inv
        mean_an = group_sum(sum_dyn * gain) * inv
        rstd = rstd_ref[:, ls]
        sum_g = zero
        for t in range(frames):
            normed = normed_ref[t, :, ls]
            grad = rstd * (dh[t, :, ls] * gain - jnp.where(lens > t, mean_a + normed * mean_an, 0.0))
            grad = grad.astype(BF)
            g1_ref[t, :, ls] = grad
            sum_g = sum_g + grad.astype(F32)
        d_scale, d_shift = d_scale.astype(BF), d_shift.astype(BF)
        dmod_ref[0, here, ls] = d_scale
        dmod_ref[1, here, ls] = d_shift
        for k, part in enumerate((sum_g, sum_dyn, sum_dy, d_scale.astype(F32), d_shift.astype(F32))):
            gs_ref[k : k + 1, ls] += jnp.sum(part, axis=0, keepdims=True)

    grad_one = g1_ref[...].reshape(rows, C)
    for a in range(KW):
        acc[a * CI : (a + 1) * CI] += lax.dot_general(
            xp[a : a + frames].reshape(rows, CI), grad_one, TN, preferred_element_type=F32
        )

    @pl.when(step == last)
    def _():
        for b in range(FIRST_N):
            for p in range(4):
                at = b * BLK + p * 32
                gw_ref[p, b] = acc[at : at + 32].astype(BF)
        for k in range(2):
            film = lax.dot_general(cond_ref[...], dmod_ref[k], TN, preferred_element_type=F32).astype(BF)
            for b in range(FILM_N):
                for p in range(4):
                    at = b * BLK + p * 32
                    gw_ref[p, FIRST_N + k * FILM_N + b] = film[at : at + 32]


def fourth_kernel(w_hbm, skip_ref, g1_ref, dskip_ref, dmod_ref, slope_ref, lens_ref, small_ref, down_ref, dx_ref,
                  dobs_ref, w_one, w_res, w_down, w_film, gp, se, so, sem):
    step = pl.program_id(0)
    frames, width, _ = skip_ref.shape
    half = frames // 2
    rows = frames * width

    @pl.when(step == 0)
    def _():
        film = fetch(w_hbm, SCALE_AT, 2 * FILM_N, w_film, sem, 0)
        one = fetch(w_hbm, FIRST_AT, FIRST_N, w_one, sem, 1)
        res = fetch(w_hbm, RES_AT, RES_N, w_res, sem, 2)
        down = fetch(w_hbm, DOWN_AT, DOWN_N, w_down, sem, 3)
        begin(film)
        begin(one)
        begin(res)
        begin(down)
        gp[0:2] = jnp.zeros((2, width, C), BF)
        gp[frames + 2 :] = jnp.zeros((2, width, C), BF)
        so[0:1] = jnp.zeros((1, width, C), BF)
        finish(film)
        back = lax.dot_general(dmod_ref[0], matrix(w_film, 1, FILM_N - 1), NT, preferred_element_type=F32)
        back = back + lax.dot_general(
            dmod_ref[1], matrix(w_film, FILM_N + 1, FILM_N - 1), NT, preferred_element_type=F32
        )
        dobs_ref[...] = back * slope_ref[...]
        finish(one)
        finish(res)
        finish(down)

    gp[2 : frames + 2] = g1_ref[...]
    total = lax.dot_general(dskip_ref[...].reshape(rows, C), matrix(w_res, 0, 2), NT, preferred_element_type=F32)
    for a in range(KW):
        total = total + lax.dot_general(
            gp[4 - a : 4 - a + frames].reshape(rows, C), matrix(w_one, 2 * a, 2), NT, preferred_element_type=F32
        )
    total = total.reshape(frames, width, CI)
    lens = lens_ref[...]
    for t in range(frames):
        for q in range(CI // 128):
            dx_ref[t, :, lanes(q)] = jnp.where(lens > t, total[t, :, lanes(q)], 0.0)
    for j in range(half):
        se[j] = skip_ref[2 * j]
        so[j + 1] = skip_ref[2 * j + 1]
    down = jnp.dot(so[0:half].reshape(half * width, C), matrix(w_down, 0, 4), preferred_element_type=F32)
    down = down + jnp.dot(se[...].reshape(half * width, C), matrix(w_down, 4, 4), preferred_element_type=F32)
    down = down + jnp.dot(
        so[1 : half + 1].reshape(half * width, C), matrix(w_down, 8, 4), preferred_element_type=F32
    )
    down_ref[...] = (down + small_ref[9:10]).astype(BF).reshape(half, width, C)


def tiles(frames, width, channels):
    return pl.BlockSpec((frames, width, channels), lambda i: (0, i, 0))


def rows_of(width, channels):
    return pl.BlockSpec((width, channels), lambda i: (i, 0))


def whole(*shape):
    return pl.BlockSpec(shape, lambda i: (0,) * len(shape))


ANY = pl.BlockSpec(memory_space=pl.ANY)
PARAMS = pltpu.CompilerParams(vmem_limit_bytes=VMEM_LIMIT, dimension_semantics=("arbitrary",))


def weight_scratch(count):
    return pltpu.VMEM((count, 4, 32, C), BF)


def shape(*dims, dtype=F32):
    return jax.ShapeDtypeStruct(dims, dtype)


def run_first(weights, x, cond, lens, inv, small, width):
    count = x.shape[1]
    return pl.pallas_call(
        first_kernel,
        grid=(count // width,),
        in_specs=[ANY, tiles(H, width, CI), whole(count, COND), rows_of(width, 128), rows_of(width, 128),
                  whole(NSMALL, C)],
        out_specs=[tiles(H, width, C), rows_of(width, C), tiles(H, width, C), whole(2, count, C)],
        out_shape=[shape(H, count, C), shape(count, C), shape(H, count, C, dtype=BF), shape(2, count, C)],
        scratch_shapes=[weight_scratch(FIRST_N), weight_scratch(2 * FILM_N), pltpu.VMEM((H + 4, width, CI), BF),
                        pltpu.VMEM((H, width, C), F32), pltpu.SemaphoreType.DMA((2, 4))],
        compiler_params=PARAMS,
        name="first",
    )(weights, x, cond, lens, inv, small)


def run_second(weights, hid, x, cs, cd, lens, inv, small, width):
    count = x.shape[1]
    blocks = SECOND_N + RES_N + DOWN_N
    return pl.pallas_call(
        second_kernel,
        grid=(count // width,),
        in_specs=[ANY, tiles(H, width, C), tiles(H, width, CI), tiles(H, width, C), tiles(HD, width, C),
                  rows_of(width, 128), rows_of(width, 128), whole(NSMALL, C)],
        out_specs=[tiles(H, width, C), tiles(H, width, C), tiles(H, width, C), whole(4, blocks, 32, C), whole(8, C)],
        out_shape=[shape(H, count, C, dtype=BF)] * 3 + [shape(4, blocks, 32, C, dtype=BF), shape(8, C)],
        scratch_shapes=[weight_scratch(SECOND_N), weight_scratch(RES_N), weight_scratch(DOWN_N),
                        pltpu.VMEM((H + 4, width, C), BF), pltpu.VMEM((HD + 1, width, C), BF),
                        pltpu.VMEM((H, width, C), F32), pltpu.VMEM((H, width, C), F32),
                        pltpu.VMEM((HD, width, C), F32), pltpu.VMEM((HD, width, C), F32),
                        pltpu.VMEM((HD, width, C), BF), pltpu.VMEM((HD + 1, width, C), BF),
                        pltpu.VMEM((blocks * BLK, C), F32), pltpu.SemaphoreType.DMA((3, 4))],
        compiler_params=PARAMS,
        name="second",
    )(weights, hid, x, cs, cd, lens, inv, small)


def run_third(weights, g2, x, cond, normed, rstd, mod, lens, inv, small, width):
    count = x.shape[1]
    blocks = FIRST_N + 2 * FILM_N
    return pl.pallas_call(
        third_kernel,
        grid=(count // width,),
        in_specs=[ANY, tiles(H, width, C), tiles(H, width, CI), whole(count, COND), tiles(H, width, C),
                  rows_of(width, C), whole(2, count, C), rows_of(width, 128), rows_of(width, 128), whole(NSMALL, C)],
        out_specs=[tiles(H, width, C), whole(2, count, C), whole(4, blocks, 32, C), whole(8, C)],
        out_shape=[shape(H, count, C, dtype=BF), shape(2, count, C, dtype=BF), shape(4, blocks, 32, C, dtype=BF),
                   shape(8, C)],
        scratch_shapes=[weight_scratch(SECOND_N), pltpu.VMEM((H + 4, width, C), BF),
                        pltpu.VMEM((H + 4, width, CI), BF), pltpu.VMEM((H, width, C), F32),
                        pltpu.VMEM((FIRST_N * BLK, C), F32), pltpu.SemaphoreType.DMA((1, 4))],
        compiler_params=PARAMS,
        name="third",
    )(weights, g2, x, cond, normed, rstd, mod, lens, inv, small)


def run_fourth(weights, skip, g1, dskip, dmod, slope, lens, small, width):
    count = skip.shape[1]
    features = slope.shape[1]
    return pl.pallas_call(
        fourth_kernel,
        grid=(count // width,),
        in_specs=[ANY, tiles(H, width, C), tiles(H, width, C), tiles(H, width, C), whole(2, count, C),
                  whole(count, features), rows_of(width, 128), whole(NSMALL, C)],
        out_specs=[tiles(HD, width, C), tiles(H, width, CI), whole(count, features)],
        out_shape=[shape(HD, count, C, dtype=BF), shape(H, count, CI), shape(count, features)],
        scratch_shapes=[weight_scratch(FIRST_N), weight_scratch(RES_N), weight_scratch(DOWN_N),
                        weight_scratch(2 * FILM_N), pltpu.VMEM((H + 4, width, C), BF),
                        pltpu.VMEM((HD, width, C), BF), pltpu.VMEM((HD + 1, width, C), BF),
                        pltpu.SemaphoreType.DMA((4, 4))],
        compiler_params=PARAMS,
        name="fourth",
    )(weights, skip, g1, dskip, dmod, slope, lens, small)


def local_work(weights, actions, shared, tsteps, lengths, cot_skip, cot_down, small_master):
    micro, samp = lengths.shape
    count = micro * samp
    lens_flat = lengths.reshape(count)
    lens = jnp.broadcast_to(lens_flat.astype(F32)[:, None], (count, 128))
    inv = 1.0 / (lens * GC)
    keep = jnp.arange(H)[:, None, None] < lens_flat[None, :, None]
    x = jnp.where(keep, actions.reshape(count, H, CI).transpose(1, 0, 2), jnp.zeros((), BF))
    cs = cot_skip.reshape(count, H, C).transpose(1, 0, 2)
    cd = cot_down.reshape(count, HD, C).transpose(1, 0, 2)
    obs = shared.reshape(count, -1).astype(F32)
    obs_act, obs_back = jax.vjp(mish, obs)
    slope = obs_back(jnp.ones_like(obs))[0]
    cond = jnp.concatenate([mish(time_embed(tsteps.reshape(count), TE)), obs_act], axis=1).astype(BF)

    width = samp
    normed, rstd, hid, mod = run_first(weights, x, cond, lens, inv, small_master, width)
    skip, dskip, g2, gw_late, gs_late = run_second(weights, hid, x, cs, cd, lens, inv, small_master, width)
    g1, dmod, gw_early, gs_early = run_third(
        weights, g2, x, cond, normed, rstd, mod, lens, inv, small_master, width
    )
    down, dx, dobs = run_fourth(weights, skip, g1, dskip, dmod, slope, lens, small_master, width)
    skip_out = skip.transpose(1, 0, 2).reshape(micro, samp, H, C)
    down_out = down.transpose(1, 0, 2).reshape(micro, samp, HD, C)
    actions_grad = dx.transpose(1, 0, 2).reshape(micro, samp, H, CI)
    obs_local = dobs.reshape(micro, samp, -1)
    g_small = jnp.concatenate(
        [gs_early[0:5], gs_late[0:5]], axis=0
    )
    return skip_out, down_out, actions_grad, obs_local, gw_early, gw_late, g_small


def body(
    actions,
    observations,
    tsteps,
    lengths,
    cot_skip,
    cot_down,
    owners,
    master,
    moment_one,
    moment_two,
    small_master,
    small_one,
    small_two,
):
    slot_count = master.shape[0]
    dp_count = lax.axis_size("dp")
    slots_all = dp_count * slot_count
    me_pair = lax.axis_index("pair")
    me_dp = lax.axis_index("dp")
    slot_index = slot_of(owners, slot_count)
    block_of = (
        jnp.full((slots_all,), -1, jnp.int32).at[slot_index].set(jnp.arange(NBLK, dtype=jnp.int32))
    )
    quarter = lax.dynamic_slice_in_dim(master, me_pair * 32, 32, axis=1).astype(BF)
    slots = lax.all_gather(quarter, "dp", axis=0, tiled=True)
    mine = jnp.take(slots, slot_index, axis=0)
    weights = lax.all_gather(mine, "pair", axis=0)
    shared = lax.all_gather(observations, "pair", axis=2, tiled=True)

    skip_out, down_out, actions_grad, obs_local, gw_early, gw_late, g_small = local_work(
        weights, actions, shared, tsteps, lengths, cot_skip, cot_down, small_master
    )

    late = lax.psum_scatter(gw_late, "pair", scatter_dimension=0)
    early = lax.psum_scatter(gw_early, "pair", scatter_dimension=0)
    grad_small = lax.psum(g_small, ("dp", "pair"))
    observations_grad = lax.psum_scatter(obs_local, "pair", scatter_dimension=2, tiled=True)
    grads = jnp.concatenate([early[:FIRST_N], late, early[FIRST_N:]], axis=0)
    spread = jnp.take(grads, jnp.maximum(block_of, 0), axis=0)
    owned = lax.psum_scatter(spread, "dp", scatter_dimension=0, tiled=True)
    owned = lax.all_gather(owned, "pair", axis=1, tiled=True)
    used = lax.dynamic_slice_in_dim(block_of, me_dp * slot_count, slot_count, axis=0) >= 0
    owned = jnp.where(used[:, None, None], owned.astype(F32), 0.0)
    new_one, new_two, new_master = adamw(master, moment_one, moment_two, owned, RATE_MATRIX)
    small_first, small_second, new_small = adamw(
        small_master, small_one, small_two, grad_small, RATE_SMALL
    )
    return (
        skip_out,
        down_out,
        actions_grad,
        observations_grad,
        new_one,
        new_two,
        new_master,
        small_first,
        small_second,
        new_small,
    )


def solution(mesh):
    placed = (
        P(None, ("dp", "pair"), None, None),
        P(None, "dp", "pair"),
        P(None, ("dp", "pair")),
        P(None, ("dp", "pair")),
        P(None, ("dp", "pair"), None, None),
        P(None, ("dp", "pair"), None, None),
        P(),
        P("dp", None, None),
        P("dp", None, None),
        P("dp", None, None),
        P(),
        P(),
        P(),
    )
    return jax.shard_map(
        body,
        mesh=mesh,
        in_specs=placed,
        out_specs=(
            P(None, ("dp", "pair"), None, None),
            P(None, ("dp", "pair"), None, None),
            P(None, ("dp", "pair"), None, None),
            P(None, "dp", "pair"),
            P("dp", None, None),
            P("dp", None, None),
            P("dp", None, None),
            P(),
            P(),
            P(),
        ),
        check_vma=False,
    )
```

```python
import functools
import math

import jax
import jax.numpy as jnp
from jax import lax
from jax.experimental import pallas as pl
from jax.experimental.pallas import tpu as pltpu
from jax.sharding import PartitionSpec as P

CI = 256
C = 512
TE = 128
KW = 5
H = 16
HD = 8
KD = 3
NSMALL = 10
STEP = 10
BLK = 128
COND = 1152
NBLK = 62
GC = 64

FIRST_N, SECOND_N, RES_N, DOWN_N, FILM_N = 10, 20, 2, 12, 9
EARLY_N = FIRST_N + 2 * FILM_N
LATE_N = SECOND_N + RES_N + DOWN_N
DOWN_IN = SECOND_N + RES_N
PIECES = 32

BETA_ONE = 0.9
BETA_TWO = 0.999
EPS_ADAM = 1e-08
DECAY = 0.01
RATE_MATRIX = 0.1
RATE_SMALL = 1.0

F32 = jnp.float32
BF = jnp.bfloat16
NT = (((1,), (1,)), ((), ()))
TN = (((0,), (0,)), ((), ()))
VMEM_LIMIT = 56 * 2**20


def mish(value):
    return value * jnp.tanh(jax.nn.softplus(value))


def time_embed(step_ids, width):
    half = width // 2
    freq = jnp.exp(-math.log(10000.0) * jnp.arange(half, dtype=F32) / (half - 1))
    angle = step_ids.astype(F32)[:, None] * freq[None, :]
    return jnp.concatenate([jnp.sin(angle), jnp.cos(angle)], axis=1)


def slot_of(owners, slot_count):
    same = owners[:, None] == owners[None, :]
    order = jnp.arange(owners.shape[0], dtype=jnp.int32)
    earlier = order[:, None] > order[None, :]
    rank = jnp.sum((same & earlier).astype(jnp.int32), axis=1)
    return owners * slot_count + rank


def adamw(weight, first_m, second_m, grad, rate):
    first_new = BETA_ONE * first_m + (1.0 - BETA_ONE) * grad
    second_new = BETA_TWO * second_m + (1.0 - BETA_TWO) * grad * grad
    fix_one = 1.0 - BETA_ONE**STEP
    fix_two = 1.0 - BETA_TWO**STEP
    update = first_new / fix_one / (jnp.sqrt(second_new / fix_two) + EPS_ADAM) + DECAY * weight
    return (first_new, second_new, weight - rate * update)


def recip(value):
    r = pl.reciprocal(value, approx=True)
    return r * (2.0 - value * r)


def mish_parts(v):
    w = jnp.exp(jnp.minimum(v, 30.0))
    n = w * (w + 2.0)
    r = recip(n + 2.0)
    return w, n * r, r


def mish_only(v):
    _, t, _ = mish_parts(v)
    return v * t


def mish_both(v):
    w, t, r = mish_parts(v)
    return v * t, t + (4.0 * v) * (((w * (1.0 + w)) * r) * r)


def group_sum(value):
    low_half = lax.broadcasted_iota(jnp.int32, value.shape, 1) < GC
    zero = jnp.zeros_like(value)
    left = jnp.sum(jnp.where(low_half, value, zero), axis=1, keepdims=True)
    right = jnp.sum(jnp.where(low_half, zero, value), axis=1, keepdims=True)
    return jnp.where(low_half, left, right)


def lanes(q):
    return slice(q * 128, (q + 1) * 128)


def flips_of(k):
    return (k >> 3) & 1, (k >> 2) & 1, (k >> 1) & 1, k & 1


def place(me, k, by_y_first, core):
    one, two, z_low, z_high = flips_of(k)
    y, x = (one, two) if by_y_first else (two, one)
    return me[0] ^ (z_high * 4 + z_low * 2 + y), me[1] ^ (x * 2 + core)


def fetch(me, sources, dst, sem):
    at = 0
    for by_y_first, pair in ((False, sources[:2]), (True, sources[2:])):
        count = pair[0].shape[1]
        for core, source in enumerate(pair):
            for k in range(16):
                row, col = place(me, k, by_y_first, core)
                pltpu.make_async_copy(
                    source.at[k],
                    dst.at[at : at + count, row, :, pl.ds(pl.multiple_of(col * 128, 128), 128)],
                    sem,
                ).start()
        at = at + count
    return pltpu.make_async_copy(dst, dst, sem)


def store_pieces(me, acc, outs, base=0):
    at = 0
    for by_y_first, pair in ((False, outs[:2]), (True, outs[2:])):
        count = pair[0].shape[1]

        def one_block(b, carry, at=at, by_y_first=by_y_first, pair=pair):
            for core, out in enumerate(pair):
                for k in range(16):
                    row, col = place(me, k, by_y_first, core)
                    rows = pl.ds(pl.multiple_of((at + b) * BLK + row * 16, 16), 16)
                    cols = pl.ds(pl.multiple_of(col * 128, 128), 128)
                    out[k, b] = acc[rows, cols].astype(BF)
            return carry

        lax.fori_loop(0, count, one_block, 0)
        at = at + count


def matrix(ref, at, count):
    return ref[at : at + count].reshape(count * BLK, C)


def first_kernel(me, pa, pb, pc, pd, x_ref, cond_ref, lens_ref, inv_ref, small_ref, normed_ref, rstd_ref, hid_ref,
                 mod_ref, w_out, w_one, xp, fst, sem):
    step = pl.program_id(0)
    frames, width, _ = x_ref.shape
    rows = frames * width

    @pl.when(step == 0)
    def _():
        arrival = fetch((me[0], me[1]), (pa, pb, pc, pd), w_one, sem.at[0])
        xp[0:2] = jnp.zeros((2, width, CI), BF)
        xp[frames + 2 :] = jnp.zeros((2, width, CI), BF)
        arrival.wait()
        pltpu.make_async_copy(w_one, w_out, sem.at[1]).start()
        for k in range(2):
            mod_ref[k] = (
                jnp.dot(cond_ref[...], matrix(w_one, FIRST_N + k * FILM_N, FILM_N), preferred_element_type=F32)
                + small_ref[3 + k : 4 + k]
            )

    xp[2 : frames + 2] = x_ref[...]
    acc = jnp.dot(xp[0:frames].reshape(rows, CI), matrix(w_one, 0, 2), preferred_element_type=F32)
    for a in range(1, KW):
        acc = acc + jnp.dot(
            xp[a : a + frames].reshape(rows, CI), matrix(w_one, 2 * a, 2), preferred_element_type=F32
        )
    fst[...] = (acc + small_ref[0:1]).reshape(frames, width, C)

    here = pl.ds(pl.multiple_of(step * width, width), width)
    lens = lens_ref[...]
    inv = inv_ref[...]
    for q in range(C // 128):
        ls = lanes(q)
        total = jnp.zeros((width, 128), F32)
        for t in range(frames):
            total = total + jnp.where(lens > t, fst[t, :, ls], 0.0)
        mean = group_sum(total) * inv
        total = jnp.zeros((width, 128), F32)
        for t in range(frames):
            centered = fst[t, :, ls] - mean
            total = total + jnp.where(lens > t, centered * centered, 0.0)
        rstd = lax.rsqrt(group_sum(total) * inv + 1e-05)
        rstd_ref[:, ls] = rstd
        gain, bias = small_ref[1:2, ls], small_ref[2:3, ls]
        scale, shift = mod_ref[0, here, ls], mod_ref[1, here, ls]
        for t in range(frames):
            normed = (fst[t, :, ls] - mean) * rstd
            normed_ref[t, :, ls] = normed
            value = scale * mish_only(normed * gain + bias) + shift
            hid_ref[t, :, ls] = jnp.where(lens > t, value, 0.0).astype(BF)

    @pl.when(step == pl.num_programs(0) - 1)
    def _():
        pltpu.make_async_copy(w_one, w_out, sem.at[1]).wait()


def second_kernel(me, pa, pb, pc, pd, hid_ref, x_ref, cs_ref, cd_ref, lens_ref, inv_ref, small_ref, skip_ref,
                  dskip_ref, g2_ref, ga, gb, gc, gd, gs_ref, w_out, w_two, hp, cdp, sec, br, dev, dod, se, so, acc,
                  sem):
    step = pl.program_id(0)
    last = pl.num_programs(0) - 1
    frames, width, _ = x_ref.shape
    half = frames // 2
    rows = frames * width

    @pl.when(step == 0)
    def _():
        arrival = fetch((me[0], me[1]), (pa, pb, pc, pd), w_two, sem.at[0])
        hp[0:2] = jnp.zeros((2, width, C), BF)
        hp[frames + 2 :] = jnp.zeros((2, width, C), BF)
        cdp[half:] = jnp.zeros((1, width, C), BF)
        so[0:1] = jnp.zeros((1, width, C), BF)
        acc[...] = jnp.zeros_like(acc)
        gs_ref[...] = jnp.zeros_like(gs_ref)
        arrival.wait()
        pltpu.make_async_copy(w_two, w_out, sem.at[1]).start()

    hp[2 : frames + 2] = hid_ref[...]
    cdp[0:half] = cd_ref[...]
    cot = cdp[0:half].reshape(half * width, C)
    cot_next = cdp[1 : half + 1].reshape(half * width, C)
    dev[...] = lax.dot_general(cot, matrix(w_two, DOWN_IN + 4, 4), NT, preferred_element_type=F32).reshape(half, width, C)
    dod[...] = (
        lax.dot_general(cot, matrix(w_two, DOWN_IN + 8, 4), NT, preferred_element_type=F32)
        + lax.dot_general(cot_next, matrix(w_two, DOWN_IN + 0, 4), NT, preferred_element_type=F32)
    ).reshape(half, width, C)
    br[...] = (
        jnp.dot(x_ref[...].reshape(rows, CI), matrix(w_two, SECOND_N, RES_N), preferred_element_type=F32) + small_ref[8:9]
    ).reshape(frames, width, C)
    total = jnp.dot(hp[0:frames].reshape(rows, C), matrix(w_two, 0, 4), preferred_element_type=F32)
    for a in range(1, KW):
        total = total + jnp.dot(
            hp[a : a + frames].reshape(rows, C), matrix(w_two, 4 * a, 4), preferred_element_type=F32
        )
    sec[...] = (total + small_ref[5:6]).reshape(frames, width, C)

    lens = lens_ref[...]
    inv = inv_ref[...]
    zero = jnp.zeros((width, 128), F32)
    for q in range(C // 128):
        ls = lanes(q)
        total = zero
        for t in range(frames):
            total = total + jnp.where(lens > t, sec[t, :, ls], 0.0)
        mean = group_sum(total) * inv
        total = zero
        for t in range(frames):
            centered = sec[t, :, ls] - mean
            total = total + jnp.where(lens > t, centered * centered, 0.0)
        rstd = lax.rsqrt(group_sum(total) * inv + 1e-05)
        gain, bias = small_ref[6:7, ls], small_ref[7:8, ls]
        sum_dy, sum_dyn, sum_ds = zero, zero, zero
        for t in range(frames):
            normed = (sec[t, :, ls] - mean) * rstd
            sec[t, :, ls] = normed
            act, slope = mish_both(normed * gain + bias)
            skip = (act + br[t, :, ls]).astype(BF)
            skip_ref[t, :, ls] = skip
            if t % 2:
                so[t // 2 + 1, :, ls] = skip
                back = dod[t // 2, :, ls]
            else:
                se[t // 2, :, ls] = skip
                back = dev[t // 2, :, ls]
            ds = (cs_ref[t, :, ls].astype(F32) + back).astype(BF)
            dskip_ref[t, :, ls] = ds
            ds = ds.astype(F32)
            sum_ds = sum_ds + ds
            dy = ds * slope
            br[t, :, ls] = dy
            sum_dy = sum_dy + dy
            sum_dyn = sum_dyn + dy * normed
        mean_a = group_sum(sum_dy * gain) * inv
        mean_an = group_sum(sum_dyn * gain) * inv
        sum_g, sum_cd = zero, zero
        for t in range(frames):
            normed = sec[t, :, ls]
            grad = rstd * (br[t, :, ls] * gain - jnp.where(lens > t, mean_a + normed * mean_an, 0.0))
            grad = grad.astype(BF)
            g2_ref[t, :, ls] = grad
            sum_g = sum_g + grad.astype(F32)
        for t in range(half):
            sum_cd = sum_cd + cd_ref[t, :, ls].astype(F32)
        for k, part in enumerate((sum_g, sum_dyn, sum_dy, sum_ds, sum_cd)):
            gs_ref[k : k + 1, ls] += jnp.sum(part, axis=0, keepdims=True)

    grad_two = g2_ref[...].reshape(rows, C)
    for a in range(KW):
        acc[a * C : (a + 1) * C] += lax.dot_general(
            hp[a : a + frames].reshape(rows, C), grad_two, TN, preferred_element_type=F32
        )
    at = KW * C
    acc[at : at + CI] += lax.dot_general(
        x_ref[...].reshape(rows, CI), dskip_ref[...].reshape(rows, C), TN, preferred_element_type=F32
    )
    at = at + CI
    for a, source in enumerate((so.at[0:half], se, so.at[1 : half + 1])):
        acc[at + a * C : at + (a + 1) * C] += lax.dot_general(
            source[...].reshape(half * width, C), cot, TN, preferred_element_type=F32
        )

    @pl.when(step == last)
    def _():
        store_pieces((me[0], me[1]), acc, (ga, gb, gc, gd))
        pltpu.make_async_copy(w_two, w_out, sem.at[1]).wait()


def third_kernel(me, w_hbm, g2_ref, x_ref, cond_ref, normed_ref, rstd_ref, mod_ref, lens_ref, inv_ref, small_ref,
                 g1_ref, dmod_ref, ga, gb, gc, gd, gs_ref, w_two, gp, xp, dh, acc, sem):
    step = pl.program_id(0)
    last = pl.num_programs(0) - 1
    frames, width, _ = x_ref.shape
    rows = frames * width

    @pl.when(step == 0)
    def _():
        arrival = pltpu.make_async_copy(w_hbm.at[0:SECOND_N], w_two, sem.at[0])
        arrival.start()
        gp[0:2] = jnp.zeros((2, width, C), BF)
        gp[frames + 2 :] = jnp.zeros((2, width, C), BF)
        xp[0:2] = jnp.zeros((2, width, CI), BF)
        xp[frames + 2 :] = jnp.zeros((2, width, CI), BF)
        acc[...] = jnp.zeros_like(acc)
        gs_ref[...] = jnp.zeros_like(gs_ref)
        arrival.wait()

    gp[2 : frames + 2] = g2_ref[...]
    xp[2 : frames + 2] = x_ref[...]
    total = lax.dot_general(gp[4 : 4 + frames].reshape(rows, C), matrix(w_two, 0, 4), NT, preferred_element_type=F32)
    for a in range(1, KW):
        total = total + lax.dot_general(
            gp[4 - a : 4 - a + frames].reshape(rows, C), matrix(w_two, 4 * a, 4), NT, preferred_element_type=F32
        )
    dh[...] = total.reshape(frames, width, C)

    here = pl.ds(pl.multiple_of(step * width, width), width)
    lens = lens_ref[...]
    inv = inv_ref[...]
    zero = jnp.zeros((width, 128), F32)
    for q in range(C // 128):
        ls = lanes(q)
        gain, bias = small_ref[1:2, ls], small_ref[2:3, ls]
        scale = mod_ref[0, here, ls]
        sum_dy, sum_dyn, d_scale, d_shift = zero, zero, zero, zero
        for t in range(frames):
            normed = normed_ref[t, :, ls]
            act, slope = mish_both(normed * gain + bias)
            grad = jnp.where(lens > t, dh[t, :, ls], 0.0)
            d_scale = d_scale + grad * act
            d_shift = d_shift + grad
            dy = (grad * scale) * slope
            dh[t, :, ls] = dy
            sum_dy = sum_dy + dy
            sum_dyn = sum_dyn + dy * normed
        mean_a = group_sum(sum_dy * gain) * inv
        mean_an = group_sum(sum_dyn * gain) * inv
        rstd = rstd_ref[:, ls]
        sum_g = zero
        for t in range(frames):
            normed = normed_ref[t, :, ls]
            grad = rstd * (dh[t, :, ls] * gain - jnp.where(lens > t, mean_a + normed * mean_an, 0.0))
            grad = grad.astype(BF)
            g1_ref[t, :, ls] = grad
            sum_g = sum_g + grad.astype(F32)
        d_scale, d_shift = d_scale.astype(BF), d_shift.astype(BF)
        dmod_ref[0, here, ls] = d_scale
        dmod_ref[1, here, ls] = d_shift
        for k, part in enumerate((sum_g, sum_dyn, sum_dy, d_scale.astype(F32), d_shift.astype(F32))):
            gs_ref[k : k + 1, ls] += jnp.sum(part, axis=0, keepdims=True)

    grad_one = g1_ref[...].reshape(rows, C)
    for a in range(KW):
        acc[a * CI : (a + 1) * CI] += lax.dot_general(
            xp[a : a + frames].reshape(rows, CI), grad_one, TN, preferred_element_type=F32
        )

    @pl.when(step == last)
    def _():
        for k in range(2):
            at = KW * CI + k * COND
            acc[at : at + COND] = lax.dot_general(cond_ref[...], dmod_ref[k], TN, preferred_element_type=F32)
        store_pieces((me[0], me[1]), acc, (ga, gb, gc, gd))


def fourth_kernel(w_early, w_late, skip_ref, g1_ref, dskip_ref, dmod_ref, slope_ref, lens_ref, small_ref, down_ref, dx_ref,
                  dobs_ref, w_one, w_two, gp, se, so, sem):
    step = pl.program_id(0)
    frames, width, _ = skip_ref.shape
    half = frames // 2
    rows = frames * width

    @pl.when(step == 0)
    def _():
        early = pltpu.make_async_copy(w_early, w_one, sem.at[0])
        late = pltpu.make_async_copy(w_late.at[SECOND_N:LATE_N], w_two, sem.at[1])
        early.start()
        late.start()
        gp[0:2] = jnp.zeros((2, width, C), BF)
        gp[frames + 2 :] = jnp.zeros((2, width, C), BF)
        so[0:1] = jnp.zeros((1, width, C), BF)
        early.wait()
        back = lax.dot_general(dmod_ref[0], matrix(w_one, FIRST_N + 1, FILM_N - 1), NT, preferred_element_type=F32)
        back = back + lax.dot_general(
            dmod_ref[1], matrix(w_one, FIRST_N + FILM_N + 1, FILM_N - 1), NT, preferred_element_type=F32
        )
        dobs_ref[...] = back * slope_ref[...]
        late.wait()

    gp[2 : frames + 2] = g1_ref[...]
    total = lax.dot_general(dskip_ref[...].reshape(rows, C), matrix(w_two, 0, RES_N), NT, preferred_element_type=F32)
    for a in range(KW):
        total = total + lax.dot_general(
            gp[4 - a : 4 - a + frames].reshape(rows, C), matrix(w_one, 2 * a, 2), NT, preferred_element_type=F32
        )
    total = total.reshape(frames, width, CI)
    lens = lens_ref[...]
    for t in range(frames):
        for q in range(CI // 128):
            dx_ref[t, :, lanes(q)] = jnp.where(lens > t, total[t, :, lanes(q)], 0.0)
    for j in range(half):
        se[j] = skip_ref[2 * j]
        so[j + 1] = skip_ref[2 * j + 1]
    down = jnp.dot(so[0:half].reshape(half * width, C), matrix(w_two, RES_N + 0, 4), preferred_element_type=F32)
    down = down + jnp.dot(se[...].reshape(half * width, C), matrix(w_two, RES_N + 4, 4), preferred_element_type=F32)
    down = down + jnp.dot(
        so[1 : half + 1].reshape(half * width, C), matrix(w_two, RES_N + 8, 4), preferred_element_type=F32
    )
    down_ref[...] = (down + small_ref[9:10]).astype(BF).reshape(half, width, C)


def adamw_kernel(me, used, own_ref, recv_ref, master_ref, one_ref, two_ref, one_out, two_out, master_out, grad):
    for slot in range(grad.shape[0]):
        keep = used[pl.program_id(0) * grad.shape[0] + slot] > 0
        for core, source in enumerate((own_ref, recv_ref)):
            for x in range(2):
                cols = pl.ds(pl.multiple_of((me[1] ^ (x * 2 + core)) * 128, 128), 128)
                for row in range(8):
                    piece = source[x, row, slot].astype(F32)
                    grad[slot, row * 16 : row * 16 + 16, cols] = jnp.where(keep, piece, 0.0)
    one_out[...], two_out[...], master_out[...] = adamw(
        master_ref[...], one_ref[...], two_ref[...], grad[...], RATE_MATRIX
    )


def tiles(frames, width, channels):
    return pl.BlockSpec((frames, width, channels), lambda i, *_: (0, i, 0))


def rows_of(width, channels):
    return pl.BlockSpec((width, channels), lambda i, *_: (i, 0))


def whole(*shape):
    return pl.BlockSpec(shape, lambda i, *_: (0,) * len(shape))


ANY = pl.BlockSpec(memory_space=pl.ANY)
PARAMS = pltpu.CompilerParams(vmem_limit_bytes=VMEM_LIMIT, dimension_semantics=("arbitrary",))


def weight_scratch(count):
    return pltpu.VMEM((count, 8, 16, C), BF)


def shape(*dims, dtype=F32):
    return jax.ShapeDtypeStruct(dims, dtype)


def half_lists(count):
    front = count // 2
    return [(16, n, 16, 128) for n in (front, front, count - front, count - front)]


def call(kernel, name, grid, scalars, ins, outs, scratch, operands, flops):
    return pl.pallas_call(
        kernel,
        grid_spec=pltpu.PrefetchScalarGridSpec(
            num_scalar_prefetch=scalars,
            grid=grid,
            in_specs=ins,
            out_specs=[spec for spec, _ in outs],
            scratch_shapes=scratch,
        ),
        out_shape=[made for _, made in outs],
        compiler_params=PARAMS,
        cost_estimate=pl.CostEstimate(flops=flops, bytes_accessed=20 * 2**20, transcendentals=0),
        name=name,
    )(*operands)


def run_first(me, pieces, x, cond, lens, inv, small, width):
    count = x.shape[1]
    return call(
        first_kernel, "first", (count // width,), 1,
        [ANY] * 4 + [tiles(H, width, CI), whole(count, COND), rows_of(width, 128), rows_of(width, 128),
                     whole(NSMALL, C)],
        [(tiles(H, width, C), shape(H, count, C)), (rows_of(width, C), shape(count, C)),
         (tiles(H, width, C), shape(H, count, C, dtype=BF)), (whole(2, count, C), shape(2, count, C)),
         (ANY, shape(EARLY_N, 8, 16, C, dtype=BF))],
        [weight_scratch(EARLY_N), pltpu.VMEM((H + 4, width, CI), BF), pltpu.VMEM((H, width, C), F32),
         pltpu.SemaphoreType.DMA((2,))],
        (me, *pieces, x, cond, lens, inv, small),
        2 * count * H * KW * CI * C,
    )


def run_second(me, pieces, hid, x, cs, cd, lens, inv, small, width):
    count = x.shape[1]
    bf_tile = (tiles(H, width, C), shape(H, count, C, dtype=BF))
    return call(
        second_kernel, "second", (count // width,), 1,
        [ANY] * 4 + [tiles(H, width, C), tiles(H, width, CI), tiles(H, width, C), tiles(HD, width, C),
                     rows_of(width, 128), rows_of(width, 128), whole(NSMALL, C)],
        [bf_tile, bf_tile, bf_tile] + [(whole(*dims), shape(*dims, dtype=BF)) for dims in half_lists(LATE_N)]
        + [(whole(8, C), shape(8, C)), (ANY, shape(LATE_N, 8, 16, C, dtype=BF))],
        [weight_scratch(LATE_N), pltpu.VMEM((H + 4, width, C), BF), pltpu.VMEM((HD + 1, width, C), BF),
         pltpu.VMEM((H, width, C), F32), pltpu.VMEM((H, width, C), F32),
         pltpu.VMEM((HD, width, C), F32), pltpu.VMEM((HD, width, C), F32),
         pltpu.VMEM((HD, width, C), BF), pltpu.VMEM((HD + 1, width, C), BF),
         pltpu.VMEM((LATE_N * BLK, C), F32), pltpu.SemaphoreType.DMA((2,))],
        (me, *pieces, hid, x, cs, cd, lens, inv, small),
        6 * count * H * KW * C * C,
    )


def run_third(me, w_late, g2, x, cond, normed, rstd, mod, lens, inv, small, width):
    count = x.shape[1]
    return call(
        third_kernel, "third", (count // width,), 1,
        [ANY, tiles(H, width, C), tiles(H, width, CI), whole(count, COND), tiles(H, width, C),
         rows_of(width, C), whole(2, count, C), rows_of(width, 128), rows_of(width, 128), whole(NSMALL, C)],
        [(tiles(H, width, C), shape(H, count, C, dtype=BF)), (whole(2, count, C), shape(2, count, C, dtype=BF))]
        + [(whole(*dims), shape(*dims, dtype=BF)) for dims in half_lists(EARLY_N)] + [(whole(8, C), shape(8, C))],
        [weight_scratch(SECOND_N), pltpu.VMEM((H + 4, width, C), BF),
         pltpu.VMEM((H + 4, width, CI), BF), pltpu.VMEM((H, width, C), F32),
         pltpu.VMEM((EARLY_N * BLK, C), F32), pltpu.SemaphoreType.DMA((1,))],
        (me, w_late, g2, x, cond, normed, rstd, mod, lens, inv, small),
        4 * count * H * KW * C * C,
    )


def run_fourth(w_early, w_late, skip, g1, dskip, dmod, slope, lens, small, width):
    count = skip.shape[1]
    features = slope.shape[1]
    return call(
        fourth_kernel, "fourth", (count // width,), 0,
        [ANY, ANY, tiles(H, width, C), tiles(H, width, C), tiles(H, width, C), whole(2, count, C),
         whole(count, features), rows_of(width, 128), whole(NSMALL, C)],
        [(tiles(HD, width, C), shape(HD, count, C, dtype=BF)), (tiles(H, width, CI), shape(H, count, CI)),
         (whole(count, features), shape(count, features))],
        [weight_scratch(EARLY_N), weight_scratch(RES_N + DOWN_N), pltpu.VMEM((H + 4, width, C), BF),
         pltpu.VMEM((HD, width, C), BF), pltpu.VMEM((HD + 1, width, C), BF), pltpu.SemaphoreType.DMA((2,))],
        (w_early, w_late, skip, g1, dskip, dmod, slope, lens, small),
        2 * count * H * KW * C * C,
    )


def run_adamw(me, used, own, recv, master, one, two):
    slots = master.shape[0]
    group = 2
    block = pl.BlockSpec((group, BLK, C), lambda i, *_: (i, 0, 0))
    piece = pl.BlockSpec((2, 8, group, 16, 128), lambda i, *_: (0, 0, i, 0, 0))
    return call(
        adamw_kernel, "adamw", (slots // group,), 2,
        [piece, piece, block, block, block],
        [(block, shape(slots, BLK, C))] * 3,
        [pltpu.VMEM((group, BLK, C), F32)],
        (me, used, own, recv, master, one, two),
        20 * slots * BLK * C,
    )


def prepare(actions, shared, tsteps, lengths, cot_skip, cot_down):
    micro, samp = lengths.shape
    count = micro * samp
    lens_flat = lengths.reshape(count)
    lens = jnp.broadcast_to(lens_flat.astype(F32)[:, None], (count, 128))
    inv = 1.0 / (lens * GC)
    keep = jnp.arange(H)[:, None, None] < lens_flat[None, :, None]
    x = jnp.where(keep, actions.reshape(count, H, CI).transpose(1, 0, 2), jnp.zeros((), BF))
    cs = cot_skip.reshape(count, H, C).transpose(1, 0, 2)
    cd = cot_down.reshape(count, HD, C).transpose(1, 0, 2)
    obs = shared.reshape(count, -1).astype(F32)
    obs_act, obs_back = jax.vjp(mish, obs)
    slope = obs_back(jnp.ones_like(obs))[0]
    cond = jnp.concatenate([mish(time_embed(tsteps.reshape(count), TE)), obs_act], axis=1).astype(BF)
    return x, cs, cd, lens, inv, cond, slope


def flip(value, axis, bit):
    size = lax.axis_size(axis)
    return lax.ppermute(value, axis, [(i, i ^ bit) for i in range(size)])


def core(value):
    return flip(value, "pair", 1)


def along_x(value):
    return flip(value, "pair", 2)


def along_y(value):
    return flip(value, "dp", 1)


def z_low(value):
    return flip(value, "dp", 2)


def z_high(value):
    return flip(value, "dp", 4)


def pieces_of(block):
    return block.reshape(-1, 8, 16, 4, 128).transpose(1, 3, 0, 2, 4)


def double(value, hop):
    return jnp.concatenate([value, hop(value)], axis=0)


def gather_list(mine):
    value = double(double(mine[None], z_high), z_low)
    front = mine.shape[0] // 2
    a, b = value[:, :front], value[:, front:]
    a = double(double(a, along_y), along_x)
    b = double(double(b, along_x), along_y)
    return a, core(a), b, core(b)


def halve(value, hop):
    size = value.shape[0] // 2
    return value[:size] + hop(value[size:])


def reduce_list(lists):
    a_own, a_other, b_own, b_other = lists
    a = a_own + core(a_other)
    b = b_own + core(b_other)
    a = halve(halve(a, along_x), along_y)
    b = halve(halve(b, along_y), along_x)
    value = jnp.concatenate([a, b], axis=1)
    return halve(halve(value, z_low), z_high)[0]


def sum_all(value):
    for axis in ("pair", "dp"):
        bit = 1
        while bit < lax.axis_size(axis):
            value = value + flip(value, axis, bit)
            bit = bit * 2
    return value


def split_order(blocks):
    return jnp.concatenate([blocks[:FIRST_N], blocks[FIRST_N + LATE_N :]], axis=0), blocks[FIRST_N : FIRST_N + LATE_N]


def join_order(early, late):
    return jnp.concatenate([early[:FIRST_N], late, early[FIRST_N:]], axis=0)


def as_lists(blocks):
    front = blocks.shape[0] // 2
    found = []
    for by_y_first, part in ((False, blocks[:front]), (True, blocks[front:])):
        cut = pieces_of(part)
        for core_bit in range(2):
            found.append(jnp.stack([cut[place((0, 0), k, by_y_first, core_bit)] for k in range(16)]))
    return tuple(found)


def from_lists(lists):
    parts = []
    for by_y_first, pair in ((False, lists[:2]), (True, lists[2:])):
        table = {}
        for core_bit, part in enumerate(pair):
            for k in range(16):
                table[place((0, 0), k, by_y_first, core_bit)] = part[k]
        cut = jnp.stack([jnp.stack([table[(row, col)] for col in range(4)]) for row in range(8)])
        parts.append(cut.transpose(2, 0, 3, 1, 4).reshape(-1, BLK, C))
    return jnp.concatenate(parts, axis=0)


def body(
    actions,
    observations,
    tsteps,
    lengths,
    cot_skip,
    cot_down,
    owners,
    master,
    moment_one,
    moment_two,
    small_master,
    small_one,
    small_two,
):
    micro, samp = lengths.shape
    slot_count = master.shape[0]
    dp_count = lax.axis_size("dp")
    slots_all = dp_count * slot_count
    me_pair = lax.axis_index("pair")
    me_dp = lax.axis_index("dp")
    by_pieces = dp_count == 8 and lax.axis_size("pair") == 4
    slot_index = slot_of(owners, slot_count)
    block_of = (
        jnp.full((slots_all,), -1, jnp.int32).at[slot_index].set(jnp.arange(NBLK, dtype=jnp.int32))
    )
    used = (lax.dynamic_slice_in_dim(block_of, me_dp * slot_count, slot_count, axis=0) >= 0).astype(jnp.int32)
    here = jnp.stack([me_dp, me_pair]).astype(jnp.int32)
    if by_pieces:
        me = here
        columns = lax.dynamic_slice_in_dim(master, me_pair * 128, 128, axis=2).astype(BF)
        columns = columns.reshape(slot_count, 8, 16, 128).transpose(1, 0, 2, 3)
        slots = lax.all_to_all(columns, "dp", 0, 0).reshape(slots_all, 16, 128)
        early_index, late_index = split_order(slot_index)
        early_lists = gather_list(jnp.take(slots, early_index, axis=0))
        late_lists = gather_list(jnp.take(slots, late_index, axis=0))
    else:
        me = jnp.zeros_like(here)
        quarter = lax.dynamic_slice_in_dim(master, me_pair * 32, 32, axis=1).astype(BF)
        slots = lax.all_gather(quarter, "dp", axis=0, tiled=True)
        mine = jnp.take(slots, slot_index, axis=0)
        early, late = split_order(lax.all_gather(mine, "pair", axis=1, tiled=True))
        early_lists, late_lists = as_lists(early), as_lists(late)
    shared = lax.all_gather(observations, "pair", axis=2, tiled=True)

    x, cs, cd, lens, inv, cond, slope = prepare(actions, shared, tsteps, lengths, cot_skip, cot_down)
    width = samp
    normed, rstd, hid, mod, w_early = run_first(me, early_lists, x, cond, lens, inv, small_master, width)
    skip, dskip, g2, *late_grads, gs_late, w_late = run_second(
        me, late_lists, hid, x, cs, cd, lens, inv, small_master, width
    )
    g1, dmod, *early_grads, gs_early = run_third(
        me, w_late, g2, x, cond, normed, rstd, mod, lens, inv, small_master, width
    )
    down, dx, dobs = run_fourth(w_early, w_late, skip, g1, dskip, dmod, slope, lens, small_master, width)
    skip_out = skip.transpose(1, 0, 2).reshape(micro, samp, H, C)
    down_out = down.transpose(1, 0, 2).reshape(micro, samp, HD, C)
    actions_grad = dx.transpose(1, 0, 2).reshape(micro, samp, H, CI)
    g_small = jnp.concatenate([gs_early[0:5], gs_late[0:5]], axis=0)
    grad_small = sum_all(g_small)
    observations_grad = lax.psum_scatter(
        dobs.reshape(micro, samp, -1), "pair", scatter_dimension=2, tiled=True
    )

    if by_pieces:
        grads = join_order(reduce_list(early_grads), reduce_list(late_grads))
        spread = jnp.take(grads, jnp.maximum(block_of, 0), axis=0).reshape(dp_count, slot_count, 16, 128)
        owned = lax.all_to_all(spread, "dp", 0, 0)
        own = jnp.stack([owned, along_x(owned)])
        recv = core(own)
    else:
        grads = join_order(from_lists(early_grads), from_lists(late_grads))
        rows = grads.reshape(-1, 4, 32, C).transpose(1, 0, 2, 3)
        rows = lax.psum_scatter(rows, "pair", scatter_dimension=0)
        spread = jnp.take(rows, jnp.maximum(block_of, 0), axis=0)
        owned = lax.psum_scatter(spread, "dp", scatter_dimension=0, tiled=True)
        owned = lax.all_gather(owned, "pair", axis=1, tiled=True)
        cut = pieces_of(owned)
        own = jnp.stack([cut[:, 0], cut[:, 2]])
        recv = jnp.stack([cut[:, 1], cut[:, 3]])
    new_one, new_two, new_master = run_adamw(me, used, own, recv, master, moment_one, moment_two)
    small_first, small_second, new_small = adamw(
        small_master, small_one, small_two, grad_small, RATE_SMALL
    )
    return (
        skip_out,
        down_out,
        actions_grad,
        observations_grad,
        new_one,
        new_two,
        new_master,
        small_first,
        small_second,
        new_small,
    )


def solution(mesh):
    placed = (
        P(None, ("dp", "pair"), None, None),
        P(None, "dp", "pair"),
        P(None, ("dp", "pair")),
        P(None, ("dp", "pair")),
        P(None, ("dp", "pair"), None, None),
        P(None, ("dp", "pair"), None, None),
        P(),
        P("dp", None, None),
        P("dp", None, None),
        P("dp", None, None),
        P(),
        P(),
        P(),
    )
    return jax.shard_map(
        body,
        mesh=mesh,
        in_specs=placed,
        out_specs=(
            P(None, ("dp", "pair"), None, None),
            P(None, ("dp", "pair"), None, None),
            P(None, ("dp", "pair"), None, None),
            P(None, "dp", "pair"),
            P("dp", None, None),
            P("dp", None, None),
            P("dp", None, None),
            P(),
            P(),
            P(),
        ),
        check_vma=False,
    )
```

```python
import functools
import math

import jax
import jax.numpy as jnp
from jax import lax
from jax.experimental.layout import Layout, with_layout_constraint
from jax.experimental import pallas as pl
from jax.experimental.pallas import tpu as pltpu
from jax.sharding import PartitionSpec as P

CI = 256
C = 512
TE = 128
KW = 5
H = 16
HD = 8
KD = 3
NSMALL = 10
STEP = 10
BLK = 128
COND = 1152
NBLK = 62
GC = 64

FIRST_N, SECOND_N, RES_N, DOWN_N, FILM_N = 10, 20, 2, 12, 9
EARLY_N = FIRST_N + 2 * FILM_N
LATE_N = SECOND_N + RES_N + DOWN_N
DOWN_IN = SECOND_N + RES_N
PIECES = 32

BETA_ONE = 0.9
BETA_TWO = 0.999
EPS_ADAM = 1e-08
DECAY = 0.01
RATE_MATRIX = 0.1
RATE_SMALL = 1.0

F32 = jnp.float32
BF = jnp.bfloat16
NT = (((1,), (1,)), ((), ()))
TN = (((0,), (0,)), ((), ()))
VMEM_LIMIT = 56 * 2**20


def mish(value):
    return value * jnp.tanh(jax.nn.softplus(value))


def time_embed(step_ids, width):
    half = width // 2
    freq = jnp.exp(-math.log(10000.0) * jnp.arange(half, dtype=F32) / (half - 1))
    angle = step_ids.astype(F32)[:, None] * freq[None, :]
    return jnp.concatenate([jnp.sin(angle), jnp.cos(angle)], axis=1)


def slot_of(owners, slot_count):
    same = owners[:, None] == owners[None, :]
    order = jnp.arange(owners.shape[0], dtype=jnp.int32)
    earlier = order[:, None] > order[None, :]
    rank = jnp.sum((same & earlier).astype(jnp.int32), axis=1)
    return owners * slot_count + rank


def adamw(weight, first_m, second_m, grad, rate):
    first_new = BETA_ONE * first_m + (1.0 - BETA_ONE) * grad
    second_new = BETA_TWO * second_m + (1.0 - BETA_TWO) * grad * grad
    fix_one = 1.0 - BETA_ONE**STEP
    fix_two = 1.0 - BETA_TWO**STEP
    update = first_new / fix_one / (jnp.sqrt(second_new / fix_two) + EPS_ADAM) + DECAY * weight
    return (first_new, second_new, weight - rate * update)


def recip(value):
    r = pl.reciprocal(value, approx=True)
    return r * (2.0 - value * r)


def mish_parts(v):
    w = jnp.exp(jnp.minimum(v, 30.0))
    n = w * (w + 2.0)
    r = recip(n + 2.0)
    return w, n * r, r


def mish_only(v):
    _, t, _ = mish_parts(v)
    return v * t


def mish_both(v):
    w, t, r = mish_parts(v)
    return v * t, t + (4.0 * v) * (((w * (1.0 + w)) * r) * r)


def group_sum(value):
    low_half = lax.broadcasted_iota(jnp.int32, value.shape, 1) < GC
    zero = jnp.zeros_like(value)
    left = jnp.sum(jnp.where(low_half, value, zero), axis=1, keepdims=True)
    right = jnp.sum(jnp.where(low_half, zero, value), axis=1, keepdims=True)
    return jnp.where(low_half, left, right)


def lanes(q):
    return slice(q * 128, (q + 1) * 128)


def flips_of(k):
    return (k >> 3) & 1, (k >> 2) & 1, (k >> 1) & 1, k & 1


def place(me, k, by_y_first, core):
    one, two, z_low, z_high = flips_of(k)
    y, x = (one, two) if by_y_first else (two, one)
    return me[0] ^ (z_high * 4 + z_low * 2 + y), me[1] ^ (x * 2 + core)


def fetch(me, sources, dst, sem):
    at = 0
    for by_y_first, pair in ((False, sources[:2]), (True, sources[2:])):
        count = pair[0].shape[1]
        for core, source in enumerate(pair):
            for k in range(16):
                row, col = place(me, k, by_y_first, core)
                pltpu.make_async_copy(
                    source.at[k],
                    dst.at[at : at + count, row, :, pl.ds(pl.multiple_of(col * 128, 128), 128)],
                    sem,
                ).start()
        at = at + count
    return pltpu.make_async_copy(dst, dst, sem)


def store_pieces(me, acc, outs, base=0):
    at = 0
    for by_y_first, pair in ((False, outs[:2]), (True, outs[2:])):
        count = pair[0].shape[1]

        def one_block(b, carry, at=at, by_y_first=by_y_first, pair=pair):
            for core, out in enumerate(pair):
                for k in range(16):
                    row, col = place(me, k, by_y_first, core)
                    rows = pl.ds(pl.multiple_of((at + b) * BLK + row * 16, 16), 16)
                    cols = pl.ds(pl.multiple_of(col * 128, 128), 128)
                    out[k, b] = acc[rows, cols].astype(BF)
            return carry

        lax.fori_loop(0, count, one_block, 0)
        at = at + count


def matrix(ref, at, count):
    return ref[at : at + count].reshape(count * BLK, C)


def first_kernel(me, pa, pb, pc, pd, x_ref, cond_ref, lens_ref, inv_ref, small_ref, normed_ref, rstd_ref, hid_ref,
                 mod_ref, w_out, w_one, xp, fst, sem):
    step = pl.program_id(0)
    frames, width, _ = x_ref.shape
    rows = frames * width

    @pl.when(step == 0)
    def _():
        arrival = fetch((me[0], me[1]), (pa, pb, pc, pd), w_one, sem.at[0])
        xp[0:2] = jnp.zeros((2, width, CI), BF)
        xp[frames + 2 :] = jnp.zeros((2, width, CI), BF)
        arrival.wait()
        pltpu.make_async_copy(w_one, w_out, sem.at[1]).start()
        for k in range(2):
            mod_ref[k] = (
                jnp.dot(cond_ref[...], matrix(w_one, FIRST_N + k * FILM_N, FILM_N), preferred_element_type=F32)
                + small_ref[3 + k : 4 + k]
            )

    xp[2 : frames + 2] = x_ref[...]
    acc = jnp.dot(xp[0:frames].reshape(rows, CI), matrix(w_one, 0, 2), preferred_element_type=F32)
    for a in range(1, KW):
        acc = acc + jnp.dot(
            xp[a : a + frames].reshape(rows, CI), matrix(w_one, 2 * a, 2), preferred_element_type=F32
        )
    fst[...] = (acc + small_ref[0:1]).reshape(frames, width, C)

    here = pl.ds(pl.multiple_of(step * width, width), width)
    lens = lens_ref[...]
    inv = inv_ref[...]
    for q in range(C // 128):
        ls = lanes(q)
        total = jnp.zeros((width, 128), F32)
        for t in range(frames):
            total = total + jnp.where(lens > t, fst[t, :, ls], 0.0)
        mean = group_sum(total) * inv
        total = jnp.zeros((width, 128), F32)
        for t in range(frames):
            centered = fst[t, :, ls] - mean
            total = total + jnp.where(lens > t, centered * centered, 0.0)
        rstd = lax.rsqrt(group_sum(total) * inv + 1e-05)
        rstd_ref[:, ls] = rstd
        gain, bias = small_ref[1:2, ls], small_ref[2:3, ls]
        scale, shift = mod_ref[0, here, ls], mod_ref[1, here, ls]
        for t in range(frames):
            normed = (fst[t, :, ls] - mean) * rstd
            normed_ref[t, :, ls] = normed
            value = scale * mish_only(normed * gain + bias) + shift
            hid_ref[t, :, ls] = jnp.where(lens > t, value, 0.0).astype(BF)

    @pl.when(step == pl.num_programs(0) - 1)
    def _():
        pltpu.make_async_copy(w_one, w_out, sem.at[1]).wait()


def second_kernel(me, pa, pb, pc, pd, hid_ref, x_ref, cs_ref, cd_ref, lens_ref, inv_ref, small_ref, skip_ref,
                  dskip_ref, g2_ref, ga, gb, gc, gd, gs_ref, w_out, w_two, hp, cdp, sec, br, dev, dod, se, so, acc,
                  sem):
    step = pl.program_id(0)
    last = pl.num_programs(0) - 1
    frames, width, _ = x_ref.shape
    half = frames // 2
    rows = frames * width

    @pl.when(step == 0)
    def _():
        arrival = fetch((me[0], me[1]), (pa, pb, pc, pd), w_two, sem.at[0])
        hp[0:2] = jnp.zeros((2, width, C), BF)
        hp[frames + 2 :] = jnp.zeros((2, width, C), BF)
        cdp[half:] = jnp.zeros((1, width, C), BF)
        so[0:1] = jnp.zeros((1, width, C), BF)
        acc[...] = jnp.zeros_like(acc)
        gs_ref[...] = jnp.zeros_like(gs_ref)
        arrival.wait()
        pltpu.make_async_copy(w_two, w_out, sem.at[1]).start()

    hp[2 : frames + 2] = hid_ref[...]
    cdp[0:half] = cd_ref[...]
    cot = cdp[0:half].reshape(half * width, C)
    cot_next = cdp[1 : half + 1].reshape(half * width, C)
    dev[...] = lax.dot_general(cot, matrix(w_two, DOWN_IN + 4, 4), NT, preferred_element_type=F32).reshape(half, width, C)
    dod[...] = (
        lax.dot_general(cot, matrix(w_two, DOWN_IN + 8, 4), NT, preferred_element_type=F32)
        + lax.dot_general(cot_next, matrix(w_two, DOWN_IN + 0, 4), NT, preferred_element_type=F32)
    ).reshape(half, width, C)
    br[...] = (
        jnp.dot(x_ref[...].reshape(rows, CI), matrix(w_two, SECOND_N, RES_N), preferred_element_type=F32) + small_ref[8:9]
    ).reshape(frames, width, C)
    total = jnp.dot(hp[0:frames].reshape(rows, C), matrix(w_two, 0, 4), preferred_element_type=F32)
    for a in range(1, KW):
        total = total + jnp.dot(
            hp[a : a + frames].reshape(rows, C), matrix(w_two, 4 * a, 4), preferred_element_type=F32
        )
    sec[...] = (total + small_ref[5:6]).reshape(frames, width, C)

    lens = lens_ref[...]
    inv = inv_ref[...]
    zero = jnp.zeros((width, 128), F32)
    for q in range(C // 128):
        ls = lanes(q)
        total = zero
        for t in range(frames):
            total = total + jnp.where(lens > t, sec[t, :, ls], 0.0)
        mean = group_sum(total) * inv
        total = zero
        for t in range(frames):
            centered = sec[t, :, ls] - mean
            total = total + jnp.where(lens > t, centered * centered, 0.0)
        rstd = lax.rsqrt(group_sum(total) * inv + 1e-05)
        gain, bias = small_ref[6:7, ls], small_ref[7:8, ls]
        sum_dy, sum_dyn, sum_ds = zero, zero, zero
        for t in range(frames):
            normed = (sec[t, :, ls] - mean) * rstd
            sec[t, :, ls] = normed
            act, slope = mish_both(normed * gain + bias)
            skip = (act + br[t, :, ls]).astype(BF)
            skip_ref[t, :, ls] = skip
            if t % 2:
                so[t // 2 + 1, :, ls] = skip
                back = dod[t // 2, :, ls]
            else:
                se[t // 2, :, ls] = skip
                back = dev[t // 2, :, ls]
            ds = (cs_ref[t, :, ls].astype(F32) + back).astype(BF)
            dskip_ref[t, :, ls] = ds
            ds = ds.astype(F32)
            sum_ds = sum_ds + ds
            dy = ds * slope
            br[t, :, ls] = dy
            sum_dy = sum_dy + dy
            sum_dyn = sum_dyn + dy * normed
        mean_a = group_sum(sum_dy * gain) * inv
        mean_an = group_sum(sum_dyn * gain) * inv
        sum_g, sum_cd = zero, zero
        for t in range(frames):
            normed = sec[t, :, ls]
            grad = rstd * (br[t, :, ls] * gain - jnp.where(lens > t, mean_a + normed * mean_an, 0.0))
            grad = grad.astype(BF)
            g2_ref[t, :, ls] = grad
            sum_g = sum_g + grad.astype(F32)
        for t in range(half):
            sum_cd = sum_cd + cd_ref[t, :, ls].astype(F32)
        for k, part in enumerate((sum_g, sum_dyn, sum_dy, sum_ds, sum_cd)):
            gs_ref[k : k + 1, ls] += jnp.sum(part, axis=0, keepdims=True)

    grad_two = g2_ref[...].reshape(rows, C)
    for a in range(KW):
        acc[a * C : (a + 1) * C] += lax.dot_general(
            hp[a : a + frames].reshape(rows, C), grad_two, TN, preferred_element_type=F32
        )
    at = KW * C
    acc[at : at + CI] += lax.dot_general(
        x_ref[...].reshape(rows, CI), dskip_ref[...].reshape(rows, C), TN, preferred_element_type=F32
    )
    at = at + CI
    for a, source in enumerate((so.at[0:half], se, so.at[1 : half + 1])):
        acc[at + a * C : at + (a + 1) * C] += lax.dot_general(
            source[...].reshape(half * width, C), cot, TN, preferred_element_type=F32
        )

    @pl.when(step == last)
    def _():
        store_pieces((me[0], me[1]), acc, (ga, gb, gc, gd))
        pltpu.make_async_copy(w_two, w_out, sem.at[1]).wait()


def third_kernel(w_hbm, g2_ref, skip_ref, normed_ref, rstd_ref, mod_ref, lens_ref, inv_ref, small_ref, g1_ref,
                 dmod_ref, down_ref, gs_ref, w_two, gp, dh, se, so, sem):
    step = pl.program_id(0)
    frames, width, _ = g2_ref.shape
    rows = frames * width
    half = frames // 2

    @pl.when(step == 0)
    def _():
        arrival = pltpu.make_async_copy(w_hbm, w_two, sem.at[0])
        arrival.start()
        gp[0:2] = jnp.zeros((2, width, C), BF)
        gp[frames + 2 :] = jnp.zeros((2, width, C), BF)
        so[0:1] = jnp.zeros((1, width, C), BF)
        gs_ref[...] = jnp.zeros_like(gs_ref)
        arrival.wait()

    gp[2 : frames + 2] = g2_ref[...]
    total = lax.dot_general(gp[4 : 4 + frames].reshape(rows, C), matrix(w_two, 0, 4), NT, preferred_element_type=F32)
    for a in range(1, KW):
        total = total + lax.dot_general(
            gp[4 - a : 4 - a + frames].reshape(rows, C), matrix(w_two, 4 * a, 4), NT, preferred_element_type=F32
        )
    dh[...] = total.reshape(frames, width, C)
    for j in range(half):
        se[j] = skip_ref[2 * j]
        so[j + 1] = skip_ref[2 * j + 1]
    down = jnp.dot(so[0:half].reshape(half * width, C), matrix(w_two, DOWN_IN, 4), preferred_element_type=F32)
    down = down + jnp.dot(
        se[...].reshape(half * width, C), matrix(w_two, DOWN_IN + 4, 4), preferred_element_type=F32
    )
    down = down + jnp.dot(
        so[1 : half + 1].reshape(half * width, C), matrix(w_two, DOWN_IN + 8, 4), preferred_element_type=F32
    )
    down_ref[...] = (down + small_ref[9:10]).astype(BF).reshape(half, width, C)

    lens = lens_ref[...]
    inv = inv_ref[...]
    zero = jnp.zeros((width, 128), F32)
    for q in range(C // 128):
        ls = lanes(q)
        gain, bias = small_ref[1:2, ls], small_ref[2:3, ls]
        scale = mod_ref[0, :, ls]
        sum_dy, sum_dyn, d_scale, d_shift = zero, zero, zero, zero
        for t in range(frames):
            normed = normed_ref[t, :, ls]
            act, slope = mish_both(normed * gain + bias)
            grad = jnp.where(lens > t, dh[t, :, ls], 0.0)
            d_scale = d_scale + grad * act
            d_shift = d_shift + grad
            dy = (grad * scale) * slope
            dh[t, :, ls] = dy
            sum_dy = sum_dy + dy
            sum_dyn = sum_dyn + dy * normed
        mean_a = group_sum(sum_dy * gain) * inv
        mean_an = group_sum(sum_dyn * gain) * inv
        rstd = rstd_ref[:, ls]
        sum_g = zero
        for t in range(frames):
            normed = normed_ref[t, :, ls]
            grad = rstd * (dh[t, :, ls] * gain - jnp.where(lens > t, mean_a + normed * mean_an, 0.0))
            grad = grad.astype(BF)
            g1_ref[t, :, ls] = grad
            sum_g = sum_g + grad.astype(F32)
        d_scale, d_shift = d_scale.astype(BF), d_shift.astype(BF)
        dmod_ref[0, :, ls] = d_scale
        dmod_ref[1, :, ls] = d_shift
        for k, part in enumerate((sum_g, sum_dyn, sum_dy, d_scale.astype(F32), d_shift.astype(F32))):
            gs_ref[k : k + 1, ls] += jnp.sum(part, axis=0, keepdims=True)


def of_halves(step, half, front, back, dst):
    @pl.when(step < half)
    def _():
        dst[...] = front[...]

    @pl.when(step >= half)
    def _():
        dst[...] = back[...]


def early_grads_kernel(me, x_ref, front_ref, back_ref, cond_ref, dmod_front, dmod_back, ga, gb, gc, gd, xp, g1, acc):
    step = pl.program_id(0)
    steps = pl.num_programs(0)
    frames, width, _ = x_ref.shape
    rows = frames * width
    near = dmod_front.shape[1]

    @pl.when(step == 0)
    def _():
        xp[0:2] = jnp.zeros((2, width, CI), BF)
        xp[frames + 2 :] = jnp.zeros((2, width, CI), BF)
        acc[0 : KW * CI] = jnp.zeros((KW * CI, C), F32)
        for k in range(2):
            at = KW * CI + k * COND
            acc[at : at + COND] = lax.dot_general(
                cond_ref[0:near], dmod_front[k], TN, preferred_element_type=F32
            ) + lax.dot_general(cond_ref[near:], dmod_back[k], TN, preferred_element_type=F32)

    xp[2 : frames + 2] = x_ref[...]
    of_halves(step, steps // 2, front_ref, back_ref, g1)
    grad_one = g1[...].reshape(rows, C)
    for a in range(KW):
        acc[a * CI : (a + 1) * CI] += lax.dot_general(
            xp[a : a + frames].reshape(rows, CI), grad_one, TN, preferred_element_type=F32
        )

    @pl.when(step == steps - 1)
    def _():
        store_pieces((me[0], me[1]), acc, (ga, gb, gc, gd))


def inputs_kernel(me, w_early, w_late, front_ref, back_ref, dskip_ref, dmod_front, dmod_back, slope_ref, lens_ref,
                  dx_ref, dobs_ref, w_one, w_res, gp, sem):
    step = pl.program_id(0)
    steps = pl.num_programs(0)
    frames, width, _ = dskip_ref.shape
    rows = frames * width
    near = dmod_front.shape[1]

    @pl.when(step == 0)
    def _():
        early = pltpu.make_async_copy(w_early, w_one, sem.at[0])
        late = pltpu.make_async_copy(w_late.at[SECOND_N:DOWN_IN], w_res, sem.at[1])
        early.start()
        late.start()
        gp[0:2] = jnp.zeros((2, width, C), BF)
        gp[frames + 2 :] = jnp.zeros((2, width, C), BF)
        early.wait()
        late.wait()
        for r in range(4):
            at = FIRST_N + 1 + 2 * (me[1] ^ r)
            for dmod, low_at, high_at in ((dmod_front, 0, near), (dmod_back, near, cond_rows(slope_ref))):
                back = lax.dot_general(
                    dmod[0], w_one[pl.ds(at, 2)].reshape(2 * BLK, C), NT, preferred_element_type=F32
                ) + lax.dot_general(
                    dmod[1], w_one[pl.ds(at + FILM_N, 2)].reshape(2 * BLK, C), NT, preferred_element_type=F32
                )
                dobs_ref[r, low_at:high_at] = back * slope_ref[r, low_at:high_at]

    of_halves(step, steps // 2, front_ref, back_ref, gp.at[2 : frames + 2])
    total = lax.dot_general(
        dskip_ref[...].reshape(rows, C), matrix(w_res, 0, RES_N), NT, preferred_element_type=F32
    )
    for a in range(KW):
        total = total + lax.dot_general(
            gp[4 - a : 4 - a + frames].reshape(rows, C), matrix(w_one, 2 * a, 2), NT, preferred_element_type=F32
        )
    total = total.reshape(frames, width, CI)
    lens = lens_ref[...]
    for t in range(frames):
        for q in range(CI // 128):
            dx_ref[t, :, lanes(q)] = jnp.where(lens > t, total[t, :, lanes(q)], 0.0)


def cond_rows(slope_ref):
    return slope_ref.shape[1]


def adamw_kernel(places, used, piece_ref, master_ref, one_ref, two_ref, *rest):
    one_out, two_out, master_out, grad = rest[-4:]
    group = grad.shape[0]
    for slot in range(group):
        keep = used[pl.program_id(1) * group + slot] > 0
        for row in range(8):
            piece = piece_ref[0, row, slot].astype(F32)
            grad[slot, row * 16 : row * 16 + 16] = jnp.where(keep, piece, 0.0)
    one_out[...], two_out[...], master_out[...] = adamw(
        master_ref[...], one_ref[...], two_ref[...], grad[...], RATE_MATRIX
    )


def tiles(frames, width, channels):
    return pl.BlockSpec((frames, width, channels), lambda i, *_: (0, i, 0))


def rows_of(width, channels):
    return pl.BlockSpec((width, channels), lambda i, *_: (i, 0))


def whole(*shape):
    return pl.BlockSpec(shape, lambda i, *_: (0,) * len(shape))


ANY = pl.BlockSpec(memory_space=pl.ANY)


def weight_scratch(count):
    return pltpu.VMEM((count, 8, 16, C), BF)


def shape(*dims, dtype=F32):
    return jax.ShapeDtypeStruct(dims, dtype)


def half_lists(count):
    front = count // 2
    return [(16, n, 16, 128) for n in (front, front, count - front, count - front)]


def call(kernel, name, grid, scalars, ins, outs, scratch, operands, flops, aliases=None):
    return pl.pallas_call(
        kernel,
        grid_spec=pltpu.PrefetchScalarGridSpec(
            num_scalar_prefetch=scalars,
            grid=grid,
            in_specs=ins,
            out_specs=[spec for spec, _ in outs],
            scratch_shapes=scratch,
        ),
        out_shape=[made for _, made in outs],
        input_output_aliases=aliases or {},
        compiler_params=pltpu.CompilerParams(
            vmem_limit_bytes=VMEM_LIMIT, dimension_semantics=("arbitrary",) * len(grid)
        ),
        cost_estimate=pl.CostEstimate(flops=flops, bytes_accessed=20 * 2**20, transcendentals=0),
        name=name,
    )(*operands)


def run_first(me, pieces, x, cond, lens, inv, small, width):
    count = x.shape[1]
    return call(
        first_kernel, "first", (count // width,), 1,
        [ANY] * 4 + [tiles(H, width, CI), whole(count, COND), rows_of(width, 128), rows_of(width, 128),
                     whole(NSMALL, C)],
        [(tiles(H, width, C), shape(H, count, C)), (rows_of(width, C), shape(count, C)),
         (tiles(H, width, C), shape(H, count, C, dtype=BF)), (whole(2, count, C), shape(2, count, C)),
         (ANY, shape(EARLY_N, 8, 16, C, dtype=BF))],
        [weight_scratch(EARLY_N), pltpu.VMEM((H + 4, width, CI), BF), pltpu.VMEM((H, width, C), F32),
         pltpu.SemaphoreType.DMA((2,))],
        (me, *pieces, x, cond, lens, inv, small),
        2 * count * H * KW * CI * C,
    )


def run_second(me, pieces, hid, x, cs, cd, lens, inv, small, width):
    count = x.shape[1]
    bf_tile = (tiles(H, width, C), shape(H, count, C, dtype=BF))
    return call(
        second_kernel, "second", (count // width,), 1,
        [ANY] * 4 + [tiles(H, width, C), tiles(H, width, CI), tiles(H, width, C), tiles(HD, width, C),
                     rows_of(width, 128), rows_of(width, 128), whole(NSMALL, C)],
        [bf_tile, bf_tile, bf_tile] + [(whole(*dims), shape(*dims, dtype=BF)) for dims in half_lists(LATE_N)]
        + [(whole(8, C), shape(8, C)), (ANY, shape(LATE_N, 8, 16, C, dtype=BF))],
        [weight_scratch(LATE_N), pltpu.VMEM((H + 4, width, C), BF), pltpu.VMEM((HD + 1, width, C), BF),
         pltpu.VMEM((H, width, C), F32), pltpu.VMEM((H, width, C), F32),
         pltpu.VMEM((HD, width, C), F32), pltpu.VMEM((HD, width, C), F32),
         pltpu.VMEM((HD, width, C), BF), pltpu.VMEM((HD + 1, width, C), BF),
         pltpu.VMEM((LATE_N * BLK, C), F32), pltpu.SemaphoreType.DMA((2,))],
        (me, *pieces, hid, x, cs, cd, lens, inv, small),
        6 * count * H * KW * C * C,
    )


def run_third(w_late, g2, skip, normed, rstd, mod, lens, inv, small, width, tiles_at, tiles_n):
    count = tiles_n * width

    def part(frames, channels):
        return pl.BlockSpec((frames, width, channels), lambda i: (0, i + tiles_at, 0))

    def part_rows(channels):
        return pl.BlockSpec((width, channels), lambda i: (i + tiles_at, 0))

    return call(
        third_kernel, "third", (tiles_n,), 0,
        [ANY, part(H, C), part(H, C), part(H, C), part_rows(C), part(2, C), part_rows(128), part_rows(128), whole(NSMALL, C)],
        [(tiles(H, width, C), shape(H, count, C, dtype=BF)), (tiles(2, width, C), shape(2, count, C, dtype=BF)),
         (tiles(HD, width, C), shape(HD, count, C, dtype=BF)), (whole(8, C), shape(8, C))],
        [weight_scratch(LATE_N), pltpu.VMEM((H + 4, width, C), BF), pltpu.VMEM((H, width, C), F32),
         pltpu.VMEM((HD, width, C), BF), pltpu.VMEM((HD + 1, width, C), BF), pltpu.SemaphoreType.DMA((1,))],
        (w_late, g2, skip, normed, rstd, mod, lens, inv, small),
        4 * count * H * KW * C * C,
    )


def front_tiles(width, channels, half):
    return pl.BlockSpec((H, width, channels), lambda i, *_: (0, jnp.minimum(i, half - 1), 0))


def back_tiles(width, channels, half):
    return pl.BlockSpec((H, width, channels), lambda i, *_: (0, jnp.maximum(i - half, 0), 0))


def run_early_grads(me, x, front, back, cond, dmod_front, dmod_back, width):
    count = x.shape[1]
    steps = count // width
    half = count // 2
    return call(
        early_grads_kernel, "early_grads", (steps,), 1,
        [tiles(H, width, CI), front_tiles(width, C, steps // 2), back_tiles(width, C, steps // 2), whole(count, COND),
         whole(2, half, C), whole(2, half, C)],
        [(whole(*dims), shape(*dims, dtype=BF)) for dims in half_lists(EARLY_N)],
        [pltpu.VMEM((H + 4, width, CI), BF), pltpu.VMEM((H, width, C), BF), pltpu.VMEM((EARLY_N * BLK, C), F32)],
        (me, x, front, back, cond, dmod_front, dmod_back),
        2 * count * H * KW * CI * C,
    )


def run_inputs(me, w_early, w_late, front, back, dskip, dmod_front, dmod_back, slope, lens, width):
    count = dskip.shape[1]
    steps = count // width
    half = count // 2
    return call(
        inputs_kernel, "inputs", (steps,), 1,
        [ANY, ANY, front_tiles(width, C, steps // 2), back_tiles(width, C, steps // 2), tiles(H, width, C),
         whole(2, half, C), whole(2, half, C), whole(*slope.shape), rows_of(width, 128)],
        [(tiles(H, width, CI), shape(H, count, CI)), (whole(*slope.shape), shape(*slope.shape))],
        [weight_scratch(EARLY_N), weight_scratch(RES_N), pltpu.VMEM((H + 4, width, C), BF),
         pltpu.SemaphoreType.DMA((2,))],
        (me, w_early, w_late, front, back, dskip, dmod_front, dmod_back, slope, lens),
        2 * count * H * (KW + 1) * CI * C,
    )


def run_adamw(places, used, pieces, master, one, two, made=None):
    slots = master.shape[0]
    group = min(slots, 8)
    block = pl.BlockSpec((group, BLK, 128), lambda k, i, places, used: (i, 0, places[k]))
    piece = pl.BlockSpec((1, 8, group, 16, 128), lambda k, i, *_: (k, 0, i, 0, 0))
    kept = list(made) if made else []
    return call(
        adamw_kernel, "adamw", (pieces.shape[0], slots // group), 2,
        [piece, block, block, block] + [ANY] * len(kept),
        [(block, shape(slots, BLK, C))] * 3,
        [pltpu.VMEM((group, BLK, 128), F32)],
        (places, used, pieces, master, one, two, *kept),
        5 * slots * BLK * C * pieces.shape[0],
        {6 + k: k for k in range(len(kept))},
    )


def prepare(actions, features, order, tsteps, lengths, cot_skip, cot_down):
    micro, samp = lengths.shape
    count = micro * samp
    lens_flat = lengths.reshape(count)
    lens = jnp.broadcast_to(lens_flat.astype(F32)[:, None], (count, 128))
    inv = 1.0 / (lens * GC)
    keep = jnp.arange(H)[:, None, None] < lens_flat[None, :, None]
    x = jnp.where(keep, actions.reshape(count, H, CI).transpose(1, 0, 2), jnp.zeros((), BF))
    cs = cot_skip.reshape(count, H, C).transpose(1, 0, 2)
    cd = cot_down.reshape(count, HD, C).transpose(1, 0, 2)
    obs = features.astype(F32)
    obs_act, obs_back = jax.vjp(mish, obs)
    slope = obs_back(jnp.ones_like(obs))[0]
    obs_act = jnp.take(obs_act.astype(BF), order, axis=0).transpose(1, 0, 2).reshape(count, -1)
    cond = jnp.concatenate([mish(time_embed(tsteps.reshape(count), TE)).astype(BF), obs_act], axis=1)
    return x, cs, cd, lens, inv, cond, slope


def flip(value, axis, bit):
    size = lax.axis_size(axis)
    return lax.ppermute(value, axis, [(i, i ^ bit) for i in range(size)])


def core(value):
    return flip(value, "pair", 1)


def along_x(value):
    return flip(value, "pair", 2)


def along_y(value):
    return flip(value, "dp", 1)


def z_low(value):
    return flip(value, "dp", 2)


def z_high(value):
    return flip(value, "dp", 4)


def pieces_of(block):
    return block.reshape(-1, 8, 16, 4, 128).transpose(1, 3, 0, 2, 4)


def double(value, hop):
    return jnp.concatenate([value, hop(value)], axis=0)


def tie(*values):
    return lax.optimization_barrier(values)


def gather_lists(early, late, features):
    def halves(value):
        front = value.shape[1] // 2
        return value[:, :front], value[:, front:]

    early = double(early[None], z_high)
    features = double(features, core)
    early, late, features = tie(early, late[None], features)
    early, late = double(early, z_low), double(late, z_high)
    early, late = tie(early, late)
    a, b = halves(early)
    a, b, late = double(a, along_y), double(b, along_x), double(late, z_low)
    a, b, late = tie(a, b, late)
    c, d = halves(late)
    a, b, c, d = double(a, along_x), double(b, along_y), double(c, along_y), double(d, along_x)
    a, b, c, d = tie(a, b, c, d)
    return (a, core(a), b, core(b)), (c, d), features


def parts(own, received=None):
    size = own.shape[0] // 2
    if received is None:
        return own[:size], own[size:]
    return own[:size] + received[:size], own[size:] + received[size:]


def sum_all(value):
    for axis in ("pair", "dp"):
        bit = 1
        while bit < lax.axis_size(axis):
            value = value + flip(value, axis, bit)
            bit = bit * 2
    return value


def split_order(blocks):
    return jnp.concatenate([blocks[:FIRST_N], blocks[FIRST_N + LATE_N :]], axis=0), blocks[FIRST_N : FIRST_N + LATE_N]


def join_order(early, late):
    return jnp.concatenate([early[:FIRST_N], late, early[FIRST_N:]], axis=0)


def as_lists(blocks):
    front = blocks.shape[0] // 2
    found = []
    for by_y_first, part in ((False, blocks[:front]), (True, blocks[front:])):
        cut = pieces_of(part)
        for core_bit in range(2):
            found.append(jnp.stack([cut[place((0, 0), k, by_y_first, core_bit)] for k in range(16)]))
    return tuple(found)


def from_lists(lists):
    parts = []
    for by_y_first, pair in ((False, lists[:2]), (True, lists[2:])):
        table = {}
        for core_bit, part in enumerate(pair):
            for k in range(16):
                table[place((0, 0), k, by_y_first, core_bit)] = part[k]
        cut = jnp.stack([jnp.stack([table[(row, col)] for col in range(4)]) for row in range(8)])
        parts.append(cut.transpose(2, 0, 3, 1, 4).reshape(-1, BLK, C))
    return jnp.concatenate(parts, axis=0)


def body(
    actions,
    observations,
    tsteps,
    lengths,
    cot_skip,
    cot_down,
    owners,
    master,
    moment_one,
    moment_two,
    small_master,
    small_one,
    small_two,
):
    micro, samp = lengths.shape
    slot_count = master.shape[0]
    dp_count = lax.axis_size("dp")
    slots_all = dp_count * slot_count
    me_pair = lax.axis_index("pair")
    me_dp = lax.axis_index("dp")
    by_pieces = dp_count == 8 and lax.axis_size("pair") == 4
    slot_index = slot_of(owners, slot_count)
    block_of = (
        jnp.full((slots_all,), -1, jnp.int32).at[slot_index].set(jnp.arange(NBLK, dtype=jnp.int32))
    )
    used = (lax.dynamic_slice_in_dim(block_of, me_dp * slot_count, slot_count, axis=0) >= 0).astype(jnp.int32)
    here = jnp.stack([me_dp, me_pair]).astype(jnp.int32)
    if by_pieces:
        me = here
        columns = lax.dynamic_slice_in_dim(master, me_pair * 128, 128, axis=2).astype(BF)
        columns = columns.reshape(slot_count, 8, 16, 128).transpose(1, 0, 2, 3)
        slots = lax.all_to_all(columns, "dp", 0, 0).reshape(slots_all, 16, 128)
        early_index, late_index = split_order(slot_index)
        quarters = double(observations.reshape(1, micro * samp, -1), along_x)
        slots, quarters = tie(slots, quarters)
        early_lists, (c, d), quarters = gather_lists(
            jnp.take(slots, early_index, axis=0), jnp.take(slots, late_index, axis=0), quarters
        )
        features = quarters[jnp.array([0, 2, 1, 3])]
    else:
        me = jnp.zeros_like(here)
        quarter = lax.dynamic_slice_in_dim(master, me_pair * 32, 32, axis=1).astype(BF)
        slots = lax.all_gather(quarter, "dp", axis=0, tiled=True)
        mine = jnp.take(slots, slot_index, axis=0)
        early, late = split_order(lax.all_gather(mine, "pair", axis=1, tiled=True))
        early_lists, late_lists = as_lists(early), as_lists(late)
        features = lax.all_gather(observations.reshape(micro * samp, -1), "pair", axis=0)


    order = jnp.arange(4, dtype=jnp.int32) ^ me[1]
    x, cs, cd, lens, inv, cond, slope = prepare(actions, features, order, tsteps, lengths, cot_skip, cot_down)
    width = samp
    if by_pieces:
        c_got, d_got = along_x(c), along_y(d)
    normed, rstd, hid, mod, w_early = run_first(me, early_lists, x, cond, lens, inv, small_master, width)
    if by_pieces:
        c_got, d_got, normed, rstd, hid, mod, w_early = tie(c_got, d_got, normed, rstd, hid, mod, w_early)
        c, d = jnp.concatenate([c, c_got], axis=0), jnp.concatenate([d, d_got], axis=0)
        late_lists = (c, core(c), d, core(d))
    skip, dskip, g2, *late_grads, gs_late, w_late = run_second(
        me, late_lists, hid, x, cs, cd, lens, inv, small_master, width
    )
    half = micro // 2
    third = functools.partial(run_third, w_late)
    rest = (normed, rstd, mod, lens, inv, small_master, width)

    def windows_first(*values):
        whole_one = jnp.concatenate(values, axis=1) if len(values) > 1 else values[0]
        turned = whole_one.transpose(1, 0, 2).reshape(micro, samp, whole_one.shape[0], whole_one.shape[2])
        return with_layout_constraint(turned, Layout(major_to_minor=(0, 1, 2, 3)))

    if by_pieces:
        a, a_send, b, b_send = late_grads
        a_got, b_got = core(a_send), core(b_send)
        g1_front, dmod_front, down_front, gs_front = third(g2, skip, *rest, 0, half)
        a_got, b_got, g1_front, dmod_front, gs_front = tie(a_got, b_got, g1_front, dmod_front, gs_front)
        (a, a_send), (b, b_send) = parts(a, a_got), parts(b, b_got)
        a_send, b_send, g2_back, gs_front = tie(a_send, b_send, g2, gs_front)
        a_got, b_got = along_x(a_send), along_y(b_send)
        g1_back, dmod_back, down_back, gs_back = third(g2_back, skip, *rest, half, micro - half)
        a_got, b_got, g1_back, dmod_back, gs_back = tie(a_got, b_got, g1_back, dmod_back, gs_back)
        (a, a_send), (b, b_send) = parts(a, a_got), parts(b, b_got)
        a_send, b_send, g1_back = tie(a_send, b_send, g1_back)
        a_got, b_got = along_y(a_send), along_x(b_send)
        early_grads = run_early_grads(me, x, g1_front, g1_back, cond, dmod_front, dmod_back, width)
        a_got, b_got, *early_grads = tie(a_got, b_got, *early_grads)
        late = jnp.concatenate([a + a_got, b + b_got], axis=1)

        small = jnp.concatenate([(gs_front + gs_back)[0:5], gs_late[0:5]], axis=0)
        a, a_send, b, b_send = early_grads
        late, late_send = parts(late)
        a_got, b_got, small_got, late_got = core(a_send), core(b_send), core(small), z_low(late_send)
        a_got, b_got, small_got = tie(a_got, b_got, small_got)
        (a, a_send), (b, b_send), small = parts(a, a_got), parts(b, b_got), small + small_got
        a_send, b_send, dskip = tie(a_send, b_send, dskip)
        a_got, b_got, small_got = along_x(a_send), along_y(b_send), along_x(small)
        dx, dobs = run_inputs(
            me, w_early, w_late, g1_front, g1_back, dskip, dmod_front, dmod_back, slope, lens, width
        )
        a_got, b_got, small_got, late_got, dx, dobs = tie(a_got, b_got, small_got, late_got, dx, dobs)
        late, late_send = parts(late, late_got)
        late_got = z_high(late_send)
        (a, a_send), (b, b_send), small = parts(a, a_got), parts(b, b_got), small + small_got
        a_got, b_got = along_y(a_send), along_x(b_send)
        skip_out = windows_first(skip)
        a_got, b_got, skip_out, small = tie(a_got, b_got, skip_out, small)
        early, early_send = parts(jnp.concatenate([a + a_got, b + b_got], axis=1))
        early_got, small_got = z_low(early_send), along_y(small)
        down_out = windows_first(down_front, down_back)
        early_got, small_got, down_out, dobs = tie(early_got, small_got, down_out, dobs)
        early, early_send = parts(early, early_got)
        early_got = z_high(early_send)
        dobs, dobs_send = parts(dobs)
        dobs_got = along_x(dobs_send)
        small = small + small_got
        early_got, late_got = tie(early_got, late_got)
        grads = join_order((early + early_got)[0], (late + late_got)[0])

        spread = jnp.take(grads, jnp.maximum(block_of, 0), axis=0).reshape(dp_count, slot_count, 16, 128)
        spread, dx, small = tie(spread, dx, small)
        owned = lax.all_to_all(spread, "dp", 0, 0)
        small_got = z_low(small)
        actions_grad = windows_first(dx)
        owned, actions_grad, small_got, dobs_got = tie(owned, actions_grad, small_got, dobs_got)
        places = me[1] ^ jnp.arange(4, dtype=jnp.int32)
        state = (master, moment_one, moment_two)
        x_got, core_got = along_x(owned), core(owned)
        small = small + small_got
        small_got = z_high(small)
        dobs, dobs_send = parts(dobs, dobs_got)
        dobs_got = core(dobs_send)
        made = run_adamw(places[0:1], used, owned[None], *state)
        core_got, small_got, dobs_got, *made = tie(core_got, small_got, dobs_got, *made)
        grad_small = small + small_got
        observations_grad = (dobs + dobs_got).reshape(observations.shape)
        made = run_adamw(places[1:2], used, core_got[None], *state, made)
        x_got, *made = tie(x_got, *made)
        core_got = core(x_got)
        made = run_adamw(places[2:3], used, x_got[None], *state, made)
        core_got, *made = tie(core_got, *made)
        new_one, new_two, new_master = run_adamw(places[3:4], used, core_got[None], *state, made)
    else:
        g1_front, dmod_front, down_front, gs_front = third(g2, skip, *rest, 0, half)
        g1_back, dmod_back, down_back, gs_back = third(g2, skip, *rest, half, micro - half)
        early_grads = run_early_grads(me, x, g1_front, g1_back, cond, dmod_front, dmod_back, width)
        dx, dobs = run_inputs(
            me, w_early, w_late, g1_front, g1_back, dskip, dmod_front, dmod_back, slope, lens, width
        )
        skip_out, down_out, actions_grad = windows_first(skip), windows_first(down_front, down_back), windows_first(dx)
        small = jnp.concatenate([(gs_front + gs_back)[0:5], gs_late[0:5]], axis=0)
        grad_small = sum_all(small)
        observations_grad = lax.psum_scatter(dobs, "pair", scatter_dimension=0).reshape(observations.shape)
        grads = join_order(from_lists(early_grads), from_lists(late_grads))
        rows = grads.reshape(-1, 4, 32, C).transpose(1, 0, 2, 3)
        rows = lax.psum_scatter(rows, "pair", scatter_dimension=0)
        spread = jnp.take(rows, jnp.maximum(block_of, 0), axis=0)
        owned = lax.psum_scatter(spread, "dp", scatter_dimension=0, tiled=True)
        owned = lax.all_gather(owned, "pair", axis=1, tiled=True)
        cut = pieces_of(owned).transpose(1, 0, 2, 3, 4)
        places = jnp.arange(4, dtype=jnp.int32)
        new_one, new_two, new_master = run_adamw(places, used, cut, master, moment_one, moment_two)
    small_first, small_second, new_small = adamw(
        small_master, small_one, small_two, grad_small, RATE_SMALL
    )
    return (
        skip_out,
        down_out,
        actions_grad,
        observations_grad,
        new_one,
        new_two,
        new_master,
        small_first,
        small_second,
        new_small,
    )


def solution(mesh):
    placed = (
        P(None, ("dp", "pair"), None, None),
        P(None, "dp", "pair"),
        P(None, ("dp", "pair")),
        P(None, ("dp", "pair")),
        P(None, ("dp", "pair"), None, None),
        P(None, ("dp", "pair"), None, None),
        P(),
        P("dp", None, None),
        P("dp", None, None),
        P("dp", None, None),
        P(),
        P(),
        P(),
    )
    return jax.shard_map(
        body,
        mesh=mesh,
        in_specs=placed,
        out_specs=(
            P(None, ("dp", "pair"), None, None),
            P(None, ("dp", "pair"), None, None),
            P(None, ("dp", "pair"), None, None),
            P(None, "dp", "pair"),
            P("dp", None, None),
            P("dp", None, None),
            P("dp", None, None),
            P(),
            P(),
            P(),
        ),
        check_vma=False,
    )
```

```python
import functools
import math

import jax
import jax.numpy as jnp
from jax import lax
from jax.experimental.layout import Layout, with_layout_constraint
from jax.experimental import pallas as pl
from jax.experimental.pallas import tpu as pltpu
from jax.sharding import PartitionSpec as P

CI = 256
C = 512
TE = 128
KW = 5
H = 16
HD = 8
KD = 3
NSMALL = 10
STEP = 10
BLK = 128
COND = 1152
NBLK = 62
GC = 64
LEAST = 4

FIRST_N, SECOND_N, RES_N, DOWN_N, FILM_N = 10, 20, 2, 12, 9
EARLY_N = FIRST_N + 2 * FILM_N
LATE_N = SECOND_N + RES_N + DOWN_N
DOWN_IN = SECOND_N + RES_N
PIECES = 32

BETA_ONE = 0.9
BETA_TWO = 0.999
EPS_ADAM = 1e-08
DECAY = 0.01
RATE_MATRIX = 0.1
RATE_SMALL = 1.0

F32 = jnp.float32
BF = jnp.bfloat16
NT = (((1,), (1,)), ((), ()))
TN = (((0,), (0,)), ((), ()))
MIB = 2**20
VMEM_LIMITS = dict(first=20, second=43, third=22, early_grads=22, inputs=20, adamw=14)


def mish(value):
    return value * jnp.tanh(jax.nn.softplus(value))


def time_embed(step_ids, width):
    half = width // 2
    freq = jnp.exp(-math.log(10000.0) * jnp.arange(half, dtype=F32) / (half - 1))
    angle = step_ids.astype(F32)[:, None] * freq[None, :]
    return jnp.concatenate([jnp.sin(angle), jnp.cos(angle)], axis=1)


def slot_of(owners, slot_count):
    same = owners[:, None] == owners[None, :]
    order = jnp.arange(owners.shape[0], dtype=jnp.int32)
    earlier = order[:, None] > order[None, :]
    rank = jnp.sum((same & earlier).astype(jnp.int32), axis=1)
    return owners * slot_count + rank


def adamw(weight, first_m, second_m, grad, rate):
    first_new = BETA_ONE * first_m + (1.0 - BETA_ONE) * grad
    second_new = BETA_TWO * second_m + (1.0 - BETA_TWO) * grad * grad
    fix_one = 1.0 - BETA_ONE**STEP
    fix_two = 1.0 - BETA_TWO**STEP
    update = first_new / fix_one / (jnp.sqrt(second_new / fix_two) + EPS_ADAM) + DECAY * weight
    return (first_new, second_new, weight - rate * update)


def keep(lens, t, value):
    return value if t < LEAST else jnp.where(lens > t, value, 0.0)


def mish_parts(v):
    w = jnp.exp(jnp.minimum(v, 30.0))
    n = w * (w + 2.0)
    return w, n, pl.reciprocal(n + 2.0, approx=True)


def mish_only(v):
    _, n, r = mish_parts(v)
    return v * (n * r)


def mish_both(v):
    w, n, r = mish_parts(v)
    t = n * r
    return v * t, t + (4.0 * v) * (((n - w) * r) * r)


def group_sum(value):
    low_half = lax.broadcasted_iota(jnp.int32, value.shape, 1) < GC
    zero = jnp.zeros_like(value)
    left = jnp.sum(jnp.where(low_half, value, zero), axis=1, keepdims=True)
    right = jnp.sum(jnp.where(low_half, zero, value), axis=1, keepdims=True)
    return jnp.where(low_half, left, right)


def lanes(q):
    return slice(q * 128, (q + 1) * 128)


def flips_of(k):
    return (k >> 3) & 1, (k >> 2) & 1, (k >> 1) & 1, k & 1


def place(me, k, by_y_first, core):
    one, two, z_low, z_high = flips_of(k)
    y, x = (one, two) if by_y_first else (two, one)
    return me[0] ^ (z_high * 4 + z_low * 2 + y), me[1] ^ (x * 2 + core)


def fetch(me, sources, dst, sem):
    at = 0
    for by_y_first, pair in ((False, sources[:2]), (True, sources[2:])):
        count = pair[0].shape[1]
        for core, source in enumerate(pair):
            for k in range(16):
                row, col = place(me, k, by_y_first, core)
                pltpu.make_async_copy(
                    source.at[k],
                    dst.at[at : at + count, row, :, pl.ds(pl.multiple_of(col * 128, 128), 128)],
                    sem,
                ).start()
        at = at + count
    return pltpu.make_async_copy(dst, dst, sem)


def store_pieces(me, acc, outs, base=0):
    at = 0
    for by_y_first, pair in ((False, outs[:2]), (True, outs[2:])):
        count = pair[0].shape[1]

        def one_block(b, carry, at=at, by_y_first=by_y_first, pair=pair):
            for core, out in enumerate(pair):
                for k in range(16):
                    row, col = place(me, k, by_y_first, core)
                    rows = pl.ds(pl.multiple_of((at + b) * BLK + row * 16, 16), 16)
                    cols = pl.ds(pl.multiple_of(col * 128, 128), 128)
                    out[k, b] = acc[rows, cols].astype(BF)
            return carry

        lax.fori_loop(0, count, one_block, 0)
        at = at + count


def matrix(ref, at, count):
    return ref[at : at + count].reshape(count * BLK, C)


def first_kernel(me, pa, pb, pc, pd, x_ref, cond_ref, lens_ref, inv_ref, small_ref, fst, mean_ref, rstd_ref, hid_ref,
                 mod_ref, w_out, w_one, xp, sem):
    step = pl.program_id(0)
    frames, width, _ = x_ref.shape
    rows = frames * width

    @pl.when(step == 0)
    def _():
        arrival = fetch((me[0], me[1]), (pa, pb, pc, pd), w_one, sem.at[0])
        xp[0:2] = jnp.zeros((2, width, CI), BF)
        xp[frames + 2 :] = jnp.zeros((2, width, CI), BF)
        arrival.wait()
        pltpu.make_async_copy(w_one, w_out, sem.at[1]).start()
        for k in range(2):
            mod_ref[k] = (
                jnp.dot(cond_ref[...], matrix(w_one, FIRST_N + k * FILM_N, FILM_N), preferred_element_type=F32)
                + small_ref[3 + k : 4 + k]
            )

    xp[2 : frames + 2] = x_ref[...]
    cut = C // 2
    for part in range(2):
        cs = slice(part * cut, (part + 1) * cut)
        total = small_ref[0:1, cs]
        for a in range(KW):
            total = total + jnp.dot(
                xp[a : a + frames].reshape(rows, CI),
                w_one[2 * a : 2 * a + 2, :, :, cs].reshape(CI, cut),
                preferred_element_type=F32,
            )
        fst[:, :, cs] = total.reshape(frames, width, cut)

    here = pl.ds(pl.multiple_of(step * width, width), width)
    lens = lens_ref[...]
    inv = inv_ref[...]
    for q in range(C // 128):
        ls = lanes(q)
        total = jnp.zeros((width, 128), F32)
        for t in range(frames):
            total = total + keep(lens, t, fst[t, :, ls])
        mean = group_sum(total) * inv
        total = jnp.zeros((width, 128), F32)
        for t in range(frames):
            centered = fst[t, :, ls] - mean
            total = total + keep(lens, t, centered * centered)
        rstd = lax.rsqrt(group_sum(total) * inv + 1e-05)
        mean_ref[:, ls] = mean
        rstd_ref[:, ls] = rstd
        slant = rstd * small_ref[1:2, ls]
        level = small_ref[2:3, ls] - mean * slant
        scale, shift = mod_ref[0, here, ls], mod_ref[1, here, ls]
        for t in range(frames):
            value = scale * mish_only(fst[t, :, ls] * slant + level) + shift
            hid_ref[t, :, ls] = keep(lens, t, value).astype(BF)

    @pl.when(step == pl.num_programs(0) - 1)
    def _():
        pltpu.make_async_copy(w_one, w_out, sem.at[1]).wait()


def second_kernel(me, pa, pb, pc, pd, hid_ref, x_ref, cs_ref, cd_ref, lens_ref, inv_ref, small_ref, skip_ref,
                  dskip_ref, g2_ref, ga, gb, gc, gd, gs_ref, w_out, w_two, hp, cdp, sec, br, dev, dod, se, so, acc,
                  sem):
    step = pl.program_id(0)
    last = pl.num_programs(0) - 1
    frames, width, _ = x_ref.shape
    half = frames // 2
    rows = frames * width

    @pl.when(step == 0)
    def _():
        arrival = fetch((me[0], me[1]), (pa, pb, pc, pd), w_two, sem.at[0])
        hp[0:2] = jnp.zeros((2, width, C), BF)
        hp[frames + 2 :] = jnp.zeros((2, width, C), BF)
        cdp[half:] = jnp.zeros((1, width, C), BF)
        so[0:1] = jnp.zeros((1, width, C), BF)
        acc[...] = jnp.zeros_like(acc)
        gs_ref[...] = jnp.zeros_like(gs_ref)
        arrival.wait()
        pltpu.make_async_copy(w_two, w_out, sem.at[1]).start()

    hp[2 : frames + 2] = hid_ref[...]
    cdp[0:half] = cd_ref[...]
    cot = cdp[0:half].reshape(half * width, C)
    cot_next = cdp[1 : half + 1].reshape(half * width, C)
    lens = lens_ref[...]
    inv = inv_ref[...]
    zero = jnp.zeros((width, 128), F32)
    cut = C // 2

    def columns(part):
        return slice(part * cut, (part + 1) * cut)

    def weight(at, count, part):
        return w_two[at : at + count, :, :, columns(part)].reshape(count * BLK, cut)

    def weight_rows(at, part):
        n = cut // BLK
        return matrix(w_two, at + part * n, n)

    def forward(part):
        cs = columns(part)
        dev[:, :, cs] = lax.dot_general(
            cot, weight_rows(DOWN_IN + 4, part), NT, preferred_element_type=F32
        ).reshape(half, width, cut)
        dod[:, :, cs] = (
            lax.dot_general(cot, weight_rows(DOWN_IN + 8, part), NT, preferred_element_type=F32)
            + lax.dot_general(cot_next, weight_rows(DOWN_IN, part), NT, preferred_element_type=F32)
        ).reshape(half, width, cut)
        br[:, :, cs] = (
            jnp.dot(x_ref[...].reshape(rows, CI), weight(SECOND_N, RES_N, part), preferred_element_type=F32)
            + small_ref[8:9, cs]
        ).reshape(frames, width, cut)
        total = jnp.dot(hp[0:frames].reshape(rows, C), weight(0, 4, part), preferred_element_type=F32)
        for a in range(1, KW):
            total = total + jnp.dot(
                hp[a : a + frames].reshape(rows, C), weight(4 * a, 4, part), preferred_element_type=F32
            )
        sec[:, :, cs] = (total + small_ref[5:6, cs]).reshape(frames, width, cut)

    def norm(q):
        ls = lanes(q)
        total = zero
        for t in range(frames):
            total = total + keep(lens, t, sec[t, :, ls])
        mean = group_sum(total) * inv
        total = zero
        for t in range(frames):
            centered = sec[t, :, ls] - mean
            total = total + keep(lens, t, centered * centered)
        rstd = lax.rsqrt(group_sum(total) * inv + 1e-05)
        gain = small_ref[6:7, ls]
        slant = rstd * gain
        level = small_ref[7:8, ls] - mean * slant
        sum_dy, sum_dyv, sum_ds = zero, zero, zero
        for t in range(frames):
            value = sec[t, :, ls]
            act, slope = mish_both(value * slant + level)
            skip = (act + br[t, :, ls]).astype(BF)
            skip_ref[t, :, ls] = skip
            if t % 2:
                so[t // 2 + 1, :, ls] = skip
                back = dod[t // 2, :, ls]
            else:
                se[t // 2, :, ls] = skip
                back = dev[t // 2, :, ls]
            ds = cs_ref[t, :, ls].astype(F32) + back
            dskip_ref[t, :, ls] = ds.astype(BF)
            sum_ds = sum_ds + ds
            dy = ds * slope
            br[t, :, ls] = dy
            sum_dy = sum_dy + dy
            sum_dyv = sum_dyv + dy * value
        sum_dyn = rstd * (sum_dyv - mean * sum_dy)
        tilt = (rstd * rstd) * (group_sum(sum_dyn * gain) * inv)
        base = rstd * (group_sum(sum_dy * gain) * inv) - mean * tilt
        sum_g, sum_cd = zero, zero
        for t in range(frames):
            grad = br[t, :, ls] * slant - keep(lens, t, base + sec[t, :, ls] * tilt)
            g2_ref[t, :, ls] = grad.astype(BF)
            sum_g = sum_g + grad
        for t in range(half):
            sum_cd = sum_cd + cd_ref[t, :, ls].astype(F32)
        for k, part in enumerate((sum_g, sum_dyn, sum_dy, sum_ds, sum_cd)):
            gs_ref[k : k + 1, ls] += jnp.sum(part, axis=0, keepdims=True)

    def gradients(part):
        cs = columns(part)
        grad_two = g2_ref[:, :, cs].reshape(rows, cut)
        for a in range(KW):
            acc[a * C : (a + 1) * C, cs] += lax.dot_general(
                hp[a : a + frames].reshape(rows, C), grad_two, TN, preferred_element_type=F32
            )
        at = KW * C
        acc[at : at + CI, cs] += lax.dot_general(
            x_ref[...].reshape(rows, CI), dskip_ref[:, :, cs].reshape(rows, cut), TN, preferred_element_type=F32
        )
        at = at + CI
        for a, source in enumerate((so.at[0:half], se, so.at[1 : half + 1])):
            low = at + a * C + part * cut
            acc[low : low + cut] += lax.dot_general(
                source[:, :, cs].reshape(half * width, cut), cot, TN, preferred_element_type=F32
            )

    per = (C // 128) // 2
    forward(0)
    for q in range(0 * per, 1 * per):
        norm(q)
    forward(1)
    gradients(0)
    for q in range(1 * per, 2 * per):
        norm(q)
    gradients(1)

    @pl.when(step == last)
    def _():
        store_pieces((me[0], me[1]), acc, (ga, gb, gc, gd))
        pltpu.make_async_copy(w_two, w_out, sem.at[1]).wait()


def third_kernel(w_hbm, g2_ref, skip_ref, first_ref, mean_ref, rstd_ref, mod_ref, lens_ref, inv_ref, small_ref,
                 g1_ref, dmod_ref, down_ref, gs_ref, w_two, gp, dh, se, so, sem):
    step = pl.program_id(0)
    frames, width, _ = g2_ref.shape
    rows = frames * width
    half = frames // 2

    @pl.when(step == 0)
    def _():
        arrival = pltpu.make_async_copy(w_hbm, w_two, sem.at[0])
        arrival.start()
        gp[0:2] = jnp.zeros((2, width, C), BF)
        gp[frames + 2 :] = jnp.zeros((2, width, C), BF)
        so[0:1] = jnp.zeros((1, width, C), BF)
        gs_ref[...] = jnp.zeros_like(gs_ref)
        arrival.wait()

    gp[2 : frames + 2] = g2_ref[...]
    cut = C // 2
    for part in range(2):
        total = jnp.zeros((rows, cut), F32)
        for a in range(KW):
            total = total + lax.dot_general(
                gp[4 - a : 4 - a + frames].reshape(rows, C),
                matrix(w_two, 4 * a + 2 * part, 2),
                NT,
                preferred_element_type=F32,
            )
        dh[:, :, part * cut : (part + 1) * cut] = total.reshape(frames, width, cut)
    for j in range(half):
        se[j] = skip_ref[2 * j]
        so[j + 1] = skip_ref[2 * j + 1]
    down = jnp.dot(so[0:half].reshape(half * width, C), matrix(w_two, DOWN_IN, 4), preferred_element_type=F32)
    down = down + jnp.dot(
        se[...].reshape(half * width, C), matrix(w_two, DOWN_IN + 4, 4), preferred_element_type=F32
    )
    down = down + jnp.dot(
        so[1 : half + 1].reshape(half * width, C), matrix(w_two, DOWN_IN + 8, 4), preferred_element_type=F32
    )
    down_ref[...] = (down + small_ref[9:10]).astype(BF).reshape(half, width, C)

    lens = lens_ref[...]
    inv = inv_ref[...]
    zero = jnp.zeros((width, 128), F32)
    for q in range(C // 128):
        ls = lanes(q)
        gain = small_ref[1:2, ls]
        mean, rstd = mean_ref[:, ls], rstd_ref[:, ls]
        slant = rstd * gain
        level = small_ref[2:3, ls] - mean * slant
        scale = mod_ref[0, :, ls]
        sum_dy, sum_dyv, d_scale, d_shift = zero, zero, zero, zero
        for t in range(frames):
            value = first_ref[t, :, ls]
            act, slope = mish_both(value * slant + level)
            grad = keep(lens, t, dh[t, :, ls])
            d_scale = d_scale + grad * act
            d_shift = d_shift + grad
            dy = (grad * scale) * slope
            dh[t, :, ls] = dy
            sum_dy = sum_dy + dy
            sum_dyv = sum_dyv + dy * value
        sum_dyn = rstd * (sum_dyv - mean * sum_dy)
        tilt = (rstd * rstd) * (group_sum(sum_dyn * gain) * inv)
        base = rstd * (group_sum(sum_dy * gain) * inv) - mean * tilt
        sum_g = zero
        for t in range(frames):
            grad = dh[t, :, ls] * slant - keep(lens, t, base + first_ref[t, :, ls] * tilt)
            g1_ref[t, :, ls] = grad.astype(BF)
            sum_g = sum_g + grad
        d_scale, d_shift = d_scale.astype(BF), d_shift.astype(BF)
        dmod_ref[0, :, ls] = d_scale
        dmod_ref[1, :, ls] = d_shift
        for k, part in enumerate((sum_g, sum_dyn, sum_dy, d_scale.astype(F32), d_shift.astype(F32))):
            gs_ref[k : k + 1, ls] += jnp.sum(part, axis=0, keepdims=True)


def of_halves(step, half, front, back, dst):
    @pl.when(step < half)
    def _():
        dst[...] = front[...]

    @pl.when(step >= half)
    def _():
        dst[...] = back[...]


def early_grads_kernel(me, x_ref, front_ref, back_ref, cond_ref, dmod_front, dmod_back, ga, gb, gc, gd, xp, g1, acc):
    step = pl.program_id(0)
    steps = pl.num_programs(0)
    frames, width, _ = x_ref.shape
    rows = frames * width
    near = dmod_front.shape[1]

    @pl.when(step == 0)
    def _():
        xp[0:2] = jnp.zeros((2, width, CI), BF)
        xp[frames + 2 :] = jnp.zeros((2, width, CI), BF)
        acc[0 : KW * CI] = jnp.zeros((KW * CI, C), F32)
        for k in range(2):
            at = KW * CI + k * COND
            acc[at : at + COND] = lax.dot_general(
                cond_ref[0:near], dmod_front[k], TN, preferred_element_type=F32
            ) + lax.dot_general(cond_ref[near:], dmod_back[k], TN, preferred_element_type=F32)

    xp[2 : frames + 2] = x_ref[...]
    of_halves(step, near // width, front_ref, back_ref, g1)
    grad_one = g1[...].reshape(rows, C)
    for a in range(KW):
        acc[a * CI : (a + 1) * CI] += lax.dot_general(
            xp[a : a + frames].reshape(rows, CI), grad_one, TN, preferred_element_type=F32
        )

    @pl.when(step == steps - 1)
    def _():
        store_pieces((me[0], me[1]), acc, (ga, gb, gc, gd))


def inputs_kernel(me, w_early, w_late, front_ref, back_ref, dskip_ref, dmod_front, dmod_back, slope_ref, lens_ref,
                  dx_ref, dobs_ref, w_one, w_res, gp, sem):
    step = pl.program_id(0)
    steps = pl.num_programs(0)
    frames, width, _ = dskip_ref.shape
    rows = frames * width
    near = dmod_front.shape[1]

    @pl.when(step == 0)
    def _():
        early = pltpu.make_async_copy(w_early, w_one, sem.at[0])
        late = pltpu.make_async_copy(w_late.at[SECOND_N:DOWN_IN], w_res, sem.at[1])
        early.start()
        late.start()
        gp[0:2] = jnp.zeros((2, width, C), BF)
        gp[frames + 2 :] = jnp.zeros((2, width, C), BF)
        early.wait()
        late.wait()
        for r in range(4):
            at = FIRST_N + 1 + 2 * (me[1] ^ r)
            for dmod, low_at, high_at in ((dmod_front, 0, near), (dmod_back, near, cond_rows(slope_ref))):
                back = lax.dot_general(
                    dmod[0], w_one[pl.ds(at, 2)].reshape(2 * BLK, C), NT, preferred_element_type=F32
                ) + lax.dot_general(
                    dmod[1], w_one[pl.ds(at + FILM_N, 2)].reshape(2 * BLK, C), NT, preferred_element_type=F32
                )
                dobs_ref[r, low_at:high_at] = back * slope_ref[r, low_at:high_at]

    of_halves(step, near // width, front_ref, back_ref, gp.at[2 : frames + 2])
    total = lax.dot_general(
        dskip_ref[...].reshape(rows, C), matrix(w_res, 0, RES_N), NT, preferred_element_type=F32
    )
    for a in range(KW):
        total = total + lax.dot_general(
            gp[4 - a : 4 - a + frames].reshape(rows, C), matrix(w_one, 2 * a, 2), NT, preferred_element_type=F32
        )
    total = total.reshape(frames, width, CI)
    lens = lens_ref[...]
    for t in range(frames):
        for q in range(CI // 128):
            dx_ref[t, :, lanes(q)] = keep(lens, t, total[t, :, lanes(q)])


def cond_rows(slope_ref):
    return slope_ref.shape[1]


def adamw_kernel(places, used, piece_ref, master_ref, one_ref, two_ref, *rest):
    one_out, two_out, master_out, grad = rest[-4:]
    group = grad.shape[0]
    for slot in range(group):
        keep = used[pl.program_id(1) * group + slot] > 0
        for row in range(8):
            piece = piece_ref[0, row, slot].astype(F32)
            grad[slot, row * 16 : row * 16 + 16] = jnp.where(keep, piece, 0.0)
    one_out[...], two_out[...], master_out[...] = adamw(
        master_ref[...], one_ref[...], two_ref[...], grad[...], RATE_MATRIX
    )


def tiles(frames, width, channels):
    return pl.BlockSpec((frames, width, channels), lambda i, *_: (0, i, 0))


def rows_of(width, channels):
    return pl.BlockSpec((width, channels), lambda i, *_: (i, 0))


def whole(*shape):
    return pl.BlockSpec(shape, lambda i, *_: (0,) * len(shape))


ANY = pl.BlockSpec(memory_space=pl.ANY)


def weight_scratch(count):
    return pltpu.VMEM((count, 8, 16, C), BF)


def shape(*dims, dtype=F32):
    return jax.ShapeDtypeStruct(dims, dtype)


def half_lists(count):
    front = count // 2
    return [(16, n, 16, 128) for n in (front, front, count - front, count - front)]


def call(kernel, name, grid, scalars, ins, outs, scratch, operands, flops, aliases=None):
    return pl.pallas_call(
        kernel,
        grid_spec=pltpu.PrefetchScalarGridSpec(
            num_scalar_prefetch=scalars,
            grid=grid,
            in_specs=ins,
            out_specs=[spec for spec, _ in outs],
            scratch_shapes=scratch,
        ),
        out_shape=[made for _, made in outs],
        input_output_aliases=aliases or {},
        compiler_params=pltpu.CompilerParams(
            vmem_limit_bytes=VMEM_LIMITS[name] * MIB, dimension_semantics=("arbitrary",) * len(grid)
        ),
        cost_estimate=pl.CostEstimate(flops=flops, bytes_accessed=20 * 2**20, transcendentals=0),
        name=name,
    )(*operands)


def run_first(me, pieces, x, cond, lens, inv, small, width):
    count = x.shape[1]
    return call(
        first_kernel, "first", (count // width,), 1,
        [ANY] * 4 + [tiles(H, width, CI), whole(count, COND), rows_of(width, 128), rows_of(width, 128),
                     whole(NSMALL, C)],
        [(tiles(H, width, C), shape(H, count, C)), (rows_of(width, C), shape(count, C)),
         (rows_of(width, C), shape(count, C)), (tiles(H, width, C), shape(H, count, C, dtype=BF)), (whole(2, count, C), shape(2, count, C)),
         (ANY, shape(EARLY_N, 8, 16, C, dtype=BF))],
        [weight_scratch(EARLY_N), pltpu.VMEM((H + 4, width, CI), BF), pltpu.SemaphoreType.DMA((2,))],
        (me, *pieces, x, cond, lens, inv, small),
        2 * count * H * KW * CI * C,
    )


def run_second(me, pieces, hid, x, cs, cd, lens, inv, small, width):
    count = x.shape[1]
    bf_tile = (tiles(H, width, C), shape(H, count, C, dtype=BF))
    return call(
        second_kernel, "second", (count // width,), 1,
        [ANY] * 4 + [tiles(H, width, C), tiles(H, width, CI), tiles(H, width, C), tiles(HD, width, C),
                     rows_of(width, 128), rows_of(width, 128), whole(NSMALL, C)],
        [bf_tile, bf_tile, bf_tile] + [(whole(*dims), shape(*dims, dtype=BF)) for dims in half_lists(LATE_N)]
        + [(whole(8, C), shape(8, C)), (ANY, shape(LATE_N, 8, 16, C, dtype=BF))],
        [weight_scratch(LATE_N), pltpu.VMEM((H + 4, width, C), BF), pltpu.VMEM((HD + 1, width, C), BF),
         pltpu.VMEM((H, width, C), F32), pltpu.VMEM((H, width, C), F32),
         pltpu.VMEM((HD, width, C), F32), pltpu.VMEM((HD, width, C), F32),
         pltpu.VMEM((HD, width, C), BF), pltpu.VMEM((HD + 1, width, C), BF),
         pltpu.VMEM((LATE_N * BLK, C), F32), pltpu.SemaphoreType.DMA((2,))],
        (me, *pieces, hid, x, cs, cd, lens, inv, small),
        6 * count * H * KW * C * C,
    )


def run_third(w_late, g2, skip, first, mean, rstd, mod, lens, inv, small, width, tiles_at, tiles_n):
    count = tiles_n * width

    def part(frames, channels):
        return pl.BlockSpec((frames, width, channels), lambda i: (0, i + tiles_at, 0))

    def part_rows(channels):
        return pl.BlockSpec((width, channels), lambda i: (i + tiles_at, 0))

    return call(
        third_kernel, "third", (tiles_n,), 0,
        [ANY, part(H, C), part(H, C), part(H, C), part_rows(C), part_rows(C), part(2, C), part_rows(128), part_rows(128), whole(NSMALL, C)],
        [(tiles(H, width, C), shape(H, count, C, dtype=BF)), (tiles(2, width, C), shape(2, count, C, dtype=BF)),
         (tiles(HD, width, C), shape(HD, count, C, dtype=BF)), (whole(8, C), shape(8, C))],
        [weight_scratch(LATE_N), pltpu.VMEM((H + 4, width, C), BF), pltpu.VMEM((H, width, C), F32),
         pltpu.VMEM((HD, width, C), BF), pltpu.VMEM((HD + 1, width, C), BF), pltpu.SemaphoreType.DMA((1,))],
        (w_late, g2, skip, first, mean, rstd, mod, lens, inv, small),
        4 * count * H * KW * C * C,
    )


def front_tiles(width, channels, half):
    return pl.BlockSpec((H, width, channels), lambda i, *_: (0, jnp.minimum(i, half - 1), 0))


def back_tiles(width, channels, half):
    return pl.BlockSpec((H, width, channels), lambda i, *_: (0, jnp.maximum(i - half, 0), 0))


def run_early_grads(me, x, front, back, cond, dmod_front, dmod_back, width):
    count = x.shape[1]
    steps = count // width
    half = front.shape[1]
    return call(
        early_grads_kernel, "early_grads", (steps,), 1,
        [tiles(H, width, CI), front_tiles(width, C, half // width), back_tiles(width, C, half // width), whole(count, COND),
         whole(2, half, C), whole(2, count - half, C)],
        [(whole(*dims), shape(*dims, dtype=BF)) for dims in half_lists(EARLY_N)],
        [pltpu.VMEM((H + 4, width, CI), BF), pltpu.VMEM((H, width, C), BF), pltpu.VMEM((EARLY_N * BLK, C), F32)],
        (me, x, front, back, cond, dmod_front, dmod_back),
        2 * count * H * KW * CI * C,
    )


def run_inputs(me, w_early, w_late, front, back, dskip, dmod_front, dmod_back, slope, lens, width):
    count = dskip.shape[1]
    steps = count // width
    half = front.shape[1]
    return call(
        inputs_kernel, "inputs", (steps,), 1,
        [ANY, ANY, front_tiles(width, C, half // width), back_tiles(width, C, half // width), tiles(H, width, C),
         whole(2, half, C), whole(2, count - half, C), whole(*slope.shape), rows_of(width, 128)],
        [(tiles(H, width, CI), shape(H, count, CI)), (whole(*slope.shape), shape(*slope.shape))],
        [weight_scratch(EARLY_N), weight_scratch(RES_N), pltpu.VMEM((H + 4, width, C), BF),
         pltpu.SemaphoreType.DMA((2,))],
        (me, w_early, w_late, front, back, dskip, dmod_front, dmod_back, slope, lens),
        2 * count * H * (KW + 1) * CI * C,
    )


def run_adamw(places, used, pieces, master, one, two, made=None):
    slots = master.shape[0]
    group = min(slots, 8)
    block = pl.BlockSpec((group, BLK, 128), lambda k, i, places, used: (i, 0, places[k]))
    piece = pl.BlockSpec((1, 8, group, 16, 128), lambda k, i, *_: (k, 0, i, 0, 0))
    kept = list(made) if made else []
    return call(
        adamw_kernel, "adamw", (pieces.shape[0], slots // group), 2,
        [piece, block, block, block] + [ANY] * len(kept),
        [(block, shape(slots, BLK, C))] * 3,
        [pltpu.VMEM((group, BLK, 128), F32)],
        (places, used, pieces, master, one, two, *kept),
        5 * slots * BLK * C * pieces.shape[0],
        {6 + k: k for k in range(len(kept))},
    )


def prepare(actions, features, order, tsteps, lengths, cot_skip, cot_down):
    micro, samp = lengths.shape
    count = micro * samp
    lens_flat = lengths.reshape(count)
    lens = jnp.broadcast_to(lens_flat.astype(F32)[:, None], (count, 128))
    inv = 1.0 / (lens * GC)
    valid = jnp.arange(H)[:, None, None] < lens_flat[None, :, None]
    x = jnp.where(valid, actions.reshape(count, H, CI).transpose(1, 0, 2), jnp.zeros((), BF))
    cs = cot_skip.reshape(count, H, C).transpose(1, 0, 2)
    cd = cot_down.reshape(count, HD, C).transpose(1, 0, 2)
    obs = features.astype(F32)
    obs_act, obs_back = jax.vjp(mish, obs)
    slope = obs_back(jnp.ones_like(obs))[0]
    obs_act = jnp.take(obs_act.astype(BF), order, axis=0).transpose(1, 0, 2).reshape(count, -1)
    cond = jnp.concatenate([mish(time_embed(tsteps.reshape(count), TE)).astype(BF), obs_act], axis=1)
    return x, cs, cd, lens, inv, cond, slope


def flip(value, axis, bit):
    size = lax.axis_size(axis)
    return lax.ppermute(value, axis, [(i, i ^ bit) for i in range(size)])


def core(value):
    return flip(value, "pair", 1)


def along_x(value):
    return flip(value, "pair", 2)


def along_y(value):
    return flip(value, "dp", 1)


def z_low(value):
    return flip(value, "dp", 2)


def z_high(value):
    return flip(value, "dp", 4)


def pieces_of(block):
    return block.reshape(-1, 8, 16, 4, 128).transpose(1, 3, 0, 2, 4)


def double(value, hop):
    return jnp.concatenate([value, hop(value)], axis=0)


def tie(*values):
    return lax.optimization_barrier(values)


def after(value, *others):
    return tie(value, *others)[0]


def gather_lists(early, late):
    def halves(value):
        front = value.shape[1] // 2
        return value[:, :front], value[:, front:]

    early = double(early[None], z_high)
    late = double(after(late[None], early), z_high)
    early = double(early, z_low)
    late = double(after(late, early), z_low)
    a, b = halves(early)
    a, b = double(a, along_y), double(b, along_x)
    c, d = halves(after(late, a, b))
    a, b = double(a, along_x), double(b, along_y)
    c, d = double(c, along_y), double(d, along_x)
    return (a, b), (c, d)


def parts(own, received=None):
    size = own.shape[0] // 2
    if received is None:
        return own[:size], own[size:]
    return own[:size] + received[:size], own[size:] + received[size:]


def sum_all(value):
    for axis in ("pair", "dp"):
        bit = 1
        while bit < lax.axis_size(axis):
            value = value + flip(value, axis, bit)
            bit = bit * 2
    return value


def split_order(blocks):
    return jnp.concatenate([blocks[:FIRST_N], blocks[FIRST_N + LATE_N :]], axis=0), blocks[FIRST_N : FIRST_N + LATE_N]


def join_order(early, late):
    return jnp.concatenate([early[:FIRST_N], late, early[FIRST_N:]], axis=0)


def as_lists(blocks):
    front = blocks.shape[0] // 2
    found = []
    for by_y_first, part in ((False, blocks[:front]), (True, blocks[front:])):
        cut = pieces_of(part)
        for core_bit in range(2):
            found.append(jnp.stack([cut[place((0, 0), k, by_y_first, core_bit)] for k in range(16)]))
    return tuple(found)


def from_lists(lists):
    parts = []
    for by_y_first, pair in ((False, lists[:2]), (True, lists[2:])):
        table = {}
        for core_bit, part in enumerate(pair):
            for k in range(16):
                table[place((0, 0), k, by_y_first, core_bit)] = part[k]
        cut = jnp.stack([jnp.stack([table[(row, col)] for col in range(4)]) for row in range(8)])
        parts.append(cut.transpose(2, 0, 3, 1, 4).reshape(-1, BLK, C))
    return jnp.concatenate(parts, axis=0)


def body(
    actions,
    observations,
    tsteps,
    lengths,
    cot_skip,
    cot_down,
    owners,
    master,
    moment_one,
    moment_two,
    small_master,
    small_one,
    small_two,
):
    micro, samp = lengths.shape
    slot_count = master.shape[0]
    dp_count = lax.axis_size("dp")
    slots_all = dp_count * slot_count
    me_pair = lax.axis_index("pair")
    me_dp = lax.axis_index("dp")
    by_pieces = dp_count == 8 and lax.axis_size("pair") == 4
    slot_index = slot_of(owners, slot_count)
    block_of = (
        jnp.full((slots_all,), -1, jnp.int32).at[slot_index].set(jnp.arange(NBLK, dtype=jnp.int32))
    )
    used = (lax.dynamic_slice_in_dim(block_of, me_dp * slot_count, slot_count, axis=0) >= 0).astype(jnp.int32)
    here = jnp.stack([me_dp, me_pair]).astype(jnp.int32)
    if by_pieces:
        me = here
        columns = lax.dynamic_slice_in_dim(master, me_pair * 128, 128, axis=2).astype(BF)
        columns = columns.reshape(slot_count, 8, 16, 128).transpose(1, 0, 2, 3)
        slots = lax.all_to_all(columns, "dp", 0, 0).reshape(slots_all, 16, 128)
        early_index, late_index = split_order(slot_index)
        quarters = double(observations.reshape(1, micro * samp, -1), along_x)
        quarters = double(after(quarters, slots), core)
        (a, b), (c, d) = gather_lists(
            jnp.take(slots, early_index, axis=0, mode="clip"), jnp.take(slots, late_index, axis=0, mode="clip")
        )
        features = quarters[jnp.array([0, 2, 1, 3])]
    else:
        me = jnp.zeros_like(here)
        quarter = lax.dynamic_slice_in_dim(master, me_pair * 32, 32, axis=1).astype(BF)
        slots = lax.all_gather(quarter, "dp", axis=0, tiled=True)
        mine = jnp.take(slots, slot_index, axis=0)
        early, late = split_order(lax.all_gather(mine, "pair", axis=1, tiled=True))
        early_lists, late_lists = as_lists(early), as_lists(late)
        features = lax.all_gather(observations.reshape(micro * samp, -1), "pair", axis=0)


    order = jnp.arange(4, dtype=jnp.int32) ^ me[1]
    x, cs, cd, lens, inv, cond, slope = prepare(actions, features, order, tsteps, lengths, cot_skip, cot_down)
    count = micro * samp
    width = 64 if count % 64 == 0 else samp
    if by_pieces:
        a, b, x, cs, cd, lens, inv, cond, slope = tie(a, b, x, cs, cd, lens, inv, cond, slope)
        early_lists = (a, core(a), b, core(b))
        c, d = after(c, a), after(d, b)
        c_got, d_got = along_x(c), along_y(d)
    first, mean, rstd, hid, mod, w_early = run_first(me, early_lists, x, cond, lens, inv, small_master, width)
    if by_pieces:
        c_got, d_got, first, mean, rstd, hid, mod, w_early = tie(c_got, d_got, first, mean, rstd, hid, mod, w_early)
        c, d = jnp.concatenate([c, c_got], axis=0), jnp.concatenate([d, d_got], axis=0)
        late_lists = (c, core(c), d, core(d))
    skip, dskip, g2, *late_grads, gs_late, w_late = run_second(
        me, late_lists, hid, x, cs, cd, lens, inv, small_master, width
    )
    half = count // width // 2
    third = functools.partial(run_third, w_late)
    rest = (first, mean, rstd, mod, lens, inv, small_master, width)

    def windows_first(*values):
        whole_one = jnp.concatenate(values, axis=1) if len(values) > 1 else values[0]
        turned = whole_one.transpose(1, 0, 2).reshape(micro, samp, whole_one.shape[0], whole_one.shape[2])
        return with_layout_constraint(turned, Layout(major_to_minor=(0, 1, 2, 3)))

    if by_pieces:
        a, a_send, b, b_send = late_grads
        a_got, b_got = core(a_send), core(b_send)
        g1_front, dmod_front, down_front, gs_front = third(g2, skip, *rest, 0, half)
        a_got, b_got, g1_front, dmod_front, gs_front = tie(a_got, b_got, g1_front, dmod_front, gs_front)
        (a, a_send), (b, b_send) = parts(a, a_got), parts(b, b_got)
        a_send, b_send, g2_back, gs_front = tie(a_send, b_send, g2, gs_front)
        a_got, b_got = along_x(a_send), along_y(b_send)
        g1_back, dmod_back, down_back, gs_back = third(g2_back, skip, *rest, half, count // width - half)
        a_got, b_got, g1_back, dmod_back, gs_back = tie(a_got, b_got, g1_back, dmod_back, gs_back)
        (a, a_send), (b, b_send) = parts(a, a_got), parts(b, b_got)
        a_send, b_send, g1_back = tie(a_send, b_send, g1_back)
        a_got, b_got = along_y(a_send), along_x(b_send)
        early_grads = run_early_grads(me, x, g1_front, g1_back, cond, dmod_front, dmod_back, width)
        a_got, b_got, *early_grads = tie(a_got, b_got, *early_grads)
        late = jnp.concatenate([a + a_got, b + b_got], axis=1)

        small = jnp.concatenate([(gs_front + gs_back)[0:5], gs_late[0:5]], axis=0)
        a, a_send, b, b_send = early_grads
        late, late_send = parts(late)
        a_got, b_got, small_got, late_got = core(a_send), core(b_send), core(small), z_low(late_send)
        a_got, b_got, small_got = tie(a_got, b_got, small_got)
        (a, a_send), (b, b_send), small = parts(a, a_got), parts(b, b_got), small + small_got
        a_send, b_send, dskip = tie(a_send, b_send, dskip)
        a_got, b_got, small_got = along_x(a_send), along_y(b_send), along_x(small)
        dx, dobs = run_inputs(
            me, w_early, w_late, g1_front, g1_back, dskip, dmod_front, dmod_back, slope, lens, width
        )
        a_got, b_got, small_got, late_got, dx, dobs = tie(a_got, b_got, small_got, late_got, dx, dobs)
        late, late_send = parts(late, late_got)
        late_got = z_high(late_send)
        (a, a_send), (b, b_send), small = parts(a, a_got), parts(b, b_got), small + small_got
        a_got, b_got = along_y(a_send), along_x(b_send)
        skip_out = windows_first(skip)
        a_got, b_got, skip_out, small = tie(a_got, b_got, skip_out, small)
        early, early_send = parts(jnp.concatenate([a + a_got, b + b_got], axis=1))
        early_got, small_got = z_low(early_send), along_y(small)
        down_out = windows_first(down_front, down_back)
        early_got, small_got, down_out, dobs = tie(early_got, small_got, down_out, dobs)
        early, early_send = parts(early, early_got)
        early_got = z_high(early_send)
        dobs, dobs_send = parts(dobs)
        dobs_got = along_x(dobs_send)
        small = small + small_got
        early_got, late_got = tie(early_got, late_got)
        grads = join_order((early + early_got)[0], (late + late_got)[0])

        spread = jnp.take(grads, jnp.maximum(block_of, 0), axis=0, mode="clip").reshape(dp_count, slot_count, 16, 128)
        spread, dx, small = tie(spread, dx, small)
        owned = lax.all_to_all(spread, "dp", 0, 0)
        small_got = z_low(small)
        actions_grad = windows_first(dx)
        owned, actions_grad = tie(owned, actions_grad)
        places = me[1] ^ jnp.arange(4, dtype=jnp.int32)
        state = (master, moment_one, moment_two)
        x_got, core_got = along_x(owned), core(owned)
        made = run_adamw(places[0:1], used, owned[None], *state)
        core_got, small, small_got, dobs, dobs_got, *made = tie(core_got, small, small_got, dobs, dobs_got, *made)
        small = small + small_got
        small_got = z_high(small)
        dobs, dobs_send = parts(dobs, dobs_got)
        dobs_got = core(dobs_send)
        made = run_adamw(places[1:2], used, core_got[None], *state, made)
        x_got, small_got, dobs_got, *made = tie(x_got, small_got, dobs_got, *made)
        core_got = core(x_got)
        grad_small = small + small_got
        observations_grad = (dobs + dobs_got).reshape(observations.shape)
        made = run_adamw(places[2:3], used, x_got[None], *state, made)
        core_got, *made = tie(core_got, *made)
        new_one, new_two, new_master = run_adamw(places[3:4], used, core_got[None], *state, made)
    else:
        g1_front, dmod_front, down_front, gs_front = third(g2, skip, *rest, 0, half)
        g1_back, dmod_back, down_back, gs_back = third(g2, skip, *rest, half, count // width - half)
        early_grads = run_early_grads(me, x, g1_front, g1_back, cond, dmod_front, dmod_back, width)
        dx, dobs = run_inputs(
            me, w_early, w_late, g1_front, g1_back, dskip, dmod_front, dmod_back, slope, lens, width
        )
        skip_out, down_out, actions_grad = windows_first(skip), windows_first(down_front, down_back), windows_first(dx)
        small = jnp.concatenate([(gs_front + gs_back)[0:5], gs_late[0:5]], axis=0)
        grad_small = sum_all(small)
        observations_grad = lax.psum_scatter(dobs, "pair", scatter_dimension=0).reshape(observations.shape)
        grads = join_order(from_lists(early_grads), from_lists(late_grads))
        rows = grads.reshape(-1, 4, 32, C).transpose(1, 0, 2, 3)
        rows = lax.psum_scatter(rows, "pair", scatter_dimension=0)
        spread = jnp.take(rows, jnp.maximum(block_of, 0), axis=0)
        owned = lax.psum_scatter(spread, "dp", scatter_dimension=0, tiled=True)
        owned = lax.all_gather(owned, "pair", axis=1, tiled=True)
        cut = pieces_of(owned).transpose(1, 0, 2, 3, 4)
        places = jnp.arange(4, dtype=jnp.int32)
        new_one, new_two, new_master = run_adamw(places, used, cut, master, moment_one, moment_two)
    small_first, small_second, new_small = adamw(
        small_master, small_one, small_two, grad_small, RATE_SMALL
    )
    return (
        skip_out,
        down_out,
        actions_grad,
        observations_grad,
        new_one,
        new_two,
        new_master,
        small_first,
        small_second,
        new_small,
    )


def solution(mesh):
    placed = (
        P(None, ("dp", "pair"), None, None),
        P(None, "dp", "pair"),
        P(None, ("dp", "pair")),
        P(None, ("dp", "pair")),
        P(None, ("dp", "pair"), None, None),
        P(None, ("dp", "pair"), None, None),
        P(),
        P("dp", None, None),
        P("dp", None, None),
        P("dp", None, None),
        P(),
        P(),
        P(),
    )
    return jax.shard_map(
        body,
        mesh=mesh,
        in_specs=placed,
        out_specs=(
            P(None, ("dp", "pair"), None, None),
            P(None, ("dp", "pair"), None, None),
            P(None, ("dp", "pair"), None, None),
            P(None, "dp", "pair"),
            P("dp", None, None),
            P("dp", None, None),
            P("dp", None, None),
            P(),
            P(),
            P(),
        ),
        check_vma=False,
    )
```

```python
import functools
import math

import jax
import jax.numpy as jnp
from jax import lax
from jax.experimental.layout import Layout, with_layout_constraint
from jax.experimental import pallas as pl
from jax.experimental.pallas import tpu as pltpu
from jax.sharding import PartitionSpec as P

CI = 256
C = 512
TE = 128
KW = 5
H = 16
HD = 8
KD = 3
NSMALL = 10
STEP = 10
BLK = 128
COND = 1152
NBLK = 62
GC = 64
LEAST = 4

FIRST_N, SECOND_N, RES_N, DOWN_N, FILM_N = 10, 20, 2, 12, 9
EARLY_N = FIRST_N + 2 * FILM_N
LATE_N = SECOND_N + RES_N + DOWN_N
DOWN_IN = SECOND_N + RES_N
PIECES = 32

BETA_ONE = 0.9
BETA_TWO = 0.999
EPS_ADAM = 1e-08
DECAY = 0.01
RATE_MATRIX = 0.1
RATE_SMALL = 1.0

F32 = jnp.float32
BF = jnp.bfloat16
NT = (((1,), (1,)), ((), ()))
TN = (((0,), (0,)), ((), ()))
MIB = 2**20
VMEM_LIMITS = dict(first=48, second=40, third=24, early_grads=20, inputs=18, adamw=56)


def mish(value):
    return value * jnp.tanh(jax.nn.softplus(value))


def time_embed(step_ids, width):
    half = width // 2
    freq = jnp.exp(-math.log(10000.0) * jnp.arange(half, dtype=F32) / (half - 1))
    angle = step_ids.astype(F32)[:, None] * freq[None, :]
    return jnp.concatenate([jnp.sin(angle), jnp.cos(angle)], axis=1)


def slot_of(owners, slot_count):
    same = owners[:, None] == owners[None, :]
    order = jnp.arange(owners.shape[0], dtype=jnp.int32)
    earlier = order[:, None] > order[None, :]
    rank = jnp.sum((same & earlier).astype(jnp.int32), axis=1)
    return owners * slot_count + rank


def adamw(weight, first_m, second_m, grad, rate):
    first_new = BETA_ONE * first_m + (1.0 - BETA_ONE) * grad
    second_new = BETA_TWO * second_m + (1.0 - BETA_TWO) * grad * grad
    fix_one = 1.0 - BETA_ONE**STEP
    fix_two = 1.0 - BETA_TWO**STEP
    update = first_new / fix_one / (jnp.sqrt(second_new / fix_two) + EPS_ADAM) + DECAY * weight
    return (first_new, second_new, weight - rate * update)


def keep(lens, t, value):
    return value if t < LEAST else jnp.where(lens > t, value, 0.0)


def mish_parts(v):
    w = jnp.exp(jnp.minimum(v, 30.0))
    n = w * (w + 2.0)
    return w, n, pl.reciprocal(n + 2.0, approx=True)


def mish_only(v):
    _, n, r = mish_parts(v)
    return v * (n * r)


def mish_both(v):
    w, n, r = mish_parts(v)
    t = n * r
    return v * t, t + (4.0 * v) * (((n - w) * r) * r)


def group_sum(value):
    low_half = lax.broadcasted_iota(jnp.int32, value.shape, 1) < GC
    zero = jnp.zeros_like(value)
    left = jnp.sum(jnp.where(low_half, value, zero), axis=1, keepdims=True)
    right = jnp.sum(jnp.where(low_half, zero, value), axis=1, keepdims=True)
    return jnp.where(low_half, left, right)


def lanes(q):
    return slice(q * 128, (q + 1) * 128)


def flips_of(k):
    return (k >> 3) & 1, (k >> 2) & 1, (k >> 1) & 1, k & 1


def place(me, k, by_y_first, core):
    one, two, z_low, z_high = flips_of(k)
    y, x = (one, two) if by_y_first else (two, one)
    return me[0] ^ (z_high * 4 + z_low * 2 + y), me[1] ^ (x * 2 + core)


def fetch(me, sources, dst, sem):
    at = 0
    for by_y_first, pair in ((False, sources[:2]), (True, sources[2:])):
        count = pair[0].shape[1]
        for core, source in enumerate(pair):
            for k in range(16):
                row, col = place(me, k, by_y_first, core)
                pltpu.make_async_copy(
                    source.at[k],
                    dst.at[at : at + count, row, :, pl.ds(pl.multiple_of(col * 128, 128), 128)],
                    sem,
                ).start()
        at = at + count
    return pltpu.make_async_copy(dst, dst, sem)


def store_pieces(me, acc, outs, base=0):
    at = 0
    for by_y_first, pair in ((False, outs[:2]), (True, outs[2:])):
        count = pair[0].shape[1]

        def one_block(b, carry, at=at, by_y_first=by_y_first, pair=pair):
            for core, out in enumerate(pair):
                for k in range(16):
                    row, col = place(me, k, by_y_first, core)
                    rows = pl.ds(pl.multiple_of((at + b) * BLK + row * 16, 16), 16)
                    cols = pl.ds(pl.multiple_of(col * 128, 128), 128)
                    out[k, b] = acc[rows, cols].astype(BF)
            return carry

        lax.fori_loop(0, count, one_block, 0)
        at = at + count


def matrix(ref, at, count):
    return ref[at : at + count].reshape(count * BLK, C)


def first_kernel(me, pa, pb, pc, pd, x_ref, cond_ref, lens_ref, inv_ref, small_ref, fst, mean_ref, rstd_ref, hid_ref,
                 mod_ref, w_out, w_one, xp, sem):
    step = pl.program_id(0)
    frames, width, _ = x_ref.shape
    rows = frames * width

    @pl.when(step == 0)
    def _():
        arrival = fetch((me[0], me[1]), (pa, pb, pc, pd), w_one, sem.at[0])
        xp[0:2] = jnp.zeros((2, width, CI), BF)
        xp[frames + 2 :] = jnp.zeros((2, width, CI), BF)
        arrival.wait()
        pltpu.make_async_copy(w_one, w_out, sem.at[1]).start()
        for k in range(2):
            mod_ref[k] = (
                jnp.dot(cond_ref[...], matrix(w_one, FIRST_N + k * FILM_N, FILM_N), preferred_element_type=F32)
                + small_ref[3 + k : 4 + k]
            )

    xp[2 : frames + 2] = x_ref[...]
    cut = C // 2
    for part in range(2):
        cs = slice(part * cut, (part + 1) * cut)
        total = small_ref[0:1, cs]
        for a in range(KW):
            total = total + jnp.dot(
                xp[a : a + frames].reshape(rows, CI),
                w_one[2 * a : 2 * a + 2, :, :, cs].reshape(CI, cut),
                preferred_element_type=F32,
            )
        fst[:, :, cs] = total.reshape(frames, width, cut)

    here = pl.ds(pl.multiple_of(step * width, width), width)
    lens = lens_ref[...]
    inv = inv_ref[...]
    for q in range(C // 128):
        ls = lanes(q)
        total = jnp.zeros((width, 128), F32)
        for t in range(frames):
            total = total + keep(lens, t, fst[t, :, ls])
        mean = group_sum(total) * inv
        total = jnp.zeros((width, 128), F32)
        for t in range(frames):
            centered = fst[t, :, ls] - mean
            total = total + keep(lens, t, centered * centered)
        rstd = lax.rsqrt(group_sum(total) * inv + 1e-05)
        mean_ref[:, ls] = mean
        rstd_ref[:, ls] = rstd
        slant = rstd * small_ref[1:2, ls]
        level = small_ref[2:3, ls] - mean * slant
        scale, shift = mod_ref[0, here, ls], mod_ref[1, here, ls]
        for t in range(frames):
            value = scale * mish_only(fst[t, :, ls] * slant + level) + shift
            hid_ref[t, :, ls] = keep(lens, t, value).astype(BF)

    @pl.when(step == pl.num_programs(0) - 1)
    def _():
        pltpu.make_async_copy(w_one, w_out, sem.at[1]).wait()


def second_kernel(me, pa, pb, pc, pd, hid_ref, x_ref, cs_ref, cd_ref, lens_ref, inv_ref, small_ref, skip_ref,
                  dskip_ref, g2_ref, ga, gb, gc, gd, gs_ref, w_out, w_two, hp, cdp, sec, br, dev, dod, se, so, acc,
                  sem):
    step = pl.program_id(0)
    last = pl.num_programs(0) - 1
    frames, width, _ = x_ref.shape
    half = frames // 2
    rows = frames * width

    @pl.when(step == 0)
    def _():
        arrival = fetch((me[0], me[1]), (pa, pb, pc, pd), w_two, sem.at[0])
        hp[0:2] = jnp.zeros((2, width, C), BF)
        hp[frames + 2 :] = jnp.zeros((2, width, C), BF)
        cdp[half:] = jnp.zeros((1, width, C), BF)
        so[0:1] = jnp.zeros((1, width, C), BF)
        acc[...] = jnp.zeros_like(acc)
        gs_ref[...] = jnp.zeros_like(gs_ref)
        arrival.wait()
        pltpu.make_async_copy(w_two, w_out, sem.at[1]).start()

    hp[2 : frames + 2] = hid_ref[...]
    cdp[0:half] = cd_ref[...]
    cot = cdp[0:half].reshape(half * width, C)
    cot_next = cdp[1 : half + 1].reshape(half * width, C)
    lens = lens_ref[...]
    inv = inv_ref[...]
    zero = jnp.zeros((width, 128), F32)
    cut = C // 2

    def columns(part):
        return slice(part * cut, (part + 1) * cut)

    def weight(at, count, part):
        return w_two[at : at + count, :, :, columns(part)].reshape(count * BLK, cut)

    def weight_rows(at, part):
        n = cut // BLK
        return matrix(w_two, at + part * n, n)

    def forward(part):
        cs = columns(part)
        dev[:, :, cs] = lax.dot_general(
            cot, weight_rows(DOWN_IN + 4, part), NT, preferred_element_type=F32
        ).reshape(half, width, cut)
        dod[:, :, cs] = (
            lax.dot_general(cot, weight_rows(DOWN_IN + 8, part), NT, preferred_element_type=F32)
            + lax.dot_general(cot_next, weight_rows(DOWN_IN, part), NT, preferred_element_type=F32)
        ).reshape(half, width, cut)
        br[:, :, cs] = (
            jnp.dot(x_ref[...].reshape(rows, CI), weight(SECOND_N, RES_N, part), preferred_element_type=F32)
            + small_ref[8:9, cs]
        ).reshape(frames, width, cut)
        total = jnp.dot(hp[0:frames].reshape(rows, C), weight(0, 4, part), preferred_element_type=F32)
        for a in range(1, KW):
            total = total + jnp.dot(
                hp[a : a + frames].reshape(rows, C), weight(4 * a, 4, part), preferred_element_type=F32
            )
        sec[:, :, cs] = (total + small_ref[5:6, cs]).reshape(frames, width, cut)

    def norm(q):
        ls = lanes(q)
        total = zero
        for t in range(frames):
            total = total + keep(lens, t, sec[t, :, ls])
        mean = group_sum(total) * inv
        total = zero
        for t in range(frames):
            centered = sec[t, :, ls] - mean
            total = total + keep(lens, t, centered * centered)
        rstd = lax.rsqrt(group_sum(total) * inv + 1e-05)
        gain = small_ref[6:7, ls]
        slant = rstd * gain
        level = small_ref[7:8, ls] - mean * slant
        sum_dy, sum_dyv, sum_ds = zero, zero, zero
        for t in range(frames):
            value = sec[t, :, ls]
            act, slope = mish_both(value * slant + level)
            skip = (act + br[t, :, ls]).astype(BF)
            skip_ref[t, :, ls] = skip
            if t % 2:
                so[t // 2 + 1, :, ls] = skip
                back = dod[t // 2, :, ls]
            else:
                se[t // 2, :, ls] = skip
                back = dev[t // 2, :, ls]
            ds = (cs_ref[t, :, ls].astype(F32) + back).astype(BF)
            dskip_ref[t, :, ls] = ds
            ds = ds.astype(F32)
            sum_ds = sum_ds + ds
            dy = ds * slope
            br[t, :, ls] = dy
            sum_dy = sum_dy + dy
            sum_dyv = sum_dyv + dy * value
        sum_dyn = rstd * (sum_dyv - mean * sum_dy)
        tilt = (rstd * rstd) * (group_sum(sum_dyn * gain) * inv)
        base = rstd * (group_sum(sum_dy * gain) * inv) - mean * tilt
        sum_g, sum_cd = zero, zero
        for t in range(frames):
            grad = br[t, :, ls] * slant - keep(lens, t, base + sec[t, :, ls] * tilt)
            grad = grad.astype(BF)
            g2_ref[t, :, ls] = grad
            sum_g = sum_g + grad.astype(F32)
        for t in range(half):
            sum_cd = sum_cd + cd_ref[t, :, ls].astype(F32)
        for k, part in enumerate((sum_g, sum_dyn, sum_dy, sum_ds, sum_cd)):
            gs_ref[k : k + 1, ls] += jnp.sum(part, axis=0, keepdims=True)

    def gradients(part):
        cs = columns(part)
        grad_two = g2_ref[:, :, cs].reshape(rows, cut)
        for a in range(KW):
            acc[a * C : (a + 1) * C, cs] += lax.dot_general(
                hp[a : a + frames].reshape(rows, C), grad_two, TN, preferred_element_type=F32
            )
        at = KW * C
        acc[at : at + CI, cs] += lax.dot_general(
            x_ref[...].reshape(rows, CI), dskip_ref[:, :, cs].reshape(rows, cut), TN, preferred_element_type=F32
        )
        at = at + CI
        for a, source in enumerate((so.at[0:half], se, so.at[1 : half + 1])):
            low = at + a * C + part * cut
            acc[low : low + cut] += lax.dot_general(
                source[:, :, cs].reshape(half * width, cut), cot, TN, preferred_element_type=F32
            )

    per = (C // 128) // 2
    forward(0)
    for q in range(0 * per, 1 * per):
        norm(q)
    forward(1)
    gradients(0)
    for q in range(1 * per, 2 * per):
        norm(q)
    gradients(1)

    @pl.when(step == last)
    def _():
        store_pieces((me[0], me[1]), acc, (ga, gb, gc, gd))
        pltpu.make_async_copy(w_two, w_out, sem.at[1]).wait()


def third_kernel(w_hbm, g2_ref, skip_ref, first_ref, mean_ref, rstd_ref, mod_ref, lens_ref, inv_ref, small_ref,
                 g1_ref, dmod_ref, down_ref, gs_ref, w_two, gp, dh, se, so, sem):
    step = pl.program_id(0)
    frames, width, _ = g2_ref.shape
    rows = frames * width
    half = frames // 2

    @pl.when(step == 0)
    def _():
        arrival = pltpu.make_async_copy(w_hbm, w_two, sem.at[0])
        arrival.start()
        gp[0:2] = jnp.zeros((2, width, C), BF)
        gp[frames + 2 :] = jnp.zeros((2, width, C), BF)
        so[0:1] = jnp.zeros((1, width, C), BF)
        gs_ref[...] = jnp.zeros_like(gs_ref)
        arrival.wait()

    gp[2 : frames + 2] = g2_ref[...]
    cut = C // 2
    for part in range(2):
        total = jnp.zeros((rows, cut), F32)
        for a in range(KW):
            total = total + lax.dot_general(
                gp[4 - a : 4 - a + frames].reshape(rows, C),
                matrix(w_two, 4 * a + 2 * part, 2),
                NT,
                preferred_element_type=F32,
            )
        dh[:, :, part * cut : (part + 1) * cut] = total.reshape(frames, width, cut)
    for j in range(half):
        se[j] = skip_ref[2 * j]
        so[j + 1] = skip_ref[2 * j + 1]
    down = jnp.dot(so[0:half].reshape(half * width, C), matrix(w_two, DOWN_IN, 4), preferred_element_type=F32)
    down = down + jnp.dot(
        se[...].reshape(half * width, C), matrix(w_two, DOWN_IN + 4, 4), preferred_element_type=F32
    )
    down = down + jnp.dot(
        so[1 : half + 1].reshape(half * width, C), matrix(w_two, DOWN_IN + 8, 4), preferred_element_type=F32
    )
    down_ref[...] = (down + small_ref[9:10]).astype(BF).reshape(half, width, C)

    lens = lens_ref[...]
    inv = inv_ref[...]
    zero = jnp.zeros((width, 128), F32)
    for q in range(C // 128):
        ls = lanes(q)
        gain = small_ref[1:2, ls]
        mean, rstd = mean_ref[:, ls], rstd_ref[:, ls]
        slant = rstd * gain
        level = small_ref[2:3, ls] - mean * slant
        scale = mod_ref[0, :, ls]
        sum_dy, sum_dyv, d_scale, d_shift = zero, zero, zero, zero
        for t in range(frames):
            value = first_ref[t, :, ls]
            act, slope = mish_both(value * slant + level)
            grad = keep(lens, t, dh[t, :, ls])
            d_scale = d_scale + grad * act
            d_shift = d_shift + grad
            dy = (grad * scale) * slope
            dh[t, :, ls] = dy
            sum_dy = sum_dy + dy
            sum_dyv = sum_dyv + dy * value
        sum_dyn = rstd * (sum_dyv - mean * sum_dy)
        tilt = (rstd * rstd) * (group_sum(sum_dyn * gain) * inv)
        base = rstd * (group_sum(sum_dy * gain) * inv) - mean * tilt
        sum_g = zero
        for t in range(frames):
            grad = dh[t, :, ls] * slant - keep(lens, t, base + first_ref[t, :, ls] * tilt)
            grad = grad.astype(BF)
            g1_ref[t, :, ls] = grad
            sum_g = sum_g + grad.astype(F32)
        d_scale, d_shift = d_scale.astype(BF), d_shift.astype(BF)
        dmod_ref[0, :, ls] = d_scale
        dmod_ref[1, :, ls] = d_shift
        for k, part in enumerate((sum_g, sum_dyn, sum_dy, d_scale.astype(F32), d_shift.astype(F32))):
            gs_ref[k : k + 1, ls] += jnp.sum(part, axis=0, keepdims=True)


def of_halves(step, half, front, back, dst):
    @pl.when(step < half)
    def _():
        dst[...] = front[...]

    @pl.when(step >= half)
    def _():
        dst[...] = back[...]


def early_grads_kernel(me, x_ref, front_ref, back_ref, cond_ref, dmod_front, dmod_back, ga, gb, gc, gd, xp, g1, acc):
    step = pl.program_id(0)
    steps = pl.num_programs(0)
    frames, width, _ = x_ref.shape
    rows = frames * width
    near = dmod_front.shape[1]

    @pl.when(step == 0)
    def _():
        xp[0:2] = jnp.zeros((2, width, CI), BF)
        xp[frames + 2 :] = jnp.zeros((2, width, CI), BF)
        acc[0 : KW * CI] = jnp.zeros((KW * CI, C), F32)
        for k in range(2):
            at = KW * CI + k * COND
            acc[at : at + COND] = lax.dot_general(
                cond_ref[0:near], dmod_front[k], TN, preferred_element_type=F32
            ) + lax.dot_general(cond_ref[near:], dmod_back[k], TN, preferred_element_type=F32)

    xp[2 : frames + 2] = x_ref[...]
    of_halves(step, near // width, front_ref, back_ref, g1)
    grad_one = g1[...].reshape(rows, C)
    for a in range(KW):
        acc[a * CI : (a + 1) * CI] += lax.dot_general(
            xp[a : a + frames].reshape(rows, CI), grad_one, TN, preferred_element_type=F32
        )

    @pl.when(step == steps - 1)
    def _():
        store_pieces((me[0], me[1]), acc, (ga, gb, gc, gd))


def inputs_kernel(me, w_early, w_late, front_ref, back_ref, dskip_ref, dmod_front, dmod_back, slope_ref, lens_ref,
                  dx_ref, dobs_ref, w_one, w_res, gp, sem):
    step = pl.program_id(0)
    steps = pl.num_programs(0)
    frames, width, _ = dskip_ref.shape
    rows = frames * width
    near = dmod_front.shape[1]

    @pl.when(step == 0)
    def _():
        early = pltpu.make_async_copy(w_early, w_one, sem.at[0])
        late = pltpu.make_async_copy(w_late.at[SECOND_N:DOWN_IN], w_res, sem.at[1])
        early.start()
        late.start()
        gp[0:2] = jnp.zeros((2, width, C), BF)
        gp[frames + 2 :] = jnp.zeros((2, width, C), BF)
        early.wait()
        late.wait()
        for r in range(4):
            at = FIRST_N + 1 + 2 * (me[1] ^ r)
            for dmod, low_at, high_at in ((dmod_front, 0, near), (dmod_back, near, cond_rows(slope_ref))):
                back = lax.dot_general(
                    dmod[0], w_one[pl.ds(at, 2)].reshape(2 * BLK, C), NT, preferred_element_type=F32
                ) + lax.dot_general(
                    dmod[1], w_one[pl.ds(at + FILM_N, 2)].reshape(2 * BLK, C), NT, preferred_element_type=F32
                )
                dobs_ref[r, low_at:high_at] = back * slope_ref[r, low_at:high_at]

    of_halves(step, near // width, front_ref, back_ref, gp.at[2 : frames + 2])
    total = lax.dot_general(
        dskip_ref[...].reshape(rows, C), matrix(w_res, 0, RES_N), NT, preferred_element_type=F32
    )
    for a in range(KW):
        total = total + lax.dot_general(
            gp[4 - a : 4 - a + frames].reshape(rows, C), matrix(w_one, 2 * a, 2), NT, preferred_element_type=F32
        )
    total = total.reshape(frames, width, CI)
    lens = lens_ref[...]
    for t in range(frames):
        for q in range(CI // 128):
            dx_ref[t, :, lanes(q)] = keep(lens, t, total[t, :, lanes(q)])


def cond_rows(slope_ref):
    return slope_ref.shape[1]


def adamw_kernel(places, used, one_piece, two_piece, master_ref, one_ref, two_ref, *rest):
    one_out, two_out, master_out, grad = rest[-4:]
    group = grad.shape[0]
    at = pl.program_id(1) * group

    def load(piece_ref):
        for slot in range(group):
            held = used[at + slot] > 0
            for row in range(8):
                piece = piece_ref[row, slot].astype(F32)
                grad[slot, row * 16 : row * 16 + 16] = jnp.where(held, piece, 0.0)

    @pl.when(pl.program_id(0) == 0)
    def _():
        load(one_piece)

    @pl.when(pl.program_id(0) == 1)
    def _():
        load(two_piece)

    one_out[...], two_out[...], master_out[...] = adamw(
        master_ref[...], one_ref[...], two_ref[...], grad[...], RATE_MATRIX
    )


def tiles(frames, width, channels):
    return pl.BlockSpec((frames, width, channels), lambda i, *_: (0, i, 0))


def rows_of(width, channels):
    return pl.BlockSpec((width, channels), lambda i, *_: (i, 0))


def whole(*shape):
    return pl.BlockSpec(shape, lambda i, *_: (0,) * len(shape), pipeline_mode=pl.Buffered(1))


ANY = pl.BlockSpec(memory_space=pl.ANY)


def weight_scratch(count):
    return pltpu.VMEM((count, 8, 16, C), BF)


def shape(*dims, dtype=F32):
    return jax.ShapeDtypeStruct(dims, dtype)


def half_lists(count):
    front = count // 2
    return [(16, n, 16, 128) for n in (front, front, count - front, count - front)]


def call(kernel, name, grid, scalars, ins, outs, scratch, operands, flops, aliases=None):
    return pl.pallas_call(
        kernel,
        grid_spec=pltpu.PrefetchScalarGridSpec(
            num_scalar_prefetch=scalars,
            grid=grid,
            in_specs=ins,
            out_specs=[spec for spec, _ in outs],
            scratch_shapes=scratch,
        ),
        out_shape=[made for _, made in outs],
        input_output_aliases=aliases or {},
        compiler_params=pltpu.CompilerParams(
            vmem_limit_bytes=VMEM_LIMITS[name] * MIB, dimension_semantics=("arbitrary",) * len(grid)
        ),
        cost_estimate=pl.CostEstimate(flops=flops, bytes_accessed=20 * 2**20, transcendentals=0),
        name=name,
    )(*operands)


def run_first(me, pieces, x, cond, lens, inv, small, width):
    count = x.shape[1]
    return call(
        first_kernel, "first", (count // width,), 1,
        [ANY] * 4 + [tiles(H, width, CI), whole(count, COND), rows_of(width, 128), rows_of(width, 128),
                     whole(NSMALL, C)],
        [(tiles(H, width, C), shape(H, count, C)), (rows_of(width, C), shape(count, C)),
         (rows_of(width, C), shape(count, C)), (tiles(H, width, C), shape(H, count, C, dtype=BF)), (whole(2, count, C), shape(2, count, C)),
         (ANY, shape(EARLY_N, 8, 16, C, dtype=BF))],
        [weight_scratch(EARLY_N), pltpu.VMEM((H + 4, width, CI), BF), pltpu.SemaphoreType.DMA((2,))],
        (me, *pieces, x, cond, lens, inv, small),
        2 * count * H * KW * CI * C,
    )


def run_second(me, pieces, hid, x, cs, cd, lens, inv, small, width):
    count = x.shape[1]
    bf_tile = (tiles(H, width, C), shape(H, count, C, dtype=BF))
    return call(
        second_kernel, "second", (count // width,), 1,
        [ANY] * 4 + [tiles(H, width, C), tiles(H, width, CI), tiles(H, width, C), tiles(HD, width, C),
                     rows_of(width, 128), rows_of(width, 128), whole(NSMALL, C)],
        [bf_tile, bf_tile, bf_tile] + [(whole(*dims), shape(*dims, dtype=BF)) for dims in half_lists(LATE_N)]
        + [(whole(8, C), shape(8, C)), (ANY, shape(LATE_N, 8, 16, C, dtype=BF))],
        [weight_scratch(LATE_N), pltpu.VMEM((H + 4, width, C), BF), pltpu.VMEM((HD + 1, width, C), BF),
         pltpu.VMEM((H, width, C), F32), pltpu.VMEM((H, width, C), F32),
         pltpu.VMEM((HD, width, C), F32), pltpu.VMEM((HD, width, C), F32),
         pltpu.VMEM((HD, width, C), BF), pltpu.VMEM((HD + 1, width, C), BF),
         pltpu.VMEM((LATE_N * BLK, C), F32), pltpu.SemaphoreType.DMA((2,))],
        (me, *pieces, hid, x, cs, cd, lens, inv, small),
        6 * count * H * KW * C * C,
    )


def run_third(w_late, g2, skip, first, mean, rstd, mod, lens, inv, small, width, tiles_at, tiles_n):
    count = tiles_n * width

    def part(frames, channels):
        return pl.BlockSpec((frames, width, channels), lambda i: (0, i + tiles_at, 0))

    def part_rows(channels):
        return pl.BlockSpec((width, channels), lambda i: (i + tiles_at, 0))

    return call(
        third_kernel, "third", (tiles_n,), 0,
        [ANY, part(H, C), part(H, C), part(H, C), part_rows(C), part_rows(C), part(2, C), part_rows(128), part_rows(128), whole(NSMALL, C)],
        [(tiles(H, width, C), shape(H, count, C, dtype=BF)), (tiles(2, width, C), shape(2, count, C, dtype=BF)),
         (tiles(HD, width, C), shape(HD, count, C, dtype=BF)), (whole(8, C), shape(8, C))],
        [weight_scratch(LATE_N), pltpu.VMEM((H + 4, width, C), BF), pltpu.VMEM((H, width, C), F32),
         pltpu.VMEM((HD, width, C), BF), pltpu.VMEM((HD + 1, width, C), BF), pltpu.SemaphoreType.DMA((1,))],
        (w_late, g2, skip, first, mean, rstd, mod, lens, inv, small),
        4 * count * H * KW * C * C,
    )


def front_tiles(width, channels, half):
    return pl.BlockSpec((H, width, channels), lambda i, *_: (0, jnp.minimum(i, half - 1), 0))


def back_tiles(width, channels, half):
    return pl.BlockSpec((H, width, channels), lambda i, *_: (0, jnp.maximum(i - half, 0), 0))


def run_early_grads(me, x, front, back, cond, dmod_front, dmod_back, width):
    count = x.shape[1]
    steps = count // width
    half = front.shape[1]
    return call(
        early_grads_kernel, "early_grads", (steps,), 1,
        [tiles(H, width, CI), front_tiles(width, C, half // width), back_tiles(width, C, half // width), whole(count, COND),
         whole(2, half, C), whole(2, count - half, C)],
        [(whole(*dims), shape(*dims, dtype=BF)) for dims in half_lists(EARLY_N)],
        [pltpu.VMEM((H + 4, width, CI), BF), pltpu.VMEM((H, width, C), BF), pltpu.VMEM((EARLY_N * BLK, C), F32)],
        (me, x, front, back, cond, dmod_front, dmod_back),
        2 * count * H * KW * CI * C,
    )


def run_inputs(me, w_early, w_late, front, back, dskip, dmod_front, dmod_back, slope, lens, width):
    count = dskip.shape[1]
    steps = count // width
    half = front.shape[1]
    return call(
        inputs_kernel, "inputs", (steps,), 1,
        [ANY, ANY, front_tiles(width, C, half // width), back_tiles(width, C, half // width), tiles(H, width, C),
         whole(2, half, C), whole(2, count - half, C), whole(*slope.shape), rows_of(width, 128)],
        [(tiles(H, width, CI), shape(H, count, CI)), (whole(*slope.shape), shape(*slope.shape))],
        [weight_scratch(EARLY_N), weight_scratch(RES_N), pltpu.VMEM((H + 4, width, C), BF),
         pltpu.SemaphoreType.DMA((2,))],
        (me, w_early, w_late, front, back, dskip, dmod_front, dmod_back, slope, lens),
        2 * count * H * (KW + 1) * CI * C,
    )


def run_adamw(places, used, pieces, master, one, two, made=None):
    slots = master.shape[0]
    group = min(slots, 8)
    block = pl.BlockSpec((group, BLK, 128), lambda k, i, places, used: (i, 0, places[k]))
    piece = pl.BlockSpec((8, group, 16, 128), lambda k, i, *_: (0, i, 0, 0))
    kept = list(made) if made else []
    return call(
        adamw_kernel, "adamw", (2, slots // group), 2,
        [piece, piece, block, block, block] + [ANY] * len(kept),
        [(block, shape(slots, BLK, C))] * 3,
        [pltpu.VMEM((group, BLK, 128), F32)],
        (places, used, *pieces, master, one, two, *kept),
        10 * slots * BLK * C,
        {7 + k: k for k in range(len(kept))},
    )


def prepare(actions, features, order, tsteps, lengths, cot_skip, cot_down):
    micro, samp = lengths.shape
    count = micro * samp
    lens_flat = lengths.reshape(count)
    lens = jnp.broadcast_to(lens_flat.astype(F32)[:, None], (count, 128))
    inv = 1.0 / (lens * GC)
    valid = jnp.arange(H)[:, None, None] < lens_flat[None, :, None]
    x = jnp.where(valid, actions.reshape(count, H, CI).transpose(1, 0, 2), jnp.zeros((), BF))
    cs = cot_skip.reshape(count, H, C).transpose(1, 0, 2)
    cd = cot_down.reshape(count, HD, C).transpose(1, 0, 2)
    obs = features.astype(F32)
    obs_act, obs_back = jax.vjp(mish, obs)
    slope = obs_back(jnp.ones_like(obs))[0]
    obs_act = jnp.take(obs_act.astype(BF), order, axis=0).transpose(1, 0, 2).reshape(count, -1)
    cond = jnp.concatenate([mish(time_embed(tsteps.reshape(count), TE)).astype(BF), obs_act], axis=1)
    return x, cs, cd, lens, inv, cond, slope


def flip(value, axis, bit):
    size = lax.axis_size(axis)
    return lax.ppermute(value, axis, [(i, i ^ bit) for i in range(size)])


def core(value):
    return flip(value, "pair", 1)


def along_x(value):
    return flip(value, "pair", 2)


def along_y(value):
    return flip(value, "dp", 1)


def z_low(value):
    return flip(value, "dp", 2)


def z_high(value):
    return flip(value, "dp", 4)


def pieces_of(block):
    return block.reshape(-1, 8, 16, 4, 128).transpose(1, 3, 0, 2, 4)


def double(value, hop):
    return jnp.concatenate([value, hop(value)], axis=0)


def tie(*values):
    return lax.optimization_barrier(values)


def after(value, *others):
    return tie(value, *others)[0]


def gather_lists(early, late):
    def halves(value):
        front = value.shape[1] // 2
        return value[:, :front], value[:, front:]

    early = double(early[None], z_high)
    late = double(after(late[None], early), z_high)
    early = double(early, z_low)
    late = double(after(late, early), z_low)
    a, b = halves(early)
    a, b = double(a, along_y), double(b, along_x)
    c, d = halves(after(late, a, b))
    a, b = double(a, along_x), double(b, along_y)
    c, d = double(c, along_y), double(d, along_x)
    return (a, b), (c, d)


def parts(own, received=None):
    size = own.shape[0] // 2
    if received is None:
        return own[:size], own[size:]
    return own[:size] + received[:size], own[size:] + received[size:]


def sum_all(value):
    for axis in ("pair", "dp"):
        bit = 1
        while bit < lax.axis_size(axis):
            value = value + flip(value, axis, bit)
            bit = bit * 2
    return value


def split_order(blocks):
    return jnp.concatenate([blocks[:FIRST_N], blocks[FIRST_N + LATE_N :]], axis=0), blocks[FIRST_N : FIRST_N + LATE_N]


def join_order(early, late):
    return jnp.concatenate([early[:FIRST_N], late, early[FIRST_N:]], axis=0)


def as_lists(blocks):
    front = blocks.shape[0] // 2
    found = []
    for by_y_first, part in ((False, blocks[:front]), (True, blocks[front:])):
        cut = pieces_of(part)
        for core_bit in range(2):
            found.append(jnp.stack([cut[place((0, 0), k, by_y_first, core_bit)] for k in range(16)]))
    return tuple(found)


def from_lists(lists):
    parts = []
    for by_y_first, pair in ((False, lists[:2]), (True, lists[2:])):
        table = {}
        for core_bit, part in enumerate(pair):
            for k in range(16):
                table[place((0, 0), k, by_y_first, core_bit)] = part[k]
        cut = jnp.stack([jnp.stack([table[(row, col)] for col in range(4)]) for row in range(8)])
        parts.append(cut.transpose(2, 0, 3, 1, 4).reshape(-1, BLK, C))
    return jnp.concatenate(parts, axis=0)


def body(
    actions,
    observations,
    tsteps,
    lengths,
    cot_skip,
    cot_down,
    owners,
    master,
    moment_one,
    moment_two,
    small_master,
    small_one,
    small_two,
):
    micro, samp = lengths.shape
    slot_count = master.shape[0]
    dp_count = lax.axis_size("dp")
    slots_all = dp_count * slot_count
    me_pair = lax.axis_index("pair")
    me_dp = lax.axis_index("dp")
    by_pieces = dp_count == 8 and lax.axis_size("pair") == 4
    slot_index = slot_of(owners, slot_count)
    block_of = (
        jnp.full((slots_all,), -1, jnp.int32).at[slot_index].set(jnp.arange(NBLK, dtype=jnp.int32))
    )
    used = (lax.dynamic_slice_in_dim(block_of, me_dp * slot_count, slot_count, axis=0) >= 0).astype(jnp.int32)
    here = jnp.stack([me_dp, me_pair]).astype(jnp.int32)
    if by_pieces:
        me = here
        columns = lax.dynamic_slice_in_dim(master, me_pair * 128, 128, axis=2).astype(BF)
        columns = columns.reshape(slot_count, 8, 16, 128).transpose(1, 0, 2, 3)
        slots = lax.all_to_all(columns, "dp", 0, 0).reshape(slots_all, 16, 128)
        early_index, late_index = split_order(slot_index)
        quarters = double(observations.reshape(1, micro * samp, -1), along_x)
        quarters = double(after(quarters, slots), core)
        (a, b), (c, d) = gather_lists(
            jnp.take(slots, early_index, axis=0, mode="clip"), jnp.take(slots, late_index, axis=0, mode="clip")
        )
        features = quarters[jnp.array([0, 2, 1, 3])]
    else:
        me = jnp.zeros_like(here)
        quarter = lax.dynamic_slice_in_dim(master, me_pair * 32, 32, axis=1).astype(BF)
        slots = lax.all_gather(quarter, "dp", axis=0, tiled=True)
        mine = jnp.take(slots, slot_index, axis=0)
        early, late = split_order(lax.all_gather(mine, "pair", axis=1, tiled=True))
        early_lists, late_lists = as_lists(early), as_lists(late)
        features = lax.all_gather(observations.reshape(micro * samp, -1), "pair", axis=0)


    order = jnp.arange(4, dtype=jnp.int32) ^ me[1]
    x, cs, cd, lens, inv, cond, slope = prepare(actions, features, order, tsteps, lengths, cot_skip, cot_down)
    count = micro * samp
    width = 64 if count % 64 == 0 else samp
    if by_pieces:
        a, b, x, cs, cd, lens, inv, cond, slope = tie(a, b, x, cs, cd, lens, inv, cond, slope)
        early_lists = (a, core(a), b, core(b))
        c, d = after(c, a), after(d, b)
        c_got, d_got = along_x(c), along_y(d)
    first, mean, rstd, hid, mod, w_early = run_first(me, early_lists, x, cond, lens, inv, small_master, width)
    if by_pieces:
        c_got, d_got, first, mean, rstd, hid, mod, w_early = tie(c_got, d_got, first, mean, rstd, hid, mod, w_early)
        c, d = jnp.concatenate([c, c_got], axis=0), jnp.concatenate([d, d_got], axis=0)
        late_lists = (c, core(c), d, core(d))
    skip, dskip, g2, *late_grads, gs_late, w_late = run_second(
        me, late_lists, hid, x, cs, cd, lens, inv, small_master, width
    )
    half = count // width // 2
    third = functools.partial(run_third, w_late)
    rest = (first, mean, rstd, mod, lens, inv, small_master, width)

    def windows_first(*values):
        whole_one = jnp.concatenate(values, axis=1) if len(values) > 1 else values[0]
        turned = whole_one.transpose(1, 0, 2).reshape(micro, samp, whole_one.shape[0], whole_one.shape[2])
        return with_layout_constraint(turned, Layout(major_to_minor=(0, 1, 2, 3)))

    if by_pieces:
        a, a_send, b, b_send = late_grads
        a_got, b_got = core(a_send), core(b_send)
        g1_front, dmod_front, down_front, gs_front = third(g2, skip, *rest, 0, half)
        a_got, b_got, g1_front, dmod_front, gs_front = tie(a_got, b_got, g1_front, dmod_front, gs_front)
        (a, a_send), (b, b_send) = parts(a, a_got), parts(b, b_got)
        a_send, b_send, g2_back, gs_front = tie(a_send, b_send, g2, gs_front)
        a_got, b_got = along_x(a_send), along_y(b_send)
        g1_back, dmod_back, down_back, gs_back = third(g2_back, skip, *rest, half, count // width - half)
        a_got, b_got, g1_back, dmod_back, gs_back = tie(a_got, b_got, g1_back, dmod_back, gs_back)
        (a, a_send), (b, b_send) = parts(a, a_got), parts(b, b_got)
        a_send, b_send, g1_back = tie(a_send, b_send, g1_back)
        a_got, b_got = along_y(a_send), along_x(b_send)
        early_grads = run_early_grads(me, x, g1_front, g1_back, cond, dmod_front, dmod_back, width)
        a_got, b_got, *early_grads = tie(a_got, b_got, *early_grads)
        late = jnp.concatenate([a + a_got, b + b_got], axis=1)

        small = jnp.concatenate([(gs_front + gs_back)[0:5], gs_late[0:5]], axis=0)
        a, a_send, b, b_send = early_grads
        late, late_send = parts(late)
        a_got, b_got, small_got, late_got = core(a_send), core(b_send), core(small), z_low(late_send)
        a_got, b_got, small_got = tie(a_got, b_got, small_got)
        (a, a_send), (b, b_send), small = parts(a, a_got), parts(b, b_got), small + small_got
        a_send, b_send, dskip = tie(a_send, b_send, dskip)
        a_got, b_got, small_got = along_x(a_send), along_y(b_send), along_x(small)
        dx, dobs = run_inputs(
            me, w_early, w_late, g1_front, g1_back, dskip, dmod_front, dmod_back, slope, lens, width
        )
        a_got, b_got, small_got, late_got, dx, dobs = tie(a_got, b_got, small_got, late_got, dx, dobs)
        late, late_send = parts(late, late_got)
        late_got = z_high(late_send)
        (a, a_send), (b, b_send), small = parts(a, a_got), parts(b, b_got), small + small_got
        a_got, b_got = along_y(a_send), along_x(b_send)
        skip_out = windows_first(skip)
        a_got, b_got, skip_out, small = tie(a_got, b_got, skip_out, small)
        early, early_send = parts(jnp.concatenate([a + a_got, b + b_got], axis=1))
        early_got, small_got = z_low(early_send), along_y(small)
        down_out = windows_first(down_front, down_back)
        early_got, small_got, down_out, dobs = tie(early_got, small_got, down_out, dobs)
        early, early_send = parts(early, early_got)
        early_got = z_high(early_send)
        dobs, dobs_send = parts(dobs)
        dobs_got = along_x(dobs_send)
        small = small + small_got
        early_got, late_got = tie(early_got, late_got)
        grads = join_order((early + early_got)[0], (late + late_got)[0])

        spread = jnp.take(grads, jnp.maximum(block_of, 0), axis=0, mode="clip").reshape(dp_count, slot_count, 16, 128)
        spread, dx, small = tie(spread, dx, small)
        owned = lax.all_to_all(spread, "dp", 0, 0)
        small_got = z_low(small)
        actions_grad = windows_first(dx)
        owned, actions_grad, small_got, dobs_got = tie(owned, actions_grad, small_got, dobs_got)
        places = me[1] ^ jnp.arange(4, dtype=jnp.int32)
        state = (master, moment_one, moment_two)
        x_got, core_got = along_x(owned), core(owned)
        small = small + small_got
        core_got, small, dobs, dobs_got = tie(core_got, small, dobs, dobs_got)
        small_got = z_high(small)
        dobs, dobs_send = parts(dobs, dobs_got)
        dobs_got = core(dobs_send)
        made = run_adamw(places[0:2], used, (owned, core_got), *state)
        x_got, small_got, dobs_got, *made = tie(x_got, small_got, dobs_got, *made)
        core_got = core(x_got)
        grad_small = small + small_got
        observations_grad = (dobs + dobs_got).reshape(observations.shape)
        new_one, new_two, new_master = run_adamw(places[2:4], used, (x_got, core_got), *state, made)
    else:
        g1_front, dmod_front, down_front, gs_front = third(g2, skip, *rest, 0, half)
        g1_back, dmod_back, down_back, gs_back = third(g2, skip, *rest, half, count // width - half)
        early_grads = run_early_grads(me, x, g1_front, g1_back, cond, dmod_front, dmod_back, width)
        dx, dobs = run_inputs(
            me, w_early, w_late, g1_front, g1_back, dskip, dmod_front, dmod_back, slope, lens, width
        )
        skip_out, down_out, actions_grad = windows_first(skip), windows_first(down_front, down_back), windows_first(dx)
        small = jnp.concatenate([(gs_front + gs_back)[0:5], gs_late[0:5]], axis=0)
        grad_small = sum_all(small)
        observations_grad = lax.psum_scatter(dobs, "pair", scatter_dimension=0).reshape(observations.shape)
        grads = join_order(from_lists(early_grads), from_lists(late_grads))
        rows = grads.reshape(-1, 4, 32, C).transpose(1, 0, 2, 3)
        rows = lax.psum_scatter(rows, "pair", scatter_dimension=0)
        spread = jnp.take(rows, jnp.maximum(block_of, 0), axis=0)
        owned = lax.psum_scatter(spread, "dp", scatter_dimension=0, tiled=True)
        owned = lax.all_gather(owned, "pair", axis=1, tiled=True)
        cut = pieces_of(owned).transpose(1, 0, 2, 3, 4)
        places = jnp.arange(4, dtype=jnp.int32)
        state = (master, moment_one, moment_two)
        made = run_adamw(places[0:2], used, (cut[0], cut[1]), *state)
        new_one, new_two, new_master = run_adamw(places[2:4], used, (cut[2], cut[3]), *state, made)
    small_first, small_second, new_small = adamw(
        small_master, small_one, small_two, grad_small, RATE_SMALL
    )
    return (
        skip_out,
        down_out,
        actions_grad,
        observations_grad,
        new_one,
        new_two,
        new_master,
        small_first,
        small_second,
        new_small,
    )


def solution(mesh):
    placed = (
        P(None, ("dp", "pair"), None, None),
        P(None, "dp", "pair"),
        P(None, ("dp", "pair")),
        P(None, ("dp", "pair")),
        P(None, ("dp", "pair"), None, None),
        P(None, ("dp", "pair"), None, None),
        P(),
        P("dp", None, None),
        P("dp", None, None),
        P("dp", None, None),
        P(),
        P(),
        P(),
    )
    return jax.shard_map(
        body,
        mesh=mesh,
        in_specs=placed,
        out_specs=(
            P(None, ("dp", "pair"), None, None),
            P(None, ("dp", "pair"), None, None),
            P(None, ("dp", "pair"), None, None),
            P(None, "dp", "pair"),
            P("dp", None, None),
            P("dp", None, None),
            P("dp", None, None),
            P(),
            P(),
            P(),
        ),
        check_vma=False,
    )
```

```python
import functools
import math

import jax
import jax.numpy as jnp
from jax import lax
from jax.experimental.layout import Layout, with_layout_constraint
from jax.experimental import pallas as pl
from jax.experimental.pallas import tpu as pltpu
from jax.sharding import PartitionSpec as P

CI = 256
C = 512
TE = 128
KW = 5
H = 16
HD = 8
KD = 3
NSMALL = 10
STEP = 10
BLK = 128
COND = 1152
NBLK = 62
GC = 64
LEAST = 4

FIRST_N, SECOND_N, RES_N, DOWN_N, FILM_N = 10, 20, 2, 12, 9
EARLY_N = FIRST_N + 2 * FILM_N
LATE_N = SECOND_N + RES_N + DOWN_N
DOWN_IN = SECOND_N + RES_N
PIECES = 32

BETA_ONE = 0.9
BETA_TWO = 0.999
EPS_ADAM = 1e-08
DECAY = 0.01
RATE_MATRIX = 0.1
RATE_SMALL = 1.0

F32 = jnp.float32
BF = jnp.bfloat16
NT = (((1,), (1,)), ((), ()))
TN = (((0,), (0,)), ((), ()))
MIB = 2**20
VMEM_LIMITS = dict(first=48, second=40, third=24, early_grads=20, inputs=18, adamw=56)


def mish(value):
    return value * jnp.tanh(jax.nn.softplus(value))


def time_embed(step_ids, width):
    half = width // 2
    freq = jnp.exp(-math.log(10000.0) * jnp.arange(half, dtype=F32) / (half - 1))
    angle = step_ids.astype(F32)[:, None] * freq[None, :]
    return jnp.concatenate([jnp.sin(angle), jnp.cos(angle)], axis=1)


def slot_of(owners, slot_count):
    same = owners[:, None] == owners[None, :]
    order = jnp.arange(owners.shape[0], dtype=jnp.int32)
    earlier = order[:, None] > order[None, :]
    rank = jnp.sum((same & earlier).astype(jnp.int32), axis=1)
    return owners * slot_count + rank


def adamw(weight, first_m, second_m, grad, rate):
    first_new = BETA_ONE * first_m + (1.0 - BETA_ONE) * grad
    second_new = BETA_TWO * second_m + (1.0 - BETA_TWO) * grad * grad
    fix_one = 1.0 - BETA_ONE**STEP
    fix_two = 1.0 - BETA_TWO**STEP
    update = first_new / fix_one / (jnp.sqrt(second_new / fix_two) + EPS_ADAM) + DECAY * weight
    return (first_new, second_new, weight - rate * update)


def keep(lens, t, value):
    return value if t < LEAST else jnp.where(lens > t, value, 0.0)


def mish_parts(v):
    w = jnp.exp(jnp.minimum(v, 30.0))
    n = w * (w + 2.0)
    return w, n, pl.reciprocal(n + 2.0, approx=True)


def mish_only(v):
    _, n, r = mish_parts(v)
    return v * (n * r)


def mish_both(v):
    w, n, r = mish_parts(v)
    t = n * r
    return v * t, t + (4.0 * v) * (((n - w) * r) * r)


def group_sum(value):
    low_half = lax.broadcasted_iota(jnp.int32, value.shape, 1) < GC
    zero = jnp.zeros_like(value)
    left = jnp.sum(jnp.where(low_half, value, zero), axis=1, keepdims=True)
    right = jnp.sum(jnp.where(low_half, zero, value), axis=1, keepdims=True)
    return jnp.where(low_half, left, right)


def lanes(q):
    return slice(q * 128, (q + 1) * 128)


def flips_of(k):
    return (k >> 3) & 1, (k >> 2) & 1, (k >> 1) & 1, k & 1


def place(me, k, by_y_first, core):
    one, two, z_low, z_high = flips_of(k)
    y, x = (one, two) if by_y_first else (two, one)
    return me[0] ^ (z_high * 4 + z_low * 2 + y), me[1] ^ (x * 2 + core)


def fetch(me, sources, dst, sem):
    at = 0
    for by_y_first, pair in ((False, sources[:2]), (True, sources[2:])):
        count = pair[0].shape[1]
        for core, source in enumerate(pair):
            for k in range(16):
                row, col = place(me, k, by_y_first, core)
                pltpu.make_async_copy(
                    source.at[k],
                    dst.at[at : at + count, row, :, pl.ds(pl.multiple_of(col * 128, 128), 128)],
                    sem,
                ).start()
        at = at + count
    return pltpu.make_async_copy(dst, dst, sem)


def store_pieces(me, acc, outs, base=0):
    at = 0
    for by_y_first, pair in ((False, outs[:2]), (True, outs[2:])):
        count = pair[0].shape[1]

        def one_block(b, carry, at=at, by_y_first=by_y_first, pair=pair):
            for core, out in enumerate(pair):
                for k in range(16):
                    row, col = place(me, k, by_y_first, core)
                    rows = pl.ds(pl.multiple_of((at + b) * BLK + row * 16, 16), 16)
                    cols = pl.ds(pl.multiple_of(col * 128, 128), 128)
                    out[k, b] = acc[rows, cols].astype(BF)
            return carry

        lax.fori_loop(0, count, one_block, 0)
        at = at + count


def matrix(ref, at, count):
    return ref[at : at + count].reshape(count * BLK, C)


def first_kernel(me, pa, pb, pc, pd, x_ref, cond_ref, lens_ref, inv_ref, small_ref, fst, mean_ref, rstd_ref, hid_ref,
                 mod_ref, w_out, w_one, xp, sem):
    step = pl.program_id(0)
    frames, width, _ = x_ref.shape
    rows = frames * width

    @pl.when(step == 0)
    def _():
        arrival = fetch((me[0], me[1]), (pa, pb, pc, pd), w_one, sem.at[0])
        xp[0:2] = jnp.zeros((2, width, CI), BF)
        xp[frames + 2 :] = jnp.zeros((2, width, CI), BF)
        arrival.wait()
        pltpu.make_async_copy(w_one, w_out, sem.at[1]).start()
        for k in range(2):
            mod_ref[k] = (
                jnp.dot(cond_ref[...], matrix(w_one, FIRST_N + k * FILM_N, FILM_N), preferred_element_type=F32)
                + small_ref[3 + k : 4 + k]
            )

    xp[2 : frames + 2] = x_ref[...]
    cut = C // 2
    for part in range(2):
        cs = slice(part * cut, (part + 1) * cut)
        total = small_ref[0:1, cs]
        for a in range(KW):
            total = total + jnp.dot(
                xp[a : a + frames].reshape(rows, CI),
                w_one[2 * a : 2 * a + 2, :, :, cs].reshape(CI, cut),
                preferred_element_type=F32,
            )
        fst[:, :, cs] = total.reshape(frames, width, cut)

    here = pl.ds(pl.multiple_of(step * width, width), width)
    lens = lens_ref[...]
    inv = inv_ref[...]
    for q in range(C // 128):
        ls = lanes(q)
        total = jnp.zeros((width, 128), F32)
        for t in range(frames):
            total = total + keep(lens, t, fst[t, :, ls])
        mean = group_sum(total) * inv
        total = jnp.zeros((width, 128), F32)
        for t in range(frames):
            centered = fst[t, :, ls] - mean
            total = total + keep(lens, t, centered * centered)
        rstd = lax.rsqrt(group_sum(total) * inv + 1e-05)
        mean_ref[:, ls] = mean
        rstd_ref[:, ls] = rstd
        slant = rstd * small_ref[1:2, ls]
        level = small_ref[2:3, ls] - mean * slant
        scale, shift = mod_ref[0, here, ls], mod_ref[1, here, ls]
        for t in range(frames):
            value = scale * mish_only(fst[t, :, ls] * slant + level) + shift
            hid_ref[t, :, ls] = keep(lens, t, value).astype(BF)

    @pl.when(step == pl.num_programs(0) - 1)
    def _():
        pltpu.make_async_copy(w_one, w_out, sem.at[1]).wait()


def second_kernel(me, pa, pb, pc, pd, hid_ref, x_ref, cs_ref, cd_ref, lens_ref, inv_ref, small_ref, skip_ref,
                  dskip_ref, g2_ref, ga, gb, gc, gd, gs_ref, w_out, w_two, hp, cdp, sec, br, dev, dod, se, so, acc,
                  sem):
    step = pl.program_id(0)
    last = pl.num_programs(0) - 1
    frames, width, _ = x_ref.shape
    half = frames // 2
    rows = frames * width

    @pl.when(step == 0)
    def _():
        arrival = fetch((me[0], me[1]), (pa, pb, pc, pd), w_two, sem.at[0])
        hp[0:2] = jnp.zeros((2, width, C), BF)
        hp[frames + 2 :] = jnp.zeros((2, width, C), BF)
        cdp[half:] = jnp.zeros((1, width, C), BF)
        so[0:1] = jnp.zeros((1, width, C), BF)
        acc[...] = jnp.zeros_like(acc)
        gs_ref[...] = jnp.zeros_like(gs_ref)
        arrival.wait()
        pltpu.make_async_copy(w_two, w_out, sem.at[1]).start()

    hp[2 : frames + 2] = hid_ref[...]
    cdp[0:half] = cd_ref[...]
    cot = cdp[0:half].reshape(half * width, C)
    cot_next = cdp[1 : half + 1].reshape(half * width, C)
    lens = lens_ref[...]
    inv = inv_ref[...]
    zero = jnp.zeros((width, 128), F32)
    cut = C // 2

    def columns(part):
        return slice(part * cut, (part + 1) * cut)

    def weight(at, count, part):
        return w_two[at : at + count, :, :, columns(part)].reshape(count * BLK, cut)

    def weight_rows(at, part):
        n = cut // BLK
        return matrix(w_two, at + part * n, n)

    def forward(part):
        cs = columns(part)
        dev[:, :, cs] = lax.dot_general(
            cot, weight_rows(DOWN_IN + 4, part), NT, preferred_element_type=F32
        ).reshape(half, width, cut)
        dod[:, :, cs] = (
            lax.dot_general(cot, weight_rows(DOWN_IN + 8, part), NT, preferred_element_type=F32)
            + lax.dot_general(cot_next, weight_rows(DOWN_IN, part), NT, preferred_element_type=F32)
        ).reshape(half, width, cut)
        br[:, :, cs] = (
            jnp.dot(x_ref[...].reshape(rows, CI), weight(SECOND_N, RES_N, part), preferred_element_type=F32)
            + small_ref[8:9, cs]
        ).reshape(frames, width, cut)
        total = jnp.dot(hp[0:frames].reshape(rows, C), weight(0, 4, part), preferred_element_type=F32)
        for a in range(1, KW):
            total = total + jnp.dot(
                hp[a : a + frames].reshape(rows, C), weight(4 * a, 4, part), preferred_element_type=F32
            )
        sec[:, :, cs] = (total + small_ref[5:6, cs]).reshape(frames, width, cut)

    def norm(q):
        ls = lanes(q)
        total = zero
        for t in range(frames):
            total = total + keep(lens, t, sec[t, :, ls])
        mean = group_sum(total) * inv
        total = zero
        for t in range(frames):
            centered = sec[t, :, ls] - mean
            total = total + keep(lens, t, centered * centered)
        rstd = lax.rsqrt(group_sum(total) * inv + 1e-05)
        gain = small_ref[6:7, ls]
        slant = rstd * gain
        level = small_ref[7:8, ls] - mean * slant
        sum_dy, sum_dyv, sum_ds = zero, zero, zero
        for t in range(frames):
            value = sec[t, :, ls]
            act, slope = mish_both(value * slant + level)
            skip = (act + br[t, :, ls]).astype(BF)
            skip_ref[t, :, ls] = skip
            if t % 2:
                so[t // 2 + 1, :, ls] = skip
                back = dod[t // 2, :, ls]
            else:
                se[t // 2, :, ls] = skip
                back = dev[t // 2, :, ls]
            ds = (cs_ref[t, :, ls].astype(F32) + back).astype(BF)
            dskip_ref[t, :, ls] = ds
            ds = ds.astype(F32)
            sum_ds = sum_ds + ds
            dy = ds * slope
            br[t, :, ls] = dy
            sum_dy = sum_dy + dy
            sum_dyv = sum_dyv + dy * value
        sum_dyn = rstd * (sum_dyv - mean * sum_dy)
        tilt = (rstd * rstd) * (group_sum(sum_dyn * gain) * inv)
        base = rstd * (group_sum(sum_dy * gain) * inv) - mean * tilt
        sum_g, sum_cd = zero, zero
        for t in range(frames):
            grad = br[t, :, ls] * slant - keep(lens, t, base + sec[t, :, ls] * tilt)
            grad = grad.astype(BF)
            g2_ref[t, :, ls] = grad
            sum_g = sum_g + grad.astype(F32)
        for t in range(half):
            sum_cd = sum_cd + cd_ref[t, :, ls].astype(F32)
        for k, part in enumerate((sum_g, sum_dyn, sum_dy, sum_ds, sum_cd)):
            gs_ref[k : k + 1, ls] += jnp.sum(part, axis=0, keepdims=True)

    def gradients(part):
        cs = columns(part)
        grad_two = g2_ref[:, :, cs].reshape(rows, cut)
        for a in range(KW):
            acc[a * C : (a + 1) * C, cs] += lax.dot_general(
                hp[a : a + frames].reshape(rows, C), grad_two, TN, preferred_element_type=F32
            )
        at = KW * C
        acc[at : at + CI, cs] += lax.dot_general(
            x_ref[...].reshape(rows, CI), dskip_ref[:, :, cs].reshape(rows, cut), TN, preferred_element_type=F32
        )
        at = at + CI
        for a, source in enumerate((so.at[0:half], se, so.at[1 : half + 1])):
            low = at + a * C + part * cut
            acc[low : low + cut] += lax.dot_general(
                source[:, :, cs].reshape(half * width, cut), cot, TN, preferred_element_type=F32
            )

    per = (C // 128) // 2
    forward(0)
    for q in range(0 * per, 1 * per):
        norm(q)
    forward(1)
    gradients(0)
    for q in range(1 * per, 2 * per):
        norm(q)
    gradients(1)

    @pl.when(step == last)
    def _():
        store_pieces((me[0], me[1]), acc, (ga, gb, gc, gd))
        pltpu.make_async_copy(w_two, w_out, sem.at[1]).wait()


def third_kernel(w_hbm, g2_ref, skip_ref, first_ref, mean_ref, rstd_ref, mod_ref, lens_ref, inv_ref, small_ref,
                 g1_ref, dmod_ref, down_ref, gs_ref, w_two, gp, dh, se, so, sem):
    step = pl.program_id(0)
    frames, width, _ = g2_ref.shape
    rows = frames * width
    half = frames // 2

    @pl.when(step == 0)
    def _():
        arrival = pltpu.make_async_copy(w_hbm, w_two, sem.at[0])
        arrival.start()
        gp[0:2] = jnp.zeros((2, width, C), BF)
        gp[frames + 2 :] = jnp.zeros((2, width, C), BF)
        so[0:1] = jnp.zeros((1, width, C), BF)
        gs_ref[...] = jnp.zeros_like(gs_ref)
        arrival.wait()

    gp[2 : frames + 2] = g2_ref[...]
    cut = C // 2
    for part in range(2):
        total = jnp.zeros((rows, cut), F32)
        for a in range(KW):
            total = total + lax.dot_general(
                gp[4 - a : 4 - a + frames].reshape(rows, C),
                matrix(w_two, 4 * a + 2 * part, 2),
                NT,
                preferred_element_type=F32,
            )
        dh[:, :, part * cut : (part + 1) * cut] = total.reshape(frames, width, cut)
    for j in range(half):
        se[j] = skip_ref[2 * j]
        so[j + 1] = skip_ref[2 * j + 1]
    down = jnp.dot(so[0:half].reshape(half * width, C), matrix(w_two, DOWN_IN, 4), preferred_element_type=F32)
    down = down + jnp.dot(
        se[...].reshape(half * width, C), matrix(w_two, DOWN_IN + 4, 4), preferred_element_type=F32
    )
    down = down + jnp.dot(
        so[1 : half + 1].reshape(half * width, C), matrix(w_two, DOWN_IN + 8, 4), preferred_element_type=F32
    )
    down_ref[...] = (down + small_ref[9:10]).astype(BF).reshape(half, width, C)

    lens = lens_ref[...]
    inv = inv_ref[...]
    zero = jnp.zeros((width, 128), F32)
    for q in range(C // 128):
        ls = lanes(q)
        gain = small_ref[1:2, ls]
        mean, rstd = mean_ref[:, ls], rstd_ref[:, ls]
        slant = rstd * gain
        level = small_ref[2:3, ls] - mean * slant
        scale = mod_ref[0, :, ls]
        sum_dy, sum_dyv, d_scale, d_shift = zero, zero, zero, zero
        for t in range(frames):
            value = first_ref[t, :, ls]
            act, slope = mish_both(value * slant + level)
            grad = keep(lens, t, dh[t, :, ls])
            d_scale = d_scale + grad * act
            d_shift = d_shift + grad
            dy = (grad * scale) * slope
            dh[t, :, ls] = dy
            sum_dy = sum_dy + dy
            sum_dyv = sum_dyv + dy * value
        sum_dyn = rstd * (sum_dyv - mean * sum_dy)
        tilt = (rstd * rstd) * (group_sum(sum_dyn * gain) * inv)
        base = rstd * (group_sum(sum_dy * gain) * inv) - mean * tilt
        sum_g = zero
        for t in range(frames):
            grad = dh[t, :, ls] * slant - keep(lens, t, base + first_ref[t, :, ls] * tilt)
            grad = grad.astype(BF)
            g1_ref[t, :, ls] = grad
            sum_g = sum_g + grad.astype(F32)
        d_scale, d_shift = d_scale.astype(BF), d_shift.astype(BF)
        dmod_ref[0, :, ls] = d_scale
        dmod_ref[1, :, ls] = d_shift
        for k, part in enumerate((sum_g, sum_dyn, sum_dy, d_scale.astype(F32), d_shift.astype(F32))):
            gs_ref[k : k + 1, ls] += jnp.sum(part, axis=0, keepdims=True)


def of_halves(step, half, front, back, dst):
    @pl.when(step < half)
    def _():
        dst[...] = front[...]

    @pl.when(step >= half)
    def _():
        dst[...] = back[...]


def early_grads_kernel(me, x_ref, front_ref, back_ref, cond_ref, dmod_front, dmod_back, ga, gb, gc, gd, xp, g1, acc):
    step = pl.program_id(0)
    steps = pl.num_programs(0)
    frames, width, _ = x_ref.shape
    rows = frames * width
    near = dmod_front.shape[1]

    @pl.when(step == 0)
    def _():
        xp[0:2] = jnp.zeros((2, width, CI), BF)
        xp[frames + 2 :] = jnp.zeros((2, width, CI), BF)
        acc[0 : KW * CI] = jnp.zeros((KW * CI, C), F32)
        for k in range(2):
            at = KW * CI + k * COND
            acc[at : at + COND] = lax.dot_general(
                cond_ref[0:near], dmod_front[k], TN, preferred_element_type=F32
            ) + lax.dot_general(cond_ref[near:], dmod_back[k], TN, preferred_element_type=F32)

    xp[2 : frames + 2] = x_ref[...]
    of_halves(step, near // width, front_ref, back_ref, g1)
    grad_one = g1[...].reshape(rows, C)
    for a in range(KW):
        acc[a * CI : (a + 1) * CI] += lax.dot_general(
            xp[a : a + frames].reshape(rows, CI), grad_one, TN, preferred_element_type=F32
        )

    @pl.when(step == steps - 1)
    def _():
        store_pieces((me[0], me[1]), acc, (ga, gb, gc, gd))


def inputs_kernel(me, w_early, w_late, front_ref, back_ref, dskip_ref, dmod_front, dmod_back, slope_ref, lens_ref,
                  dx_ref, dobs_ref, w_one, w_res, gp, sem):
    step = pl.program_id(0)
    steps = pl.num_programs(0)
    frames, width, _ = dskip_ref.shape
    rows = frames * width
    near = dmod_front.shape[1]

    @pl.when(step == 0)
    def _():
        early = pltpu.make_async_copy(w_early, w_one, sem.at[0])
        late = pltpu.make_async_copy(w_late.at[SECOND_N:DOWN_IN], w_res, sem.at[1])
        early.start()
        late.start()
        gp[0:2] = jnp.zeros((2, width, C), BF)
        gp[frames + 2 :] = jnp.zeros((2, width, C), BF)
        early.wait()
        late.wait()
        for r in range(4):
            at = FIRST_N + 1 + 2 * (me[1] ^ r)
            for dmod, low_at, high_at in ((dmod_front, 0, near), (dmod_back, near, cond_rows(slope_ref))):
                back = lax.dot_general(
                    dmod[0], w_one[pl.ds(at, 2)].reshape(2 * BLK, C), NT, preferred_element_type=F32
                ) + lax.dot_general(
                    dmod[1], w_one[pl.ds(at + FILM_N, 2)].reshape(2 * BLK, C), NT, preferred_element_type=F32
                )
                dobs_ref[r, low_at:high_at] = back * slope_ref[r, low_at:high_at]

    of_halves(step, near // width, front_ref, back_ref, gp.at[2 : frames + 2])
    total = lax.dot_general(
        dskip_ref[...].reshape(rows, C), matrix(w_res, 0, RES_N), NT, preferred_element_type=F32
    )
    for a in range(KW):
        total = total + lax.dot_general(
            gp[4 - a : 4 - a + frames].reshape(rows, C), matrix(w_one, 2 * a, 2), NT, preferred_element_type=F32
        )
    total = total.reshape(frames, width, CI)
    lens = lens_ref[...]
    for t in range(frames):
        for q in range(CI // 128):
            dx_ref[t, :, lanes(q)] = keep(lens, t, total[t, :, lanes(q)])


def cond_rows(slope_ref):
    return slope_ref.shape[1]


def adamw_kernel(places, used, one_piece, two_piece, master_ref, one_ref, two_ref, *rest):
    one_out, two_out, master_out, grad = rest[-4:]
    group = grad.shape[0]
    at = pl.program_id(1) * group

    def load(piece_ref):
        for slot in range(group):
            held = used[at + slot] > 0
            for row in range(8):
                piece = piece_ref[row, slot].astype(F32)
                grad[slot, row * 16 : row * 16 + 16] = jnp.where(held, piece, 0.0)

    @pl.when(pl.program_id(0) == 0)
    def _():
        load(one_piece)

    @pl.when(pl.program_id(0) == 1)
    def _():
        load(two_piece)

    one_out[...], two_out[...], master_out[...] = adamw(
        master_ref[...], one_ref[...], two_ref[...], grad[...], RATE_MATRIX
    )


def tiles(frames, width, channels):
    return pl.BlockSpec((frames, width, channels), lambda i, *_: (0, i, 0))


def rows_of(width, channels):
    return pl.BlockSpec((width, channels), lambda i, *_: (i, 0))


def whole(*shape):
    return pl.BlockSpec(shape, lambda i, *_: (0,) * len(shape), pipeline_mode=pl.Buffered(1))


ANY = pl.BlockSpec(memory_space=pl.ANY)


def weight_scratch(count):
    return pltpu.VMEM((count, 8, 16, C), BF)


def shape(*dims, dtype=F32):
    return jax.ShapeDtypeStruct(dims, dtype)


def half_lists(count):
    front = count // 2
    return [(16, n, 16, 128) for n in (front, front, count - front, count - front)]


def call(kernel, name, grid, scalars, ins, outs, scratch, operands, flops, aliases=None):
    return pl.pallas_call(
        kernel,
        grid_spec=pltpu.PrefetchScalarGridSpec(
            num_scalar_prefetch=scalars,
            grid=grid,
            in_specs=ins,
            out_specs=[spec for spec, _ in outs],
            scratch_shapes=scratch,
        ),
        out_shape=[made for _, made in outs],
        input_output_aliases=aliases or {},
        compiler_params=pltpu.CompilerParams(
            vmem_limit_bytes=VMEM_LIMITS[name] * MIB, dimension_semantics=("arbitrary",) * len(grid)
        ),
        cost_estimate=pl.CostEstimate(flops=flops, bytes_accessed=20 * 2**20, transcendentals=0),
        name=name,
    )(*operands)


def run_first(me, pieces, x, cond, lens, inv, small, width):
    count = x.shape[1]
    return call(
        first_kernel, "first", (count // width,), 1,
        [ANY] * 4 + [tiles(H, width, CI), whole(count, COND), rows_of(width, 128), rows_of(width, 128),
                     whole(NSMALL, C)],
        [(tiles(H, width, C), shape(H, count, C)), (rows_of(width, C), shape(count, C)),
         (rows_of(width, C), shape(count, C)), (tiles(H, width, C), shape(H, count, C, dtype=BF)), (whole(2, count, C), shape(2, count, C)),
         (ANY, shape(EARLY_N, 8, 16, C, dtype=BF))],
        [weight_scratch(EARLY_N), pltpu.VMEM((H + 4, width, CI), BF), pltpu.SemaphoreType.DMA((2,))],
        (me, *pieces, x, cond, lens, inv, small),
        2 * count * H * KW * CI * C,
    )


def run_second(me, pieces, hid, x, cs, cd, lens, inv, small, width):
    count = x.shape[1]
    bf_tile = (tiles(H, width, C), shape(H, count, C, dtype=BF))
    return call(
        second_kernel, "second", (count // width,), 1,
        [ANY] * 4 + [tiles(H, width, C), tiles(H, width, CI), tiles(H, width, C), tiles(HD, width, C),
                     rows_of(width, 128), rows_of(width, 128), whole(NSMALL, C)],
        [bf_tile, bf_tile, bf_tile] + [(whole(*dims), shape(*dims, dtype=BF)) for dims in half_lists(LATE_N)]
        + [(whole(8, C), shape(8, C)), (ANY, shape(LATE_N, 8, 16, C, dtype=BF))],
        [weight_scratch(LATE_N), pltpu.VMEM((H + 4, width, C), BF), pltpu.VMEM((HD + 1, width, C), BF),
         pltpu.VMEM((H, width, C), F32), pltpu.VMEM((H, width, C), F32),
         pltpu.VMEM((HD, width, C), F32), pltpu.VMEM((HD, width, C), F32),
         pltpu.VMEM((HD, width, C), BF), pltpu.VMEM((HD + 1, width, C), BF),
         pltpu.VMEM((LATE_N * BLK, C), F32), pltpu.SemaphoreType.DMA((2,))],
        (me, *pieces, hid, x, cs, cd, lens, inv, small),
        6 * count * H * KW * C * C,
    )


def run_third(w_late, g2, skip, first, mean, rstd, mod, lens, inv, small, width, tiles_at, tiles_n):
    count = tiles_n * width

    def part(frames, channels):
        return pl.BlockSpec((frames, width, channels), lambda i: (0, i + tiles_at, 0))

    def part_rows(channels):
        return pl.BlockSpec((width, channels), lambda i: (i + tiles_at, 0))

    return call(
        third_kernel, "third", (tiles_n,), 0,
        [ANY, part(H, C), part(H, C), part(H, C), part_rows(C), part_rows(C), part(2, C), part_rows(128), part_rows(128), whole(NSMALL, C)],
        [(tiles(H, width, C), shape(H, count, C, dtype=BF)), (tiles(2, width, C), shape(2, count, C, dtype=BF)),
         (tiles(HD, width, C), shape(HD, count, C, dtype=BF)), (whole(8, C), shape(8, C))],
        [weight_scratch(LATE_N), pltpu.VMEM((H + 4, width, C), BF), pltpu.VMEM((H, width, C), F32),
         pltpu.VMEM((HD, width, C), BF), pltpu.VMEM((HD + 1, width, C), BF), pltpu.SemaphoreType.DMA((1,))],
        (w_late, g2, skip, first, mean, rstd, mod, lens, inv, small),
        4 * count * H * KW * C * C,
    )


def front_tiles(width, channels, half):
    return pl.BlockSpec((H, width, channels), lambda i, *_: (0, jnp.minimum(i, half - 1), 0))


def back_tiles(width, channels, half):
    return pl.BlockSpec((H, width, channels), lambda i, *_: (0, jnp.maximum(i - half, 0), 0))


def run_early_grads(me, x, front, back, cond, dmod_front, dmod_back, width):
    count = x.shape[1]
    steps = count // width
    half = front.shape[1]
    return call(
        early_grads_kernel, "early_grads", (steps,), 1,
        [tiles(H, width, CI), front_tiles(width, C, half // width), back_tiles(width, C, half // width), whole(count, COND),
         whole(2, half, C), whole(2, count - half, C)],
        [(whole(*dims), shape(*dims, dtype=BF)) for dims in half_lists(EARLY_N)],
        [pltpu.VMEM((H + 4, width, CI), BF), pltpu.VMEM((H, width, C), BF), pltpu.VMEM((EARLY_N * BLK, C), F32)],
        (me, x, front, back, cond, dmod_front, dmod_back),
        2 * count * H * KW * CI * C,
    )


def run_inputs(me, w_early, w_late, front, back, dskip, dmod_front, dmod_back, slope, lens, width):
    count = dskip.shape[1]
    steps = count // width
    half = front.shape[1]
    return call(
        inputs_kernel, "inputs", (steps,), 1,
        [ANY, ANY, front_tiles(width, C, half // width), back_tiles(width, C, half // width), tiles(H, width, C),
         whole(2, half, C), whole(2, count - half, C), whole(*slope.shape), rows_of(width, 128)],
        [(tiles(H, width, CI), shape(H, count, CI)), (whole(*slope.shape), shape(*slope.shape))],
        [weight_scratch(EARLY_N), weight_scratch(RES_N), pltpu.VMEM((H + 4, width, C), BF),
         pltpu.SemaphoreType.DMA((2,))],
        (me, w_early, w_late, front, back, dskip, dmod_front, dmod_back, slope, lens),
        2 * count * H * (KW + 1) * CI * C,
    )


def run_adamw(places, used, pieces, master, one, two, made=None):
    slots = master.shape[0]
    group = min(slots, 8)
    block = pl.BlockSpec((group, BLK, 128), lambda k, i, places, used: (i, 0, places[k]))
    piece = pl.BlockSpec((8, group, 16, 128), lambda k, i, *_: (0, i, 0, 0))
    kept = list(made) if made else []
    return call(
        adamw_kernel, "adamw", (2, slots // group), 2,
        [piece, piece, block, block, block] + [ANY] * len(kept),
        [(block, shape(slots, BLK, C))] * 3,
        [pltpu.VMEM((group, BLK, 128), F32)],
        (places, used, *pieces, master, one, two, *kept),
        10 * slots * BLK * C,
        {7 + k: k for k in range(len(kept))},
    )


def prepare(actions, features, order, tsteps, lengths, cot_skip, cot_down):
    micro, samp = lengths.shape
    count = micro * samp
    lens_flat = lengths.reshape(count)
    lens = jnp.broadcast_to(lens_flat.astype(F32)[:, None], (count, 128))
    inv = 1.0 / (lens * GC)
    valid = jnp.arange(H)[:, None, None] < lens_flat[None, :, None]
    x = jnp.where(valid, actions.reshape(count, H, CI).transpose(1, 0, 2), jnp.zeros((), BF))
    cs = cot_skip.reshape(count, H, C).transpose(1, 0, 2)
    cd = cot_down.reshape(count, HD, C).transpose(1, 0, 2)
    obs = features.astype(F32)
    obs_act, obs_back = jax.vjp(mish, obs)
    slope = obs_back(jnp.ones_like(obs))[0]
    obs_act = jnp.take(obs_act.astype(BF), order, axis=0).transpose(1, 0, 2).reshape(count, -1)
    cond = jnp.concatenate([mish(time_embed(tsteps.reshape(count), TE)).astype(BF), obs_act], axis=1)
    return x, cs, cd, lens, inv, cond, slope


def flip(value, axis, bit):
    size = lax.axis_size(axis)
    return lax.ppermute(value, axis, [(i, i ^ bit) for i in range(size)])


def core(value):
    return flip(value, "pair", 1)


def along_x(value):
    return flip(value, "pair", 2)


def along_y(value):
    return flip(value, "dp", 1)


def z_low(value):
    return flip(value, "dp", 2)


def z_high(value):
    return flip(value, "dp", 4)


def pieces_of(block):
    return block.reshape(-1, 8, 16, 4, 128).transpose(1, 3, 0, 2, 4)


def double(value, hop):
    return jnp.concatenate([value, hop(value)], axis=0)


def tie(*values):
    return lax.optimization_barrier(values)


def after(value, *others):
    return tie(value, *others)[0]


def gather_lists(early, late):
    def halves(value):
        front = value.shape[1] // 2
        return value[:, :front], value[:, front:]

    early = double(early[None], z_high)
    late = double(after(late[None], early), z_high)
    early = double(early, z_low)
    late = double(after(late, early), z_low)
    a, b = halves(early)
    a, b = double(a, along_y), double(b, along_x)
    c, d = halves(after(late, a, b))
    a, b = double(a, along_x), double(b, along_y)
    c, d = double(c, along_y), double(d, along_x)
    return (a, b), (c, d)


def parts(own, received=None):
    size = own.shape[0] // 2
    if received is None:
        return own[:size], own[size:]
    return own[:size] + received[:size], own[size:] + received[size:]


def sum_all(value):
    for axis in ("pair", "dp"):
        bit = 1
        while bit < lax.axis_size(axis):
            value = value + flip(value, axis, bit)
            bit = bit * 2
    return value


def split_order(blocks):
    return jnp.concatenate([blocks[:FIRST_N], blocks[FIRST_N + LATE_N :]], axis=0), blocks[FIRST_N : FIRST_N + LATE_N]


def join_order(early, late):
    return jnp.concatenate([early[:FIRST_N], late, early[FIRST_N:]], axis=0)


def as_lists(blocks):
    front = blocks.shape[0] // 2
    found = []
    for by_y_first, part in ((False, blocks[:front]), (True, blocks[front:])):
        cut = pieces_of(part)
        for core_bit in range(2):
            found.append(jnp.stack([cut[place((0, 0), k, by_y_first, core_bit)] for k in range(16)]))
    return tuple(found)


def from_lists(lists):
    parts = []
    for by_y_first, pair in ((False, lists[:2]), (True, lists[2:])):
        table = {}
        for core_bit, part in enumerate(pair):
            for k in range(16):
                table[place((0, 0), k, by_y_first, core_bit)] = part[k]
        cut = jnp.stack([jnp.stack([table[(row, col)] for col in range(4)]) for row in range(8)])
        parts.append(cut.transpose(2, 0, 3, 1, 4).reshape(-1, BLK, C))
    return jnp.concatenate(parts, axis=0)


def body(
    actions,
    observations,
    tsteps,
    lengths,
    cot_skip,
    cot_down,
    owners,
    master,
    moment_one,
    moment_two,
    small_master,
    small_one,
    small_two,
):
    micro, samp = lengths.shape
    slot_count = master.shape[0]
    dp_count = lax.axis_size("dp")
    slots_all = dp_count * slot_count
    me_pair = lax.axis_index("pair")
    me_dp = lax.axis_index("dp")
    by_pieces = dp_count == 8 and lax.axis_size("pair") == 4
    slot_index = slot_of(owners, slot_count)
    block_of = (
        jnp.full((slots_all,), -1, jnp.int32).at[slot_index].set(jnp.arange(NBLK, dtype=jnp.int32))
    )
    used = (lax.dynamic_slice_in_dim(block_of, me_dp * slot_count, slot_count, axis=0) >= 0).astype(jnp.int32)
    here = jnp.stack([me_dp, me_pair]).astype(jnp.int32)
    if by_pieces:
        me = here
        columns = lax.dynamic_slice_in_dim(master, me_pair * 128, 128, axis=2).astype(BF)
        columns = columns.reshape(slot_count, 8, 16, 128).transpose(1, 0, 2, 3)
        slots = lax.all_to_all(columns, "dp", 0, 0).reshape(slots_all, 16, 128)
        early_index, late_index = split_order(slot_index)
        quarters = double(after(observations, columns).reshape(1, micro * samp, -1), along_x)
        quarters = double(after(quarters, slots), core)
        (a, b), (c, d) = gather_lists(
            jnp.take(slots, early_index, axis=0, mode="clip"), jnp.take(slots, late_index, axis=0, mode="clip")
        )
        features = quarters[jnp.array([0, 2, 1, 3])]
    else:
        me = jnp.zeros_like(here)
        quarter = lax.dynamic_slice_in_dim(master, me_pair * 32, 32, axis=1).astype(BF)
        slots = lax.all_gather(quarter, "dp", axis=0, tiled=True)
        mine = jnp.take(slots, slot_index, axis=0)
        early, late = split_order(lax.all_gather(mine, "pair", axis=1, tiled=True))
        early_lists, late_lists = as_lists(early), as_lists(late)
        features = lax.all_gather(observations.reshape(micro * samp, -1), "pair", axis=0)


    order = jnp.arange(4, dtype=jnp.int32) ^ me[1]
    x, cs, cd, lens, inv, cond, slope = prepare(actions, features, order, tsteps, lengths, cot_skip, cot_down)
    count = micro * samp
    width = 64 if count % 64 == 0 else samp
    if by_pieces:
        a, b, x, cs, cd, lens, inv, cond, slope = tie(a, b, x, cs, cd, lens, inv, cond, slope)
        early_lists = (a, core(a), b, core(b))
        c, d = after(c, a), after(d, b)
        c_got, d_got = along_x(c), along_y(d)
    first, mean, rstd, hid, mod, w_early = run_first(me, early_lists, x, cond, lens, inv, small_master, width)
    if by_pieces:
        c_got, d_got, first, mean, rstd, hid, mod, w_early = tie(c_got, d_got, first, mean, rstd, hid, mod, w_early)
        c, d = jnp.concatenate([c, c_got], axis=0), jnp.concatenate([d, d_got], axis=0)
        late_lists = (c, core(c), d, core(d))
    skip, dskip, g2, *late_grads, gs_late, w_late = run_second(
        me, late_lists, hid, x, cs, cd, lens, inv, small_master, width
    )
    half = count // width // 2
    third = functools.partial(run_third, w_late)
    rest = (first, mean, rstd, mod, lens, inv, small_master, width)

    def windows_first(*values):
        whole_one = jnp.concatenate(values, axis=1) if len(values) > 1 else values[0]
        turned = whole_one.transpose(1, 0, 2).reshape(micro, samp, whole_one.shape[0], whole_one.shape[2])
        return with_layout_constraint(turned, Layout(major_to_minor=(0, 1, 2, 3)))

    if by_pieces:
        a, a_send, b, b_send = late_grads
        a_got, b_got = core(a_send), core(b_send)
        g1_front, dmod_front, down_front, gs_front = third(g2, skip, *rest, 0, half)
        a_got, b_got, g1_front, dmod_front, gs_front = tie(a_got, b_got, g1_front, dmod_front, gs_front)
        (a, a_send), (b, b_send) = parts(a, a_got), parts(b, b_got)
        a_send, b_send, g2_back, gs_front = tie(a_send, b_send, g2, gs_front)
        a_got, b_got = along_x(a_send), along_y(b_send)
        g1_back, dmod_back, down_back, gs_back = third(g2_back, skip, *rest, half, count // width - half)
        a_got, b_got, g1_back, dmod_back, gs_back = tie(a_got, b_got, g1_back, dmod_back, gs_back)
        (a, a_send), (b, b_send) = parts(a, a_got), parts(b, b_got)
        a_send, b_send, g1_back = tie(a_send, b_send, g1_back)
        a_got, b_got = along_y(a_send), along_x(b_send)
        early_grads = run_early_grads(me, x, g1_front, g1_back, cond, dmod_front, dmod_back, width)
        a_got, b_got, *early_grads = tie(a_got, b_got, *early_grads)
        late = jnp.concatenate([a + a_got, b + b_got], axis=1)

        small = jnp.concatenate([(gs_front + gs_back)[0:5], gs_late[0:5]], axis=0)
        a, a_send, b, b_send = early_grads
        late, late_send = parts(late)
        a_got, b_got, small_got, late_got = core(a_send), core(b_send), core(small), z_low(late_send)
        a_got, b_got, small_got = tie(a_got, b_got, small_got)
        (a, a_send), (b, b_send), small = parts(a, a_got), parts(b, b_got), small + small_got
        a_send, b_send, dskip = tie(a_send, b_send, dskip)
        a_got, b_got, small_got = along_x(a_send), along_y(b_send), along_x(small)
        dx, dobs = run_inputs(
            me, w_early, w_late, g1_front, g1_back, dskip, dmod_front, dmod_back, slope, lens, width
        )
        a_got, b_got, small_got, late_got, dx, dobs = tie(a_got, b_got, small_got, late_got, dx, dobs)
        late, late_send = parts(late, late_got)
        late_got = z_high(late_send)
        (a, a_send), (b, b_send), small = parts(a, a_got), parts(b, b_got), small + small_got
        a_got, b_got = along_y(a_send), along_x(b_send)
        skip_out = windows_first(skip)
        a_got, b_got, skip_out, small = tie(a_got, b_got, skip_out, small)
        early, early_send = parts(jnp.concatenate([a + a_got, b + b_got], axis=1))
        early_got, small_got = z_low(early_send), along_y(small)
        down_out = windows_first(down_front, down_back)
        early_got, small_got, down_out, dobs = tie(early_got, small_got, down_out, dobs)
        early, early_send = parts(early, early_got)
        early_got = z_high(early_send)
        dobs, dobs_send = parts(dobs)
        dobs_got = along_x(dobs_send)
        small = small + small_got
        early_got, late_got = tie(early_got, late_got)
        grads = join_order((early + early_got)[0], (late + late_got)[0])

        spread = jnp.take(grads, jnp.maximum(block_of, 0), axis=0, mode="clip").reshape(dp_count, slot_count, 16, 128)
        spread, dx, small = tie(spread, dx, small)
        owned = lax.all_to_all(spread, "dp", 0, 0)
        small_got = z_low(small)
        actions_grad = windows_first(dx)
        owned, actions_grad, small_got, dobs_got = tie(owned, actions_grad, small_got, dobs_got)
        places = me[1] ^ jnp.arange(4, dtype=jnp.int32)
        state = (master, moment_one, moment_two)
        x_got, core_got = along_x(owned), core(owned)
        small = small + small_got
        core_got, small, dobs, dobs_got = tie(core_got, small, dobs, dobs_got)
        small_got = z_high(small)
        dobs, dobs_send = parts(dobs, dobs_got)
        dobs_got = core(dobs_send)
        made = run_adamw(places[0:2], used, (owned, core_got), *state)
        x_got, small_got, dobs_got, *made = tie(x_got, small_got, dobs_got, *made)
        core_got = core(x_got)
        grad_small = small + small_got
        observations_grad = (dobs + dobs_got).reshape(observations.shape)
        new_one, new_two, new_master = run_adamw(places[2:4], used, (x_got, core_got), *state, made)
    else:
        g1_front, dmod_front, down_front, gs_front = third(g2, skip, *rest, 0, half)
        g1_back, dmod_back, down_back, gs_back = third(g2, skip, *rest, half, count // width - half)
        early_grads = run_early_grads(me, x, g1_front, g1_back, cond, dmod_front, dmod_back, width)
        dx, dobs = run_inputs(
            me, w_early, w_late, g1_front, g1_back, dskip, dmod_front, dmod_back, slope, lens, width
        )
        skip_out, down_out, actions_grad = windows_first(skip), windows_first(down_front, down_back), windows_first(dx)
        small = jnp.concatenate([(gs_front + gs_back)[0:5], gs_late[0:5]], axis=0)
        grad_small = sum_all(small)
        observations_grad = lax.psum_scatter(dobs, "pair", scatter_dimension=0).reshape(observations.shape)
        grads = join_order(from_lists(early_grads), from_lists(late_grads))
        rows = grads.reshape(-1, 4, 32, C).transpose(1, 0, 2, 3)
        rows = lax.psum_scatter(rows, "pair", scatter_dimension=0)
        spread = jnp.take(rows, jnp.maximum(block_of, 0), axis=0)
        owned = lax.psum_scatter(spread, "dp", scatter_dimension=0, tiled=True)
        owned = lax.all_gather(owned, "pair", axis=1, tiled=True)
        cut = pieces_of(owned).transpose(1, 0, 2, 3, 4)
        places = jnp.arange(4, dtype=jnp.int32)
        state = (master, moment_one, moment_two)
        made = run_adamw(places[0:2], used, (cut[0], cut[1]), *state)
        new_one, new_two, new_master = run_adamw(places[2:4], used, (cut[2], cut[3]), *state, made)
    small_first, small_second, new_small = adamw(
        small_master, small_one, small_two, grad_small, RATE_SMALL
    )
    return (
        skip_out,
        down_out,
        actions_grad,
        observations_grad,
        new_one,
        new_two,
        new_master,
        small_first,
        small_second,
        new_small,
    )


def solution(mesh):
    placed = (
        P(None, ("dp", "pair"), None, None),
        P(None, "dp", "pair"),
        P(None, ("dp", "pair")),
        P(None, ("dp", "pair")),
        P(None, ("dp", "pair"), None, None),
        P(None, ("dp", "pair"), None, None),
        P(),
        P("dp", None, None),
        P("dp", None, None),
        P("dp", None, None),
        P(),
        P(),
        P(),
    )
    return jax.shard_map(
        body,
        mesh=mesh,
        in_specs=placed,
        out_specs=(
            P(None, ("dp", "pair"), None, None),
            P(None, ("dp", "pair"), None, None),
            P(None, ("dp", "pair"), None, None),
            P(None, "dp", "pair"),
            P("dp", None, None),
            P("dp", None, None),
            P("dp", None, None),
            P(),
            P(),
            P(),
        ),
        check_vma=False,
    )
```

```python
import functools
import math

import jax
import jax.numpy as jnp
from jax import lax
from jax.experimental.layout import Layout, with_layout_constraint
from jax.experimental import pallas as pl
from jax.experimental.pallas import tpu as pltpu
from jax.sharding import PartitionSpec as P

CI = 256
C = 512
TE = 128
KW = 5
H = 16
HD = 8
KD = 3
NSMALL = 10
STEP = 10
BLK = 128
COND = 1152
NBLK = 62
GC = 64
LEAST = 4

FIRST_N, SECOND_N, RES_N, DOWN_N, FILM_N = 10, 20, 2, 12, 9
EARLY_N = FIRST_N + 2 * FILM_N
LATE_N = SECOND_N + RES_N + DOWN_N
DOWN_IN = SECOND_N + RES_N
PIECES = 32

BETA_ONE = 0.9
BETA_TWO = 0.999
EPS_ADAM = 1e-08
DECAY = 0.01
RATE_MATRIX = 0.1
RATE_SMALL = 1.0

F32 = jnp.float32
BF = jnp.bfloat16
NT = (((1,), (1,)), ((), ()))
TN = (((0,), (0,)), ((), ()))
MIB = 2**20
VMEM_LIMITS = dict(first=48, second=44, third=24, early_grads=20, inputs=18, adamw=56)


def mish(value):
    return value * jnp.tanh(jax.nn.softplus(value))


def time_embed(step_ids, width):
    half = width // 2
    freq = jnp.exp(-math.log(10000.0) * jnp.arange(half, dtype=F32) / (half - 1))
    angle = step_ids.astype(F32)[:, None] * freq[None, :]
    return jnp.concatenate([jnp.sin(angle), jnp.cos(angle)], axis=1)


def slot_of(owners, slot_count):
    same = owners[:, None] == owners[None, :]
    order = jnp.arange(owners.shape[0], dtype=jnp.int32)
    earlier = order[:, None] > order[None, :]
    rank = jnp.sum((same & earlier).astype(jnp.int32), axis=1)
    return owners * slot_count + rank


def adamw(weight, first_m, second_m, grad, rate):
    first_new = BETA_ONE * first_m + (1.0 - BETA_ONE) * grad
    second_new = BETA_TWO * second_m + (1.0 - BETA_TWO) * grad * grad
    fix_one = 1.0 - BETA_ONE**STEP
    fix_two = 1.0 - BETA_TWO**STEP
    update = first_new / fix_one / (jnp.sqrt(second_new / fix_two) + EPS_ADAM) + DECAY * weight
    return (first_new, second_new, weight - rate * update)


def keep(lens, t, value):
    return value if t < LEAST else jnp.where(lens > t, value, 0.0)


def mish_parts(v):
    w = jnp.exp(jnp.minimum(v, 30.0))
    n = w * (w + 2.0)
    return w, n, pl.reciprocal(n + 2.0, approx=True)


def mish_only(v):
    _, n, r = mish_parts(v)
    return v * (n * r)


def mish_both(v):
    w, n, r = mish_parts(v)
    t = n * r
    return v * t, t + (4.0 * v) * (((n - w) * r) * r)


def group_sum(value):
    low_half = lax.broadcasted_iota(jnp.int32, value.shape, 1) < GC
    zero = jnp.zeros_like(value)
    left = jnp.sum(jnp.where(low_half, value, zero), axis=1, keepdims=True)
    right = jnp.sum(jnp.where(low_half, zero, value), axis=1, keepdims=True)
    return jnp.where(low_half, left, right)


def lanes(q):
    return slice(q * 128, (q + 1) * 128)


def flips_of(k):
    return (k >> 3) & 1, (k >> 2) & 1, (k >> 1) & 1, k & 1


def place(me, k, by_y_first, core):
    one, two, z_low, z_high = flips_of(k)
    y, x = (one, two) if by_y_first else (two, one)
    return me[0] ^ (z_high * 4 + z_low * 2 + y), me[1] ^ (x * 2 + core)


def fetch(me, sources, dst, sem):
    at = 0
    for by_y_first, pair in ((False, sources[:2]), (True, sources[2:])):
        count = pair[0].shape[1]
        for core, source in enumerate(pair):
            for k in range(16):
                row, col = place(me, k, by_y_first, core)
                pltpu.make_async_copy(
                    source.at[k],
                    dst.at[at : at + count, row, :, pl.ds(pl.multiple_of(col * 128, 128), 128)],
                    sem,
                ).start()
        at = at + count
    return pltpu.make_async_copy(dst, dst, sem)


def store_pieces(me, acc, outs, base=0):
    at = 0
    for by_y_first, pair in ((False, outs[:2]), (True, outs[2:])):
        count = pair[0].shape[1]

        def one_block(b, carry, at=at, by_y_first=by_y_first, pair=pair):
            for core, out in enumerate(pair):
                for k in range(16):
                    row, col = place(me, k, by_y_first, core)
                    rows = pl.ds(pl.multiple_of((at + b) * BLK + row * 16, 16), 16)
                    cols = pl.ds(pl.multiple_of(col * 128, 128), 128)
                    out[k, b] = acc[rows, cols].astype(BF)
            return carry

        lax.fori_loop(0, count, one_block, 0)
        at = at + count


def matrix(ref, at, count):
    return ref[at : at + count].reshape(count * BLK, C)


def first_kernel(me, pa, pb, pc, pd, x_ref, cond_ref, lens_ref, inv_ref, small_ref, fst, mean_ref, rstd_ref, hid_ref,
                 mod_ref, w_out, w_one, xp, sem):
    step = pl.program_id(0)
    frames, width, _ = x_ref.shape
    rows = frames * width

    @pl.when(step == 0)
    def _():
        arrival = fetch((me[0], me[1]), (pa, pb, pc, pd), w_one, sem.at[0])
        xp[0:2] = jnp.zeros((2, width, CI), BF)
        xp[frames + 2 :] = jnp.zeros((2, width, CI), BF)
        arrival.wait()
        pltpu.make_async_copy(w_one, w_out, sem.at[1]).start()
        for k in range(2):
            mod_ref[k] = (
                jnp.dot(cond_ref[...], matrix(w_one, FIRST_N + k * FILM_N, FILM_N), preferred_element_type=F32)
                + small_ref[3 + k : 4 + k]
            )

    xp[2 : frames + 2] = x_ref[...]
    cut = C // 2
    for part in range(2):
        cs = slice(part * cut, (part + 1) * cut)
        total = small_ref[0:1, cs]
        for a in range(KW):
            total = total + jnp.dot(
                xp[a : a + frames].reshape(rows, CI),
                w_one[2 * a : 2 * a + 2, :, :, cs].reshape(CI, cut),
                preferred_element_type=F32,
            )
        fst[:, :, cs] = total.reshape(frames, width, cut)

    here = pl.ds(pl.multiple_of(step * width, width), width)
    lens = lens_ref[...]
    inv = inv_ref[...]
    for q in range(C // 128):
        ls = lanes(q)
        total = jnp.zeros((width, 128), F32)
        for t in range(frames):
            total = total + keep(lens, t, fst[t, :, ls])
        mean = group_sum(total) * inv
        total = jnp.zeros((width, 128), F32)
        for t in range(frames):
            centered = fst[t, :, ls] - mean
            total = total + keep(lens, t, centered * centered)
        rstd = lax.rsqrt(group_sum(total) * inv + 1e-05)
        mean_ref[:, ls] = mean
        rstd_ref[:, ls] = rstd
        slant = rstd * small_ref[1:2, ls]
        level = small_ref[2:3, ls] - mean * slant
        scale, shift = mod_ref[0, here, ls], mod_ref[1, here, ls]
        for t in range(frames):
            value = scale * mish_only(fst[t, :, ls] * slant + level) + shift
            hid_ref[t, :, ls] = keep(lens, t, value).astype(BF)

    @pl.when(step == pl.num_programs(0) - 1)
    def _():
        pltpu.make_async_copy(w_one, w_out, sem.at[1]).wait()


def second_kernel(me, pa, pb, pc, pd, hid_ref, x_ref, cs_ref, cd_ref, lens_ref, inv_ref, small_ref, skip_ref,
                  dskip_ref, g2_ref, ga, gb, gc, gd, gs_ref, w_out, w_two, hp, cdp, sec, br, dev, dod, se, so, acc,
                  sem):
    step = pl.program_id(0)
    last = pl.num_programs(0) - 1
    frames, width, _ = x_ref.shape
    half = frames // 2
    rows = frames * width

    @pl.when(step == 0)
    def _():
        arrival = fetch((me[0], me[1]), (pa, pb, pc, pd), w_two, sem.at[0])
        hp[0:2] = jnp.zeros((2, width, C), BF)
        hp[frames + 2 :] = jnp.zeros((2, width, C), BF)
        cdp[half:] = jnp.zeros((1, width, C), BF)
        so[0:1] = jnp.zeros((1, width, C), BF)
        acc[...] = jnp.zeros_like(acc)
        gs_ref[...] = jnp.zeros_like(gs_ref)
        arrival.wait()
        pltpu.make_async_copy(w_two, w_out, sem.at[1]).start()

    hp[2 : frames + 2] = hid_ref[...]
    cdp[0:half] = cd_ref[...]
    cot = cdp[0:half].reshape(half * width, C)
    cot_next = cdp[1 : half + 1].reshape(half * width, C)
    lens = lens_ref[...]
    inv = inv_ref[...]
    zero = jnp.zeros((width, 128), F32)
    cut = C // 2

    def columns(part):
        return slice(part * cut, (part + 1) * cut)

    def weight(at, count, part):
        return w_two[at : at + count, :, :, columns(part)].reshape(count * BLK, cut)

    def weight_rows(at, part):
        n = cut // BLK
        return matrix(w_two, at + part * n, n)

    def forward(part):
        cs = columns(part)
        dev[:, :, cs] = lax.dot_general(
            cot, weight_rows(DOWN_IN + 4, part), NT, preferred_element_type=F32
        ).reshape(half, width, cut)
        dod[:, :, cs] = (
            lax.dot_general(cot, weight_rows(DOWN_IN + 8, part), NT, preferred_element_type=F32)
            + lax.dot_general(cot_next, weight_rows(DOWN_IN, part), NT, preferred_element_type=F32)
        ).reshape(half, width, cut)
        br[:, :, cs] = (
            jnp.dot(x_ref[...].reshape(rows, CI), weight(SECOND_N, RES_N, part), preferred_element_type=F32)
            + small_ref[8:9, cs]
        ).reshape(frames, width, cut)
        total = jnp.dot(hp[0:frames].reshape(rows, C), weight(0, 4, part), preferred_element_type=F32)
        for a in range(1, KW):
            total = total + jnp.dot(
                hp[a : a + frames].reshape(rows, C), weight(4 * a, 4, part), preferred_element_type=F32
            )
        sec[:, :, cs] = (total + small_ref[5:6, cs]).reshape(frames, width, cut)

    def norm(q):
        ls = lanes(q)
        total = zero
        for t in range(frames):
            total = total + keep(lens, t, sec[t, :, ls])
        mean = group_sum(total) * inv
        total = zero
        for t in range(frames):
            centered = sec[t, :, ls] - mean
            total = total + keep(lens, t, centered * centered)
        rstd = lax.rsqrt(group_sum(total) * inv + 1e-05)
        gain = small_ref[6:7, ls]
        slant = rstd * gain
        level = small_ref[7:8, ls] - mean * slant
        sum_dy, sum_dyv, sum_ds = zero, zero, zero
        for t in range(frames):
            value = sec[t, :, ls]
            act, slope = mish_both(value * slant + level)
            skip = (act + br[t, :, ls]).astype(BF)
            skip_ref[t, :, ls] = skip
            if t % 2:
                so[t // 2 + 1, :, ls] = skip
                back = dod[t // 2, :, ls]
            else:
                se[t // 2, :, ls] = skip
                back = dev[t // 2, :, ls]
            ds = (cs_ref[t, :, ls].astype(F32) + back).astype(BF)
            dskip_ref[t, :, ls] = ds
            ds = ds.astype(F32)
            sum_ds = sum_ds + ds
            dy = ds * slope
            br[t, :, ls] = dy
            sum_dy = sum_dy + dy
            sum_dyv = sum_dyv + dy * value
        sum_dyn = rstd * (sum_dyv - mean * sum_dy)
        tilt = (rstd * rstd) * (group_sum(sum_dyn * gain) * inv)
        base = rstd * (group_sum(sum_dy * gain) * inv) - mean * tilt
        sum_g, sum_cd = zero, zero
        for t in range(frames):
            grad = br[t, :, ls] * slant - keep(lens, t, base + sec[t, :, ls] * tilt)
            grad = grad.astype(BF)
            g2_ref[t, :, ls] = grad
            sum_g = sum_g + grad.astype(F32)
        for t in range(half):
            sum_cd = sum_cd + cd_ref[t, :, ls].astype(F32)
        for k, part in enumerate((sum_g, sum_dyn, sum_dy, sum_ds, sum_cd)):
            gs_ref[k : k + 1, ls] += jnp.sum(part, axis=0, keepdims=True)

    def gradients(part):
        cs = columns(part)
        grad_two = g2_ref[:, :, cs].reshape(rows, cut)
        for a in range(KW):
            acc[a * C : (a + 1) * C, cs] += lax.dot_general(
                hp[a : a + frames].reshape(rows, C), grad_two, TN, preferred_element_type=F32
            )
        at = KW * C
        acc[at : at + CI, cs] += lax.dot_general(
            x_ref[...].reshape(rows, CI), dskip_ref[:, :, cs].reshape(rows, cut), TN, preferred_element_type=F32
        )
        at = at + CI
        for a, source in enumerate((so.at[0:half], se, so.at[1 : half + 1])):
            low = at + a * C + part * cut
            acc[low : low + cut] += lax.dot_general(
                source[:, :, cs].reshape(half * width, cut), cot, TN, preferred_element_type=F32
            )

    per = (C // 128) // 2
    forward(0)
    for q in range(0 * per, 1 * per):
        norm(q)
    forward(1)
    gradients(0)
    for q in range(1 * per, 2 * per):
        norm(q)
    gradients(1)

    @pl.when(step == last)
    def _():
        store_pieces((me[0], me[1]), acc, (ga, gb, gc, gd))
        pltpu.make_async_copy(w_two, w_out, sem.at[1]).wait()


def third_kernel(w_hbm, g2_ref, skip_ref, first_ref, mean_ref, rstd_ref, mod_ref, lens_ref, inv_ref, small_ref,
                 g1_ref, dmod_ref, down_ref, gs_ref, w_two, gp, dh, se, so, sem):
    step = pl.program_id(0)
    frames, width, _ = g2_ref.shape
    rows = frames * width
    half = frames // 2

    @pl.when(step == 0)
    def _():
        arrival = pltpu.make_async_copy(w_hbm, w_two, sem.at[0])
        arrival.start()
        gp[0:2] = jnp.zeros((2, width, C), BF)
        gp[frames + 2 :] = jnp.zeros((2, width, C), BF)
        so[0:1] = jnp.zeros((1, width, C), BF)
        gs_ref[...] = jnp.zeros_like(gs_ref)
        arrival.wait()

    gp[2 : frames + 2] = g2_ref[...]
    cut = C // 2
    for part in range(2):
        total = jnp.zeros((rows, cut), F32)
        for a in range(KW):
            total = total + lax.dot_general(
                gp[4 - a : 4 - a + frames].reshape(rows, C),
                matrix(w_two, 4 * a + 2 * part, 2),
                NT,
                preferred_element_type=F32,
            )
        dh[:, :, part * cut : (part + 1) * cut] = total.reshape(frames, width, cut)
    for j in range(half):
        se[j] = skip_ref[2 * j]
        so[j + 1] = skip_ref[2 * j + 1]
    down = jnp.dot(so[0:half].reshape(half * width, C), matrix(w_two, DOWN_IN, 4), preferred_element_type=F32)
    down = down + jnp.dot(
        se[...].reshape(half * width, C), matrix(w_two, DOWN_IN + 4, 4), preferred_element_type=F32
    )
    down = down + jnp.dot(
        so[1 : half + 1].reshape(half * width, C), matrix(w_two, DOWN_IN + 8, 4), preferred_element_type=F32
    )
    down_ref[...] = (down + small_ref[9:10]).astype(BF).reshape(half, width, C)

    lens = lens_ref[...]
    inv = inv_ref[...]
    zero = jnp.zeros((width, 128), F32)
    for q in range(C // 128):
        ls = lanes(q)
        gain = small_ref[1:2, ls]
        mean, rstd = mean_ref[:, ls], rstd_ref[:, ls]
        slant = rstd * gain
        level = small_ref[2:3, ls] - mean * slant
        scale = mod_ref[0, :, ls]
        sum_dy, sum_dyv, d_scale, d_shift = zero, zero, zero, zero
        for t in range(frames):
            value = first_ref[t, :, ls]
            act, slope = mish_both(value * slant + level)
            grad = keep(lens, t, dh[t, :, ls])
            d_scale = d_scale + grad * act
            d_shift = d_shift + grad
            dy = (grad * scale) * slope
            dh[t, :, ls] = dy
            sum_dy = sum_dy + dy
            sum_dyv = sum_dyv + dy * value
        sum_dyn = rstd * (sum_dyv - mean * sum_dy)
        tilt = (rstd * rstd) * (group_sum(sum_dyn * gain) * inv)
        base = rstd * (group_sum(sum_dy * gain) * inv) - mean * tilt
        sum_g = zero
        for t in range(frames):
            grad = dh[t, :, ls] * slant - keep(lens, t, base + first_ref[t, :, ls] * tilt)
            grad = grad.astype(BF)
            g1_ref[t, :, ls] = grad
            sum_g = sum_g + grad.astype(F32)
        d_scale, d_shift = d_scale.astype(BF), d_shift.astype(BF)
        dmod_ref[0, :, ls] = d_scale
        dmod_ref[1, :, ls] = d_shift
        for k, part in enumerate((sum_g, sum_dyn, sum_dy, d_scale.astype(F32), d_shift.astype(F32))):
            gs_ref[k : k + 1, ls] += jnp.sum(part, axis=0, keepdims=True)


def of_halves(step, half, front, back, dst):
    @pl.when(step < half)
    def _():
        dst[...] = front[...]

    @pl.when(step >= half)
    def _():
        dst[...] = back[...]


def early_grads_kernel(me, x_ref, front_ref, back_ref, cond_ref, dmod_front, dmod_back, ga, gb, gc, gd, xp, g1, acc):
    step = pl.program_id(0)
    steps = pl.num_programs(0)
    frames, width, _ = x_ref.shape
    rows = frames * width
    near = dmod_front.shape[1]

    @pl.when(step == 0)
    def _():
        xp[0:2] = jnp.zeros((2, width, CI), BF)
        xp[frames + 2 :] = jnp.zeros((2, width, CI), BF)
        acc[0 : KW * CI] = jnp.zeros((KW * CI, C), F32)
        for k in range(2):
            at = KW * CI + k * COND
            acc[at : at + COND] = lax.dot_general(
                cond_ref[0:near], dmod_front[k], TN, preferred_element_type=F32
            ) + lax.dot_general(cond_ref[near:], dmod_back[k], TN, preferred_element_type=F32)

    xp[2 : frames + 2] = x_ref[...]
    of_halves(step, near // width, front_ref, back_ref, g1)
    grad_one = g1[...].reshape(rows, C)
    for a in range(KW):
        acc[a * CI : (a + 1) * CI] += lax.dot_general(
            xp[a : a + frames].reshape(rows, CI), grad_one, TN, preferred_element_type=F32
        )

    @pl.when(step == steps - 1)
    def _():
        store_pieces((me[0], me[1]), acc, (ga, gb, gc, gd))


def inputs_kernel(me, w_early, w_late, front_ref, back_ref, dskip_ref, dmod_front, dmod_back, slope_ref, lens_ref,
                  dx_ref, dobs_ref, w_one, w_res, gp, sem):
    step = pl.program_id(0)
    steps = pl.num_programs(0)
    frames, width, _ = dskip_ref.shape
    rows = frames * width
    near = dmod_front.shape[1]

    @pl.when(step == 0)
    def _():
        early = pltpu.make_async_copy(w_early, w_one, sem.at[0])
        late = pltpu.make_async_copy(w_late.at[SECOND_N:DOWN_IN], w_res, sem.at[1])
        early.start()
        late.start()
        gp[0:2] = jnp.zeros((2, width, C), BF)
        gp[frames + 2 :] = jnp.zeros((2, width, C), BF)
        early.wait()
        late.wait()
        for r in range(4):
            at = FIRST_N + 1 + 2 * (me[1] ^ r)
            for dmod, low_at, high_at in ((dmod_front, 0, near), (dmod_back, near, cond_rows(slope_ref))):
                back = lax.dot_general(
                    dmod[0], w_one[pl.ds(at, 2)].reshape(2 * BLK, C), NT, preferred_element_type=F32
                ) + lax.dot_general(
                    dmod[1], w_one[pl.ds(at + FILM_N, 2)].reshape(2 * BLK, C), NT, preferred_element_type=F32
                )
                dobs_ref[r, low_at:high_at] = back * slope_ref[r, low_at:high_at]

    of_halves(step, near // width, front_ref, back_ref, gp.at[2 : frames + 2])
    total = lax.dot_general(
        dskip_ref[...].reshape(rows, C), matrix(w_res, 0, RES_N), NT, preferred_element_type=F32
    )
    for a in range(KW):
        total = total + lax.dot_general(
            gp[4 - a : 4 - a + frames].reshape(rows, C), matrix(w_one, 2 * a, 2), NT, preferred_element_type=F32
        )
    total = total.reshape(frames, width, CI)
    lens = lens_ref[...]
    for t in range(frames):
        for q in range(CI // 128):
            dx_ref[t, :, lanes(q)] = keep(lens, t, total[t, :, lanes(q)])


def cond_rows(slope_ref):
    return slope_ref.shape[1]


def adamw_kernel(places, used, one_piece, two_piece, master_ref, one_ref, two_ref, *rest):
    one_out, two_out, master_out, grad = rest[-4:]
    group = grad.shape[0]
    at = pl.program_id(1) * group

    def load(piece_ref):
        for slot in range(group):
            held = used[at + slot] > 0
            for row in range(8):
                piece = piece_ref[row, slot].astype(F32)
                grad[slot, row * 16 : row * 16 + 16] = jnp.where(held, piece, 0.0)

    @pl.when(pl.program_id(0) == 0)
    def _():
        load(one_piece)

    @pl.when(pl.program_id(0) == 1)
    def _():
        load(two_piece)

    one_out[...], two_out[...], master_out[...] = adamw(
        master_ref[...], one_ref[...], two_ref[...], grad[...], RATE_MATRIX
    )


def tiles(frames, width, channels):
    return pl.BlockSpec((frames, width, channels), lambda i, *_: (0, i, 0))


def rows_of(width, channels):
    return pl.BlockSpec((width, channels), lambda i, *_: (i, 0))


def whole(*shape):
    return pl.BlockSpec(shape, lambda i, *_: (0,) * len(shape), pipeline_mode=pl.Buffered(1))


ANY = pl.BlockSpec(memory_space=pl.ANY)


def weight_scratch(count):
    return pltpu.VMEM((count, 8, 16, C), BF)


def shape(*dims, dtype=F32):
    return jax.ShapeDtypeStruct(dims, dtype)


def half_lists(count):
    front = count // 2
    return [(16, n, 16, 128) for n in (front, front, count - front, count - front)]


def call(kernel, name, grid, scalars, ins, outs, scratch, operands, flops, aliases=None):
    return pl.pallas_call(
        kernel,
        grid_spec=pltpu.PrefetchScalarGridSpec(
            num_scalar_prefetch=scalars,
            grid=grid,
            in_specs=ins,
            out_specs=[spec for spec, _ in outs],
            scratch_shapes=scratch,
        ),
        out_shape=[made for _, made in outs],
        input_output_aliases=aliases or {},
        compiler_params=pltpu.CompilerParams(
            vmem_limit_bytes=VMEM_LIMITS[name] * MIB, dimension_semantics=("arbitrary",) * len(grid)
        ),
        cost_estimate=pl.CostEstimate(flops=flops, bytes_accessed=20 * 2**20, transcendentals=0),
        name=name,
    )(*operands)


def run_first(me, pieces, x, cond, lens, inv, small, width):
    count = x.shape[1]
    return call(
        first_kernel, "first", (count // width,), 1,
        [ANY] * 4 + [tiles(H, width, CI), whole(count, COND), rows_of(width, 128), rows_of(width, 128),
                     whole(NSMALL, C)],
        [(tiles(H, width, C), shape(H, count, C)), (rows_of(width, C), shape(count, C)),
         (rows_of(width, C), shape(count, C)), (tiles(H, width, C), shape(H, count, C, dtype=BF)), (whole(2, count, C), shape(2, count, C)),
         (ANY, shape(EARLY_N, 8, 16, C, dtype=BF))],
        [weight_scratch(EARLY_N), pltpu.VMEM((H + 4, width, CI), BF), pltpu.SemaphoreType.DMA((2,))],
        (me, *pieces, x, cond, lens, inv, small),
        2 * count * H * KW * CI * C,
    )


def run_second(me, pieces, hid, x, cs, cd, lens, inv, small, width):
    count = x.shape[1]
    bf_tile = (tiles(H, width, C), shape(H, count, C, dtype=BF))
    return call(
        second_kernel, "second", (count // width,), 1,
        [ANY] * 4 + [tiles(H, width, C), tiles(H, width, CI), tiles(H, width, C), tiles(HD, width, C),
                     rows_of(width, 128), rows_of(width, 128), whole(NSMALL, C)],
        [bf_tile, bf_tile, bf_tile] + [(whole(*dims), shape(*dims, dtype=BF)) for dims in half_lists(LATE_N)]
        + [(whole(8, C), shape(8, C)), (ANY, shape(LATE_N, 8, 16, C, dtype=BF))],
        [weight_scratch(LATE_N), pltpu.VMEM((H + 4, width, C), BF), pltpu.VMEM((HD + 1, width, C), BF),
         pltpu.VMEM((H, width, C), F32), pltpu.VMEM((H, width, C), F32),
         pltpu.VMEM((HD, width, C), F32), pltpu.VMEM((HD, width, C), F32),
         pltpu.VMEM((HD, width, C), BF), pltpu.VMEM((HD + 1, width, C), BF),
         pltpu.VMEM((LATE_N * BLK, C), F32), pltpu.SemaphoreType.DMA((2,))],
        (me, *pieces, hid, x, cs, cd, lens, inv, small),
        6 * count * H * KW * C * C,
    )


def run_third(w_late, g2, skip, first, mean, rstd, mod, lens, inv, small, width, tiles_at, tiles_n):
    count = tiles_n * width

    def part(frames, channels):
        return pl.BlockSpec((frames, width, channels), lambda i: (0, i + tiles_at, 0))

    def part_rows(channels):
        return pl.BlockSpec((width, channels), lambda i: (i + tiles_at, 0))

    return call(
        third_kernel, "third", (tiles_n,), 0,
        [ANY, part(H, C), part(H, C), part(H, C), part_rows(C), part_rows(C), part(2, C), part_rows(128), part_rows(128), whole(NSMALL, C)],
        [(tiles(H, width, C), shape(H, count, C, dtype=BF)), (tiles(2, width, C), shape(2, count, C, dtype=BF)),
         (tiles(HD, width, C), shape(HD, count, C, dtype=BF)), (whole(8, C), shape(8, C))],
        [weight_scratch(LATE_N), pltpu.VMEM((H + 4, width, C), BF), pltpu.VMEM((H, width, C), F32),
         pltpu.VMEM((HD, width, C), BF), pltpu.VMEM((HD + 1, width, C), BF), pltpu.SemaphoreType.DMA((1,))],
        (w_late, g2, skip, first, mean, rstd, mod, lens, inv, small),
        4 * count * H * KW * C * C,
    )


def front_tiles(width, channels, half):
    return pl.BlockSpec((H, width, channels), lambda i, *_: (0, jnp.minimum(i, half - 1), 0))


def back_tiles(width, channels, half):
    return pl.BlockSpec((H, width, channels), lambda i, *_: (0, jnp.maximum(i - half, 0), 0))


def run_early_grads(me, x, front, back, cond, dmod_front, dmod_back, width):
    count = x.shape[1]
    steps = count // width
    half = front.shape[1]
    return call(
        early_grads_kernel, "early_grads", (steps,), 1,
        [tiles(H, width, CI), front_tiles(width, C, half // width), back_tiles(width, C, half // width), whole(count, COND),
         whole(2, half, C), whole(2, count - half, C)],
        [(whole(*dims), shape(*dims, dtype=BF)) for dims in half_lists(EARLY_N)],
        [pltpu.VMEM((H + 4, width, CI), BF), pltpu.VMEM((H, width, C), BF), pltpu.VMEM((EARLY_N * BLK, C), F32)],
        (me, x, front, back, cond, dmod_front, dmod_back),
        2 * count * H * KW * CI * C,
    )


def run_inputs(me, w_early, w_late, front, back, dskip, dmod_front, dmod_back, slope, lens, width):
    count = dskip.shape[1]
    steps = count // width
    half = front.shape[1]
    return call(
        inputs_kernel, "inputs", (steps,), 1,
        [ANY, ANY, front_tiles(width, C, half // width), back_tiles(width, C, half // width), tiles(H, width, C),
         whole(2, half, C), whole(2, count - half, C), whole(*slope.shape), rows_of(width, 128)],
        [(tiles(H, width, CI), shape(H, count, CI)), (whole(*slope.shape), shape(*slope.shape))],
        [weight_scratch(EARLY_N), weight_scratch(RES_N), pltpu.VMEM((H + 4, width, C), BF),
         pltpu.SemaphoreType.DMA((2,))],
        (me, w_early, w_late, front, back, dskip, dmod_front, dmod_back, slope, lens),
        2 * count * H * (KW + 1) * CI * C,
    )


def run_adamw(places, used, pieces, master, one, two, made=None):
    slots = master.shape[0]
    group = min(slots, 8)
    block = pl.BlockSpec((group, BLK, 128), lambda k, i, places, used: (i, 0, places[k]))
    piece = pl.BlockSpec((8, group, 16, 128), lambda k, i, *_: (0, i, 0, 0))
    kept = list(made) if made else []
    return call(
        adamw_kernel, "adamw", (2, slots // group), 2,
        [piece, piece, block, block, block] + [ANY] * len(kept),
        [(block, shape(slots, BLK, C))] * 3,
        [pltpu.VMEM((group, BLK, 128), F32)],
        (places, used, *pieces, master, one, two, *kept),
        10 * slots * BLK * C,
        {7 + k: k for k in range(len(kept))},
    )


def prepare(actions, features, order, tsteps, lengths, cot_skip, cot_down):
    micro, samp = lengths.shape
    count = micro * samp
    lens_flat = lengths.reshape(count)
    lens = jnp.broadcast_to(lens_flat.astype(F32)[:, None], (count, 128))
    inv = 1.0 / (lens * GC)
    valid = jnp.arange(H)[:, None, None] < lens_flat[None, :, None]
    x = jnp.where(valid, actions.reshape(count, H, CI).transpose(1, 0, 2), jnp.zeros((), BF))
    cs = cot_skip.reshape(count, H, C).transpose(1, 0, 2)
    cd = cot_down.reshape(count, HD, C).transpose(1, 0, 2)
    obs = features.astype(F32)
    obs_act, obs_back = jax.vjp(mish, obs)
    slope = obs_back(jnp.ones_like(obs))[0]
    obs_act = jnp.take(obs_act.astype(BF), order, axis=0).transpose(1, 0, 2).reshape(count, -1)
    cond = jnp.concatenate([mish(time_embed(tsteps.reshape(count), TE)).astype(BF), obs_act], axis=1)
    return x, cs, cd, lens, inv, cond, slope


def flip(value, axis, bit):
    size = lax.axis_size(axis)
    return lax.ppermute(value, axis, [(i, i ^ bit) for i in range(size)])


def core(value):
    return flip(value, "pair", 1)


def along_x(value):
    return flip(value, "pair", 2)


def along_y(value):
    return flip(value, "dp", 1)


def z_low(value):
    return flip(value, "dp", 2)


def z_high(value):
    return flip(value, "dp", 4)


def pieces_of(block):
    return block.reshape(-1, 8, 16, 4, 128).transpose(1, 3, 0, 2, 4)


def double(value, hop):
    return jnp.concatenate([value, hop(value)], axis=0)


def tie(*values):
    return lax.optimization_barrier(values)


def after(value, *others):
    return tie(value, *others)[0]


def gather_lists(early, late):
    def halves(value):
        front = value.shape[1] // 2
        return value[:, :front], value[:, front:]

    early = double(early[None], z_high)
    late = double(after(late[None], early), z_high)
    early = double(early, z_low)
    late = double(after(late, early), z_low)
    a, b = halves(early)
    a, b = double(a, along_y), double(b, along_x)
    c, d = halves(after(late, a, b))
    a, b = double(a, along_x), double(b, along_y)
    c, d = double(c, along_y), double(d, along_x)
    return (a, b), (c, d)


def parts(own, received=None):
    size = own.shape[0] // 2
    if received is None:
        return own[:size], own[size:]
    return own[:size] + received[:size], own[size:] + received[size:]


def sum_all(value):
    for axis in ("pair", "dp"):
        bit = 1
        while bit < lax.axis_size(axis):
            value = value + flip(value, axis, bit)
            bit = bit * 2
    return value


def split_order(blocks):
    return jnp.concatenate([blocks[:FIRST_N], blocks[FIRST_N + LATE_N :]], axis=0), blocks[FIRST_N : FIRST_N + LATE_N]


def join_order(early, late):
    return jnp.concatenate([early[:FIRST_N], late, early[FIRST_N:]], axis=0)


def as_lists(blocks):
    front = blocks.shape[0] // 2
    found = []
    for by_y_first, part in ((False, blocks[:front]), (True, blocks[front:])):
        cut = pieces_of(part)
        for core_bit in range(2):
            found.append(jnp.stack([cut[place((0, 0), k, by_y_first, core_bit)] for k in range(16)]))
    return tuple(found)


def from_lists(lists):
    parts = []
    for by_y_first, pair in ((False, lists[:2]), (True, lists[2:])):
        table = {}
        for core_bit, part in enumerate(pair):
            for k in range(16):
                table[place((0, 0), k, by_y_first, core_bit)] = part[k]
        cut = jnp.stack([jnp.stack([table[(row, col)] for col in range(4)]) for row in range(8)])
        parts.append(cut.transpose(2, 0, 3, 1, 4).reshape(-1, BLK, C))
    return jnp.concatenate(parts, axis=0)


def body(
    actions,
    observations,
    tsteps,
    lengths,
    cot_skip,
    cot_down,
    owners,
    master,
    moment_one,
    moment_two,
    small_master,
    small_one,
    small_two,
):
    micro, samp = lengths.shape
    slot_count = master.shape[0]
    dp_count = lax.axis_size("dp")
    slots_all = dp_count * slot_count
    me_pair = lax.axis_index("pair")
    me_dp = lax.axis_index("dp")
    by_pieces = dp_count == 8 and lax.axis_size("pair") == 4
    slot_index = slot_of(owners, slot_count)
    block_of = (
        jnp.full((slots_all,), -1, jnp.int32).at[slot_index].set(jnp.arange(NBLK, dtype=jnp.int32))
    )
    used = (lax.dynamic_slice_in_dim(block_of, me_dp * slot_count, slot_count, axis=0) >= 0).astype(jnp.int32)
    here = jnp.stack([me_dp, me_pair]).astype(jnp.int32)
    if by_pieces:
        me = here
        columns = lax.dynamic_slice_in_dim(master, me_pair * 128, 128, axis=2).astype(BF)
        columns = columns.reshape(slot_count, 8, 16, 128).transpose(1, 0, 2, 3)
        slots = lax.all_to_all(columns, "dp", 0, 0).reshape(slots_all, 16, 128)
        early_index, late_index = split_order(slot_index)
        quarters = double(after(observations, columns).reshape(1, micro * samp, -1), along_x)
        quarters = double(after(quarters, slots), core)
        (a, b), (c, d) = gather_lists(
            jnp.take(slots, early_index, axis=0, mode="clip"), jnp.take(slots, late_index, axis=0, mode="clip")
        )
        features = quarters[jnp.array([0, 2, 1, 3])]
    else:
        me = jnp.zeros_like(here)
        quarter = lax.dynamic_slice_in_dim(master, me_pair * 32, 32, axis=1).astype(BF)
        slots = lax.all_gather(quarter, "dp", axis=0, tiled=True)
        mine = jnp.take(slots, slot_index, axis=0)
        early, late = split_order(lax.all_gather(mine, "pair", axis=1, tiled=True))
        early_lists, late_lists = as_lists(early), as_lists(late)
        features = lax.all_gather(observations.reshape(micro * samp, -1), "pair", axis=0)


    order = jnp.arange(4, dtype=jnp.int32) ^ me[1]
    x, cs, cd, lens, inv, cond, slope = prepare(actions, features, order, tsteps, lengths, cot_skip, cot_down)
    count = micro * samp
    width = 64 if count % 64 == 0 else samp
    if by_pieces:
        a, b, x, cs, cd, lens, inv, cond, slope = tie(a, b, x, cs, cd, lens, inv, cond, slope)
        early_lists = (a, core(a), b, core(b))
        c, d = after(c, a), after(d, b)
        c_got, d_got = along_x(c), along_y(d)
    first, mean, rstd, hid, mod, w_early = run_first(me, early_lists, x, cond, lens, inv, small_master, width)
    if by_pieces:
        c_got, d_got, first, mean, rstd, hid, mod, w_early = tie(c_got, d_got, first, mean, rstd, hid, mod, w_early)
        c, d = jnp.concatenate([c, c_got], axis=0), jnp.concatenate([d, d_got], axis=0)
        late_lists = (c, core(c), d, core(d))
    skip, dskip, g2, *late_grads, gs_late, w_late = run_second(
        me, late_lists, hid, x, cs, cd, lens, inv, small_master, width
    )
    half = count // width // 2
    third = functools.partial(run_third, w_late)
    rest = (first, mean, rstd, mod, lens, inv, small_master, width)

    def windows_first(*values):
        whole_one = jnp.concatenate(values, axis=1) if len(values) > 1 else values[0]
        turned = whole_one.transpose(1, 0, 2).reshape(micro, samp, whole_one.shape[0], whole_one.shape[2])
        return with_layout_constraint(turned, Layout(major_to_minor=(0, 1, 2, 3)))

    if by_pieces:
        a, a_send, b, b_send = late_grads
        a_got, b_got = core(a_send), core(b_send)
        g1_front, dmod_front, down_front, gs_front = third(g2, skip, *rest, 0, half)
        a_got, b_got, g1_front, dmod_front, gs_front = tie(a_got, b_got, g1_front, dmod_front, gs_front)
        (a, a_send), (b, b_send) = parts(a, a_got), parts(b, b_got)
        a_send, b_send, g2_back, gs_front = tie(a_send, b_send, g2, gs_front)
        a_got, b_got = along_x(a_send), along_y(b_send)
        g1_back, dmod_back, down_back, gs_back = third(g2_back, skip, *rest, half, count // width - half)
        a_got, b_got, g1_back, dmod_back, gs_back = tie(a_got, b_got, g1_back, dmod_back, gs_back)
        (a, a_send), (b, b_send) = parts(a, a_got), parts(b, b_got)
        a_send, b_send, g1_back = tie(a_send, b_send, g1_back)
        a_got, b_got = along_y(a_send), along_x(b_send)
        early_grads = run_early_grads(me, x, g1_front, g1_back, cond, dmod_front, dmod_back, width)
        a_got, b_got, *early_grads = tie(a_got, b_got, *early_grads)
        late = jnp.concatenate([a + a_got, b + b_got], axis=1)

        small = jnp.concatenate([(gs_front + gs_back)[0:5], gs_late[0:5]], axis=0)
        a, a_send, b, b_send = early_grads
        late, late_send = parts(late)
        a_got, b_got, small_got, late_got = core(a_send), core(b_send), core(small), z_low(late_send)
        a_got, b_got, small_got = tie(a_got, b_got, small_got)
        (a, a_send), (b, b_send), small = parts(a, a_got), parts(b, b_got), small + small_got
        a_send, b_send, dskip = tie(a_send, b_send, dskip)
        a_got, b_got, small_got = along_x(a_send), along_y(b_send), along_x(small)
        dx, dobs = run_inputs(
            me, w_early, w_late, g1_front, g1_back, dskip, dmod_front, dmod_back, slope, lens, width
        )
        a_got, b_got, small_got, late_got, dx, dobs = tie(a_got, b_got, small_got, late_got, dx, dobs)
        late, late_send = parts(late, late_got)
        late_got = z_high(late_send)
        (a, a_send), (b, b_send), small = parts(a, a_got), parts(b, b_got), small + small_got
        a_got, b_got = along_y(a_send), along_x(b_send)
        skip_out = windows_first(skip)
        a_got, b_got, skip_out, small = tie(a_got, b_got, skip_out, small)
        early, early_send = parts(jnp.concatenate([a + a_got, b + b_got], axis=1))
        early_got, small_got = z_low(early_send), along_y(small)
        down_out = windows_first(down_front, down_back)
        early_got, small_got, down_out, dobs = tie(early_got, small_got, down_out, dobs)
        early, early_send = parts(early, early_got)
        early_got = z_high(early_send)
        dobs, dobs_send = parts(dobs)
        dobs_got = along_x(dobs_send)
        small = small + small_got
        early_got, late_got = tie(early_got, late_got)
        grads = join_order((early + early_got)[0], (late + late_got)[0])

        spread = jnp.take(grads, jnp.maximum(block_of, 0), axis=0, mode="clip").reshape(dp_count, slot_count, 16, 128)
        spread, dx, small = tie(spread, dx, small)
        owned = lax.all_to_all(spread, "dp", 0, 0)
        small_got = z_low(small)
        actions_grad = windows_first(dx)
        owned, actions_grad, small_got, dobs_got = tie(owned, actions_grad, small_got, dobs_got)
        places = me[1] ^ jnp.arange(4, dtype=jnp.int32)
        state = (master, moment_one, moment_two)
        x_got, core_got = along_x(owned), core(owned)
        small = small + small_got
        core_got, small, dobs, dobs_got = tie(core_got, small, dobs, dobs_got)
        small_got = z_high(small)
        dobs, dobs_send = parts(dobs, dobs_got)
        dobs_got = core(dobs_send)
        made = run_adamw(places[0:2], used, (owned, core_got), *state)
        x_got, small_got, dobs_got, *made = tie(x_got, small_got, dobs_got, *made)
        core_got = core(x_got)
        grad_small = small + small_got
        observations_grad = (dobs + dobs_got).reshape(observations.shape)
        new_one, new_two, new_master = run_adamw(places[2:4], used, (x_got, core_got), *state, made)
    else:
        g1_front, dmod_front, down_front, gs_front = third(g2, skip, *rest, 0, half)
        g1_back, dmod_back, down_back, gs_back = third(g2, skip, *rest, half, count // width - half)
        early_grads = run_early_grads(me, x, g1_front, g1_back, cond, dmod_front, dmod_back, width)
        dx, dobs = run_inputs(
            me, w_early, w_late, g1_front, g1_back, dskip, dmod_front, dmod_back, slope, lens, width
        )
        skip_out, down_out, actions_grad = windows_first(skip), windows_first(down_front, down_back), windows_first(dx)
        small = jnp.concatenate([(gs_front + gs_back)[0:5], gs_late[0:5]], axis=0)
        grad_small = sum_all(small)
        observations_grad = lax.psum_scatter(dobs, "pair", scatter_dimension=0).reshape(observations.shape)
        grads = join_order(from_lists(early_grads), from_lists(late_grads))
        rows = grads.reshape(-1, 4, 32, C).transpose(1, 0, 2, 3)
        rows = lax.psum_scatter(rows, "pair", scatter_dimension=0)
        spread = jnp.take(rows, jnp.maximum(block_of, 0), axis=0)
        owned = lax.psum_scatter(spread, "dp", scatter_dimension=0, tiled=True)
        owned = lax.all_gather(owned, "pair", axis=1, tiled=True)
        cut = pieces_of(owned).transpose(1, 0, 2, 3, 4)
        places = jnp.arange(4, dtype=jnp.int32)
        state = (master, moment_one, moment_two)
        made = run_adamw(places[0:2], used, (cut[0], cut[1]), *state)
        new_one, new_two, new_master = run_adamw(places[2:4], used, (cut[2], cut[3]), *state, made)
    small_first, small_second, new_small = adamw(
        small_master, small_one, small_two, grad_small, RATE_SMALL
    )
    return (
        skip_out,
        down_out,
        actions_grad,
        observations_grad,
        new_one,
        new_two,
        new_master,
        small_first,
        small_second,
        new_small,
    )


def solution(mesh):
    placed = (
        P(None, ("dp", "pair"), None, None),
        P(None, "dp", "pair"),
        P(None, ("dp", "pair")),
        P(None, ("dp", "pair")),
        P(None, ("dp", "pair"), None, None),
        P(None, ("dp", "pair"), None, None),
        P(),
        P("dp", None, None),
        P("dp", None, None),
        P("dp", None, None),
        P(),
        P(),
        P(),
    )
    return jax.shard_map(
        body,
        mesh=mesh,
        in_specs=placed,
        out_specs=(
            P(None, ("dp", "pair"), None, None),
            P(None, ("dp", "pair"), None, None),
            P(None, ("dp", "pair"), None, None),
            P(None, "dp", "pair"),
            P("dp", None, None),
            P("dp", None, None),
            P("dp", None, None),
            P(),
            P(),
            P(),
        ),
        check_vma=False,
    )
```
